512 devices in a mesh: inner: 64 (over y, z_lo, core), outer: 8 (over z_hi, x).
Axes of the slice: x: 4, y: 4, z: 16 (z_hi: 2, z_lo: 8; z = z_hi * 8 + z_lo), core: 2. Of those that a mesh axis runs over, the one named last changes fastest.
Arguments:
- grads: float32 [64, 8, 128, 8192], P('inner', 'outer'), may hold values from -0.875 to 0.875
- first_exponents: int32 [64, 8, 128, 64], P('inner', 'outer'), may hold values from -13 to -9
- second_exponents: int32 [8, 128, 64], P('outer', None, 'inner'), may hold values from -11 to -6
Outputs:
- reduced: float32 [128, 8192], P('outer', 'inner')
The draws below stay inside these ranges and needn't reach their ends.
All inputs are finite; a program needn't handle non-finite values.
Results may differ from the reference program's by a relative error of at most 0.01.
Values may be sent and summed in bfloat16 or wider, within the bound.
A program may use at most 64 MiB of HBM per device.

```python
import math
import jax
import jax.numpy as jnp
from jax import lax

D = 8192
ROWS = 128
BLOCKS = 64
N_INNER = 64
N_OUTER = 8


def plant(result, stream_key, smallest, largest):
    longest = result.shape.index(max(result.shape))
    spots = []
    for shift in (0, 1):
        where = [jax.random.randint(jax.random.fold_in(stream_key, axis), (), 0, length) for axis, length in enumerate(result.shape)]
        where[longest] = (where[longest] + shift) % result.shape[longest]
        spots.append(tuple(where))
    return result.at[spots[0]].set(smallest).at[spots[1]].set(largest)


def raised(result, own_key, source, target, shards_of, factor):
    def block_of(position):
        return (jnp.arange(result.shape[position]) // (result.shape[position] // shards_of)).reshape((-1,) + (1,) * (result.ndim - 1 - position))

    one_side = jax.random.permutation(own_key, shards_of)[block_of(target)]
    second = (block_of(target) + shards_of // 2) % shards_of
    return jnp.where((block_of(source) == one_side) | (block_of(source) == second), factor * result, result)


def level_of(rng, extent, pieces, least, largest):
    def one(axis_at, parts):
        heights = jax.random.uniform(jax.random.fold_in(jax.random.fold_in(rng, 6), axis_at), (parts,), jnp.float32, least / len(pieces), largest / len(pieces))
        return jnp.repeat(jnp.exp(heights), extent[axis_at] // parts).reshape((-1,) + (1,) * (len(extent) - axis_at - 1))

    level = one(*pieces[0])
    for cut in pieces[1:]:
        level = level * one(*cut)
    return level


def gaussian_with(rng, extent, scale, bound, shards, heavy, kind=jnp.bfloat16):
    result = scale * jax.random.normal(rng, extent, jnp.float32)
    if shards:
        result = result * level_of(rng, extent, shards, -0.22, 0.18)
    return jnp.clip(raised(result, jax.random.fold_in(rng, 3), *heavy), -bound, bound).astype(kind)


def setup_inputs(seed: int = 0) -> dict:
    streams_of = jax.random.split(jax.random.key(seed), 4)
    grads = gaussian_with(streams_of[0], (N_INNER, N_OUTER, ROWS, D), 0.05, 0.875, ((0, 64), (1, 8)), (0, 3, 64, 4.0), jnp.float32)
    first_exponents = plant(jax.random.randint(streams_of[1], (N_INNER, N_OUTER, ROWS, BLOCKS), -13, -8), jax.random.fold_in(streams_of[1], 1), -13, (-8) - 1).astype(jnp.int32)
    second_exponents = plant(jax.random.randint(streams_of[2], (N_OUTER, ROWS, BLOCKS), -11, -5), jax.random.fold_in(streams_of[2], 1), -11, (-5) - 1).astype(jnp.int32)
    return {"grads": grads, "first_exponents": first_exponents, "second_exponents": second_exponents}


saturation = 448.0

def hadamard_table():
    row_index = jnp.arange(128, dtype=jnp.int32)[:, None]
    col_index = jnp.arange(128, dtype=jnp.int32)[None, :]
    signs = jnp.ones((128, 128), dtype=jnp.float32)
    for level in range(7):
        shared = row_index // 2 ** level % 2 * (col_index // 2 ** level % 2)
        signs = signs * (1 - 2 * shared).astype(jnp.float32)
    return signs / jnp.float32(math.sqrt(128.0))

def reference(grads, first_exponents, second_exponents):
    rotation = hadamard_table()

    def encode_group(index):
        gradient = grads[:, index]
        exponent = first_exponents[:, index]
        rotated = jnp.dot(gradient.reshape(-1, 128), rotation, precision=lax.Precision.HIGHEST)
        rotated = rotated.reshape(N_INNER, ROWS, BLOCKS, 128)
        scale_in = jnp.exp2(exponent.astype(jnp.float32))[..., None]
        encoded = jnp.clip(rotated / scale_in, -saturation, saturation).astype(jnp.bfloat16)
        partial_value = lax.optimization_barrier(jnp.sum(encoded.astype(jnp.float32) * scale_in, axis=0))
        scale_two = jnp.exp2(second_exponents[index].astype(jnp.float32))[..., None]
        reencoded = jnp.clip(partial_value / scale_two, -saturation, saturation).astype(jnp.bfloat16)
        return reencoded.astype(jnp.float32) * scale_two
    decoded = lax.map(encode_group, jnp.arange(N_OUTER, dtype=jnp.int32))
    summed = lax.optimization_barrier(jnp.sum(decoded, axis=0))
    reduced = jnp.dot(summed.reshape(-1, 128), rotation, precision=lax.Precision.HIGHEST)
    return reduced.reshape(ROWS, D)
```

```python
import functools
import math

import jax
import jax.numpy as jnp
from jax import lax
from jax.experimental import pallas as pl
from jax.experimental.pallas import tpu as pltpu
from jax.sharding import PartitionSpec as P

SATURATION = 448.0
RSQRT = 1.0 / math.sqrt(128.0)
LOGICAL = pl.DeviceIdType.MESH
CHUNKS = 4
CHUNK_ROWS = 32
F32 = jnp.float32
BF16 = jnp.bfloat16


def sign_table():
    row = lax.broadcasted_iota(jnp.int32, (256, 256), 0)
    col = lax.broadcasted_iota(jnp.int32, (256, 256), 1)
    shared = row & col & 127
    shared = shared ^ (shared >> 4)
    shared = shared ^ (shared >> 2)
    shared = shared ^ (shared >> 1)
    signs = (1 - 2 * (shared & 1)).astype(F32)
    return jnp.where((row // 128) == (col // 128), signs, 0.0).astype(BF16)


def limits(exponents):
    return jnp.left_shift(1, exponents + 13).astype(F32) * F32(SATURATION / 8192.0)


def kernel(
    grads_ref, first_ref, second_ref, out_ref,
    gbuf, table, lim1, lim2, enc, arecv, s1, m1recv, m2recv, m3send, m3recv,
    s2, z1recv, zkeep, z2send, z2recv, fsend, frecv,
    load_sem, a_send, a_recv, m_send, m1_rsem, m2_rsem, m3_rsem,
    z1_send, z1_rsem, z2_send, z2_rsem, f_send_sem, f_recv_sem,
):
    inner = lax.axis_index("inner")
    outer = lax.axis_index("outer")
    core = inner % 2
    z = (inner // 2) % 8
    y = inner // 16
    run, role = z // 4, z % 4
    other_run = 1 - run

    def inner_of(yy, zz, cc):
        return (yy * 8 + zz) * 2 + cc

    right_y, left_y, far_y = (y + 1) % 4, (y + 3) % 4, (y + 2) % 4
    sibling = inner_of(y, z, 1 - core)
    right = inner_of(right_y, z, core)
    left = inner_of(left_y, z, core)
    across = inner_of(y, other_run * 4 + role, core)
    mates = [inner_of(y, run * 4 + (role + d) % 4, core) for d in (1, 2, 3)]

    def remote(src, dst, ssem, rsem, i, o=None):
        return pltpu.make_async_remote_copy(
            src_ref=src, dst_ref=dst, send_sem=ssem, recv_sem=rsem,
            device_id=(i, outer if o is None else o), device_id_type=LOGICAL,
        )

    loads = [
        pltpu.make_async_copy(
            grads_ref.at[pl.ds(q * CHUNK_ROWS, CHUNK_ROWS)], gbuf.at[q], load_sem.at[q]
        )
        for q in range(CHUNKS)
    ]
    for load in loads:
        load.start()

    barrier = pltpu.get_barrier_semaphore()
    partners = [sibling, right, left, across] + mates
    for i in partners:
        pl.semaphore_signal(barrier, inc=1, device_id=(i, outer), device_id_type=LOGICAL)
    for d in range(1, 8):
        pl.semaphore_signal(
            barrier, inc=1, device_id=(inner, (outer + d) % 8), device_id_type=LOGICAL
        )

    table[...] = sign_table()
    first = limits(first_ref[...])
    lim1[...] = jnp.concatenate([first, first], axis=0).T
    lim2[...] = jnp.broadcast_to(limits(second_ref[...]), (128, 128)).T

    started = []

    def send(*args):
        copy = remote(*args)
        copy.start()
        started.append(copy)

    def encode(q):
        loads[q].wait()
        weights = table[...]
        for group in range(4):
            base = group * 8
            lhs = jnp.concatenate(
                [gbuf[q, :, (base + k) * 256 : (base + k + 1) * 256].astype(BF16) for k in range(8)],
                axis=0,
            )
            rotated = jnp.dot(lhs, weights, preferred_element_type=F32) * F32(RSQRT)
            for k in range(8):
                for c in range(2):
                    block = 2 * (base + k) + c
                    bound = jnp.broadcast_to(
                        lim1[q * CHUNK_ROWS : (q + 1) * CHUNK_ROWS, block : block + 1],
                        (CHUNK_ROWS, 128),
                    )
                    value = rotated[k * CHUNK_ROWS : (k + 1) * CHUNK_ROWS, c * 128 : (c + 1) * 128]
                    value = jnp.minimum(jnp.maximum(value, -bound), bound)
                    enc[q, c, (base + k) // 8, ((base + k) % 8) // 4, (base + k) % 4] = value.astype(BF16)

    def pair_send(q):
        send(enc.at[q, 1 - core], arecv.at[q], a_send.at[q], a_recv.at[q], sibling)

    def wait_recv(dst, rsem):
        remote(dst, dst, rsem, rsem, sibling).wait_recv()

    def add_pair(q, yy):
        s1[q, yy] = (enc[q, core, yy].astype(F32) + arecv[q, yy].astype(F32)).astype(BF16)

    def ring_one(q):
        wait_recv(arecv.at[q], a_recv.at[q])
        add_pair(q, far_y)
        send(s1.at[q, far_y, 0], m1recv.at[q, 0], m_send.at[q, 0], m1_rsem.at[q, 0], right)
        send(s1.at[q, far_y, 1], m1recv.at[q, 1], m_send.at[q, 1], m1_rsem.at[q, 1], left)
        add_pair(q, right_y)
        send(s1.at[q, right_y, 1], m2recv.at[q, 0], m_send.at[q, 2], m2_rsem.at[q, 0], right)
        add_pair(q, left_y)
        send(s1.at[q, left_y, 0], m2recv.at[q, 1], m_send.at[q, 3], m2_rsem.at[q, 1], left)
        add_pair(q, y)

    def ring_two(q):
        wait_recv(m1recv.at[q, 0], m1_rsem.at[q, 0])
        m3send[q, 0] = (s1[q, right_y, 0].astype(F32) + m1recv[q, 0].astype(F32)).astype(BF16)
        send(m3send.at[q, 0], m3recv.at[q, 0], m_send.at[q, 4], m3_rsem.at[q, 0], right)
        wait_recv(m1recv.at[q, 1], m1_rsem.at[q, 1])
        m3send[q, 1] = (s1[q, left_y, 1].astype(F32) + m1recv[q, 1].astype(F32)).astype(BF16)
        send(m3send.at[q, 1], m3recv.at[q, 1], m_send.at[q, 5], m3_rsem.at[q, 1], left)

    def run_one(q):
        wait_recv(m2recv.at[q, 0], m2_rsem.at[q, 0])
        wait_recv(m2recv.at[q, 1], m2_rsem.at[q, 1])
        wait_recv(m3recv.at[q, 0], m3_rsem.at[q, 0])
        wait_recv(m3recv.at[q, 1], m3_rsem.at[q, 1])
        for d in (1, 2, 3, 0):
            r = (role + d) % 4
            low = s1[q, y, 0, r].astype(F32) + m3recv[q, 0, r].astype(F32) + m2recv[q, 1, r].astype(F32)
            high = s1[q, y, 1, r].astype(F32) + m2recv[q, 0, r].astype(F32) + m3recv[q, 1, r].astype(F32)
            s2[q, r, 0] = low.astype(BF16)
            s2[q, r, 1] = high.astype(BF16)
            if d:
                send(s2.at[q, r], z1recv.at[q, d - 1], z1_send.at[q, d - 1], z1_rsem.at[q, d - 1], mates[d - 1])

    def run_two(q):
        for d in range(3):
            wait_recv(z1recv.at[q, d], z1_rsem.at[q, d])

        def total(part):
            value = s2[q, role, part].astype(F32)
            for d in range(3):
                value = value + z1recv[q, d, part].astype(F32)
            return value

        z2send[q] = total(other_run).astype(BF16)
        send(z2send.at[q], z2recv.at[q], z2_send.at[q], z2_rsem.at[q], across)
        zkeep[q] = total(run)

    def group_send(q):
        wait_recv(z2recv.at[q], z2_rsem.at[q])
        bound = lim2[q * CHUNK_ROWS : (q + 1) * CHUNK_ROWS, :]
        value = zkeep[q] + z2recv[q].astype(F32)
        value = jnp.minimum(jnp.maximum(value, -bound), bound).astype(BF16)
        for h in range(2):
            owner = 2 * q + h
            fsend[owner] = value[h * 16 : (h + 1) * 16]

            @pl.when(owner != outer)
            def _():
                remote(
                    fsend.at[owner], frecv.at[outer], f_send_sem.at[owner], f_recv_sem.at[outer],
                    inner, owner,
                ).start()

    stages = [encode, pair_send, ring_one, ring_two, run_one, run_two, group_send]
    waited = False
    delays = [0, 0, 1, 2, 3, 4, 5]
    for step in range(CHUNKS + delays[-1]):
        for stage, delay in zip(stages, delays):
            q = step - delay
            if 0 <= q < CHUNKS:
                if stage is pair_send and not waited:
                    pl.semaphore_wait(barrier, len(partners) + 7)
                    waited = True
                stage(q)

    total = fsend[outer].astype(F32)
    for d in range(1, 8):
        source = (outer + d) % 8
        wait_recv(frecv.at[source], f_recv_sem.at[source])
        total = total + frecv[source].astype(F32)
    high = total.astype(BF16)
    low = (total - high.astype(F32)).astype(BF16)
    signs = table[0:128, 0:128]
    result = jnp.dot(high, signs, preferred_element_type=F32)
    result = result + jnp.dot(low, signs, preferred_element_type=F32)
    out_ref[...] = result * F32(RSQRT)

    for copy in started:
        copy.wait_send()
    for d in range(1, 8):
        owner = (outer + d) % 8
        remote(
            fsend.at[owner], frecv.at[outer], f_send_sem.at[owner], f_recv_sem.at[outer],
            inner, owner,
        ).wait_send()


def shards(grads, first_exponents, second_exponents):
    rows, columns = grads.shape[2], grads.shape[3]
    first = first_exponents.reshape(rows, columns // 128).T
    second = second_exponents.reshape(1, rows)
    dma = pltpu.SemaphoreType.DMA
    c, r = CHUNKS, CHUNK_ROWS
    return pl.pallas_call(
        kernel,
        out_shape=jax.ShapeDtypeStruct((16, 128), F32),
        in_specs=[
            pl.BlockSpec(memory_space=pl.ANY),
            pl.BlockSpec(memory_space=pltpu.VMEM),
            pl.BlockSpec(memory_space=pltpu.VMEM),
        ],
        out_specs=pl.BlockSpec(memory_space=pltpu.VMEM),
        scratch_shapes=[
            pltpu.VMEM((c, r, columns), F32),
            pltpu.VMEM((256, 256), BF16),
            pltpu.VMEM((128, 128), F32),
            pltpu.VMEM((128, 128), F32),
            pltpu.VMEM((c, 2, 4, 2, 4, r, 128), BF16),
            pltpu.VMEM((c, 4, 2, 4, r, 128), BF16),
            pltpu.VMEM((c, 4, 2, 4, r, 128), BF16),
            pltpu.VMEM((c, 2, 4, r, 128), BF16),
            pltpu.VMEM((c, 2, 4, r, 128), BF16),
            pltpu.VMEM((c, 2, 4, r, 128), BF16),
            pltpu.VMEM((c, 2, 4, r, 128), BF16),
            pltpu.VMEM((c, 4, 2, r, 128), BF16),
            pltpu.VMEM((c, 3, 2, r, 128), BF16),
            pltpu.VMEM((c, r, 128), F32),
            pltpu.VMEM((c, r, 128), BF16),
            pltpu.VMEM((c, r, 128), BF16),
            pltpu.VMEM((8, 16, 128), BF16),
            pltpu.VMEM((8, 16, 128), BF16),
            dma((c,)),
            dma((c,)),
            dma((c,)),
            dma((c, 6)),
            dma((c, 2)),
            dma((c, 2)),
            dma((c, 2)),
            dma((c, 3)),
            dma((c, 3)),
            dma((c,)),
            dma((c,)),
            dma((8,)),
            dma((8,)),
        ],
        compiler_params=pltpu.CompilerParams(
            collective_id=0, has_side_effects=True, vmem_limit_bytes=60 * 1024 * 1024
        ),
        name="reduce_scatter",
    )(grads.reshape(rows, columns), first, second)


def solution(mesh):
    placed = (
        P("inner", "outer", None, None),
        P("inner", "outer", None, None),
        P("outer", None, "inner"),
    )
    return jax.shard_map(
        shards, mesh=mesh, in_specs=placed, out_specs=P("outer", "inner"), check_vma=False
    )
```

```python
import functools
import math

import jax
import jax.numpy as jnp
from jax import lax
from jax.experimental import pallas as pl
from jax.experimental.pallas import tpu as pltpu
from jax.sharding import PartitionSpec as P

SATURATION = 448.0
RSQRT = 1.0 / math.sqrt(128.0)
LOGICAL = pl.DeviceIdType.MESH
CHUNKS = 8
CHUNK_ROWS = 16
GROUP = 256 // CHUNK_ROWS
ORDER = tuple(
    (item[0], int(item[1:]))
    for line in (
        "e0 a0 e1 a1", "e2 a2 e3 a3", "e4 a4 e5 m0", "m1 m2 a5 e6", "m3 m4 a6 e7", "n0 a7 n1 m5",
        "n2 m6 n3 m7", "n4 r0 r1 n5", "r2 n6 r3 n7", "s0 r4 s1 r5", "r6 s2 r7 s3", "g0 s4 g1 s5",
        "s6 g2 s7 g3", "g4 g5 g6 g7",
    )
    for item in line.split()
)
F32 = jnp.float32
BF16 = jnp.bfloat16


def sign_table():
    row = lax.broadcasted_iota(jnp.int32, (256, 256), 0)
    col = lax.broadcasted_iota(jnp.int32, (256, 256), 1)
    shared = row & col & 127
    shared = shared ^ (shared >> 4)
    shared = shared ^ (shared >> 2)
    shared = shared ^ (shared >> 1)
    signs = (1 - 2 * (shared & 1)).astype(F32)
    return jnp.where((row // 128) == (col // 128), signs, 0.0).astype(BF16)


def limits(exponents):
    return jnp.left_shift(1, exponents + 13).astype(F32) * F32(SATURATION / 8192.0)


def kernel(
    grads_ref, first_ref, second_ref, out_ref,
    gbuf, first_buf, second_buf, table, lim1, lim2, enc, arecv, s1, m1recv, m2recv, m3send, m3recv,
    s2, s2own, z1recv, zkeep, z2send, z2recv, fsend, frecv,
    load_sem, scale_sem, a_send, a_recv, m_send, m1_rsem, m2_rsem, m3_rsem,
    z1_send, z1_rsem, z2_send, z2_rsem, f_send_sem, f_recv_sem,
):
    inner = lax.axis_index("inner")
    outer = lax.axis_index("outer")
    core = inner % 2
    z = (inner // 2) % 8
    y = inner // 16
    run, role = z // 4, z % 4
    other_run = 1 - run

    def inner_of(yy, zz, cc):
        return (yy * 8 + zz) * 2 + cc

    right_y, left_y, far_y = (y + 1) % 4, (y + 3) % 4, (y + 2) % 4
    sibling = inner_of(y, z, 1 - core)
    right = inner_of(right_y, z, core)
    left = inner_of(left_y, z, core)
    across = inner_of(y, other_run * 4 + role, core)
    mates = [inner_of(y, run * 4 + (role + d) % 4, core) for d in (1, 2, 3)]

    def remote(src, dst, ssem, rsem, i, o=None):
        return pltpu.make_async_remote_copy(
            src_ref=src, dst_ref=dst, send_sem=ssem, recv_sem=rsem,
            device_id=(i, outer if o is None else o), device_id_type=LOGICAL,
        )

    loads = [
        pltpu.make_async_copy(
            grads_ref.at[pl.ds(q * CHUNK_ROWS, CHUNK_ROWS)], gbuf.at[q], load_sem.at[q]
        )
        for q in range(CHUNKS)
    ]
    scale_loads = [
        pltpu.make_async_copy(first_ref, first_buf, scale_sem.at[0]),
        pltpu.make_async_copy(second_ref, second_buf, scale_sem.at[1]),
    ]
    for load in scale_loads + loads:
        load.start()

    barrier = pltpu.get_barrier_semaphore()
    partners = [sibling, right, left, across] + mates
    for i in partners:
        pl.semaphore_signal(barrier, inc=1, device_id=(i, outer), device_id_type=LOGICAL)
    for d in range(1, 8):
        pl.semaphore_signal(
            barrier, inc=1, device_id=(inner, (outer + d) % 8), device_id_type=LOGICAL
        )

    table[...] = sign_table()
    for load in scale_loads:
        load.wait()
    first = limits(first_buf[...])
    lim1[...] = jnp.concatenate([first, first], axis=0).T
    lim2[...] = jnp.broadcast_to(limits(second_buf[...]), (128, 128)).T

    started = []

    def send(*args):
        copy = remote(*args)
        copy.start()
        started.append(copy)

    def encode(q):
        loads[q].wait()
        weights = table[...]
        for base in range(0, 32, GROUP):
            lhs = jnp.concatenate(
                [gbuf[q, :, (base + k) * 256 : (base + k + 1) * 256].astype(BF16) for k in range(GROUP)],
                axis=0,
            )
            rotated = jnp.dot(lhs, weights, preferred_element_type=F32) * F32(RSQRT)
            for k in range(GROUP):
                for c in range(2):
                    block = 2 * (base + k) + c
                    bound = jnp.broadcast_to(
                        lim1[q * CHUNK_ROWS : (q + 1) * CHUNK_ROWS, block : block + 1],
                        (CHUNK_ROWS, 128),
                    )
                    value = rotated[k * CHUNK_ROWS : (k + 1) * CHUNK_ROWS, c * 128 : (c + 1) * 128]
                    value = jnp.minimum(jnp.maximum(value, -bound), bound)
                    enc[q, c, (base + k) // 8, ((base + k) % 8) // 4, (base + k) % 4] = value.astype(BF16)

    def pair_send(q):
        send(enc.at[q, 1 - core], arecv.at[q], a_send.at[q], a_recv.at[q], sibling)

    def wait_recv(dst, rsem):
        remote(dst, dst, rsem, rsem, sibling).wait_recv()

    def add_pair(q, yy):
        s1[q, yy] = (enc[q, core, yy].astype(F32) + arecv[q, yy].astype(F32)).astype(BF16)

    def ring_one(q):
        wait_recv(arecv.at[q], a_recv.at[q])
        add_pair(q, far_y)
        send(s1.at[q, far_y, 0], m1recv.at[q, 0], m_send.at[q, 0], m1_rsem.at[q, 0], right)
        send(s1.at[q, far_y, 1], m1recv.at[q, 1], m_send.at[q, 1], m1_rsem.at[q, 1], left)
        add_pair(q, right_y)
        send(s1.at[q, right_y, 1], m2recv.at[q, 0], m_send.at[q, 2], m2_rsem.at[q, 0], right)
        add_pair(q, left_y)
        send(s1.at[q, left_y, 0], m2recv.at[q, 1], m_send.at[q, 3], m2_rsem.at[q, 1], left)

    def ring_two(q):
        wait_recv(m1recv.at[q, 0], m1_rsem.at[q, 0])
        m3send[q, 0] = (s1[q, right_y, 0].astype(F32) + m1recv[q, 0].astype(F32)).astype(BF16)
        send(m3send.at[q, 0], m3recv.at[q, 0], m_send.at[q, 4], m3_rsem.at[q, 0], right)
        wait_recv(m1recv.at[q, 1], m1_rsem.at[q, 1])
        m3send[q, 1] = (s1[q, left_y, 1].astype(F32) + m1recv[q, 1].astype(F32)).astype(BF16)
        send(m3send.at[q, 1], m3recv.at[q, 1], m_send.at[q, 5], m3_rsem.at[q, 1], left)

    def run_one(q):
        wait_recv(m2recv.at[q, 0], m2_rsem.at[q, 0])
        wait_recv(m2recv.at[q, 1], m2_rsem.at[q, 1])
        wait_recv(m3recv.at[q, 0], m3_rsem.at[q, 0])
        wait_recv(m3recv.at[q, 1], m3_rsem.at[q, 1])
        for d in (1, 2, 3, 0):
            r = (role + d) % 4
            own = enc[q, core, y, :, r].astype(F32) + arecv[q, y, :, r].astype(F32)
            low = own[0] + m3recv[q, 0, r].astype(F32) + m2recv[q, 1, r].astype(F32)
            high = own[1] + m2recv[q, 0, r].astype(F32) + m3recv[q, 1, r].astype(F32)
            if d == 0:
                s2own[q, 0] = low
                s2own[q, 1] = high
            else:
                s2[q, r, 0] = low.astype(BF16)
                s2[q, r, 1] = high.astype(BF16)
                send(s2.at[q, r], z1recv.at[q, d - 1], z1_send.at[q, d - 1], z1_rsem.at[q, d - 1], mates[d - 1])

    def run_two(q):
        for d in range(3):
            wait_recv(z1recv.at[q, d], z1_rsem.at[q, d])

        def total(part):
            value = s2own[q, part]
            for d in range(3):
                value = value + z1recv[q, d, part].astype(F32)
            return value

        z2send[q] = total(other_run).astype(BF16)
        send(z2send.at[q], z2recv.at[q], z2_send.at[q], z2_rsem.at[q], across)
        zkeep[q] = total(run)

    def group_send(q):
        wait_recv(z2recv.at[q], z2_rsem.at[q])
        bound = lim2[q * CHUNK_ROWS : (q + 1) * CHUNK_ROWS, :]
        value = zkeep[q] + z2recv[q].astype(F32)
        value = jnp.minimum(jnp.maximum(value, -bound), bound).astype(BF16)
        for h in range(CHUNK_ROWS // 16):
            owner = CHUNK_ROWS // 16 * q + h
            fsend[owner] = value[h * 16 : (h + 1) * 16]

            @pl.when(owner != outer)
            def _():
                remote(
                    fsend.at[owner], frecv.at[outer], f_send_sem.at[owner], f_recv_sem.at[outer],
                    inner, owner,
                ).start()

    stages = {
        "e": encode, "a": pair_send, "m": ring_one, "n": ring_two,
        "r": run_one, "s": run_two, "g": group_send,
    }
    waited = False
    for name, q in ORDER:
        if name == "a" and not waited:
            pl.semaphore_wait(barrier, len(partners) + 7)
            waited = True
        stages[name](q)

    for copy in started:
        copy.wait_send()
    total = fsend[outer].astype(F32)
    for d in range(1, 8):
        source = (outer + d) % 8
        wait_recv(frecv.at[source], f_recv_sem.at[source])
        total = total + frecv[source].astype(F32)
    high = total.astype(BF16)
    low = (total - high.astype(F32)).astype(BF16)
    signs = table[0:128, 0:128]
    result = jnp.dot(high, signs, preferred_element_type=F32)
    result = result + jnp.dot(low, signs, preferred_element_type=F32)
    out_ref[...] = result * F32(RSQRT)

    for d in range(1, 8):
        owner = (outer + d) % 8
        remote(
            fsend.at[owner], frecv.at[outer], f_send_sem.at[owner], f_recv_sem.at[outer],
            inner, owner,
        ).wait_send()


def shards(grads, first_exponents, second_exponents):
    rows, columns = grads.shape[2], grads.shape[3]
    first = first_exponents.reshape(rows, columns // 128).T
    second = second_exponents.reshape(1, rows)
    dma = pltpu.SemaphoreType.DMA
    c, r = CHUNKS, CHUNK_ROWS
    return pl.pallas_call(
        kernel,
        out_shape=jax.ShapeDtypeStruct((16, 128), F32),
        in_specs=[
            pl.BlockSpec(memory_space=pltpu.HBM),
            pl.BlockSpec(memory_space=pltpu.HBM),
            pl.BlockSpec(memory_space=pltpu.HBM),
        ],
        out_specs=pl.BlockSpec(memory_space=pltpu.VMEM),
        scratch_shapes=[
            pltpu.VMEM((c, r, columns), F32),
            pltpu.VMEM((columns // 128, rows), jnp.int32),
            pltpu.VMEM((1, rows), jnp.int32),
            pltpu.VMEM((256, 256), BF16),
            pltpu.VMEM((128, 128), F32),
            pltpu.VMEM((128, 128), F32),
            pltpu.VMEM((c, 2, 4, 2, 4, r, 128), BF16),
            pltpu.VMEM((c, 4, 2, 4, r, 128), BF16),
            pltpu.VMEM((c, 4, 2, 4, r, 128), BF16),
            pltpu.VMEM((c, 2, 4, r, 128), BF16),
            pltpu.VMEM((c, 2, 4, r, 128), BF16),
            pltpu.VMEM((c, 2, 4, r, 128), BF16),
            pltpu.VMEM((c, 2, 4, r, 128), BF16),
            pltpu.VMEM((c, 4, 2, r, 128), BF16),
            pltpu.VMEM((c, 2, r, 128), F32),
            pltpu.VMEM((c, 3, 2, r, 128), BF16),
            pltpu.VMEM((c, r, 128), F32),
            pltpu.VMEM((c, r, 128), BF16),
            pltpu.VMEM((c, r, 128), BF16),
            pltpu.VMEM((8, 16, 128), BF16),
            pltpu.VMEM((8, 16, 128), BF16),
            dma((c,)),
            dma((2,)),
            dma((c,)),
            dma((c,)),
            dma((c, 6)),
            dma((c, 2)),
            dma((c, 2)),
            dma((c, 2)),
            dma((c, 3)),
            dma((c, 3)),
            dma((c,)),
            dma((c,)),
            dma((8,)),
            dma((8,)),
        ],
        compiler_params=pltpu.CompilerParams(
            collective_id=0, has_side_effects=True, vmem_limit_bytes=48 * 1024 * 1024
        ),
        name="reduce_scatter",
    )(*(pltpu.with_memory_space_constraint(x, pltpu.HBM) for x in (grads.reshape(rows, columns), first, second)))


def solution(mesh):
    placed = (
        P("inner", "outer", None, None),
        P("inner", "outer", None, None),
        P("outer", None, "inner"),
    )
    return jax.shard_map(
        shards, mesh=mesh, in_specs=placed, out_specs=P("outer", "inner"), check_vma=False
    )
```

```python
import functools
import math

import jax
import jax.numpy as jnp
from jax import lax
from jax.experimental import pallas as pl
from jax.experimental.pallas import tpu as pltpu
from jax.sharding import PartitionSpec as P

SATURATION = 448.0
RSQRT = 1.0 / math.sqrt(128.0)
LOGICAL = pl.DeviceIdType.MESH
CHUNKS = 2
CHUNK_ROWS = 64
GROUP = 256 // CHUNK_ROWS
ORDER = tuple(
    (item[0], int(item[1:]))
    for line in ("e0 a0 e1 a1", "m0 m1 n0 n1", "r0 r1 s0 s1", "g0 g1")
    for item in line.split()
)
F32 = jnp.float32
BF16 = jnp.bfloat16


def sign_table():
    row = lax.broadcasted_iota(jnp.int32, (256, 256), 0)
    col = lax.broadcasted_iota(jnp.int32, (256, 256), 1)
    shared = row & col & 127
    shared = shared ^ (shared >> 4)
    shared = shared ^ (shared >> 2)
    shared = shared ^ (shared >> 1)
    signs = (1 - 2 * (shared & 1)).astype(F32)
    return jnp.where((row // 128) == (col // 128), signs, 0.0).astype(BF16)


def limits(exponents):
    return jnp.left_shift(1, exponents + 13).astype(F32) * F32(SATURATION / 8192.0)


def kernel(
    grads_ref, first_ref, second_ref, out_ref,
    gbuf, first_buf, second_buf, table, lim1, lim2, enc, arecv, s1, m1recv, m2recv, m3send, m3recv,
    s2, s2own, z1recv, zkeep, z2send, z2recv, fsend, frecv,
    load_sem, scale_sem, a_send, a_recv, m_send, m1_rsem, m2_rsem, m3_rsem,
    z1_send, z1_rsem, z2_send, z2_rsem, f_send_sem, f_recv_sem,
):
    inner = lax.axis_index("inner")
    outer = lax.axis_index("outer")
    core = inner % 2
    z = (inner // 2) % 8
    y = inner // 16
    run, role = z // 4, z % 4
    other_run = 1 - run

    def inner_of(yy, zz, cc):
        return (yy * 8 + zz) * 2 + cc

    right_y, left_y, far_y = (y + 1) % 4, (y + 3) % 4, (y + 2) % 4
    sibling = inner_of(y, z, 1 - core)
    right = inner_of(right_y, z, core)
    left = inner_of(left_y, z, core)
    across = inner_of(y, other_run * 4 + role, core)
    mates = [inner_of(y, run * 4 + (role + d) % 4, core) for d in (1, 2, 3)]

    def remote(src, dst, ssem, rsem, i, o=None):
        return pltpu.make_async_remote_copy(
            src_ref=src, dst_ref=dst, send_sem=ssem, recv_sem=rsem,
            device_id=(i, outer if o is None else o), device_id_type=LOGICAL,
        )

    loads = [
        pltpu.make_async_copy(
            grads_ref.at[pl.ds(q * CHUNK_ROWS, CHUNK_ROWS)], gbuf.at[q], load_sem.at[q]
        )
        for q in range(CHUNKS)
    ]
    scale_loads = [
        pltpu.make_async_copy(first_ref, first_buf, scale_sem.at[0]),
        pltpu.make_async_copy(second_ref, second_buf, scale_sem.at[1]),
    ]
    for load in scale_loads + loads:
        load.start()

    barrier = pltpu.get_barrier_semaphore()
    partners = [sibling, right, left, across] + mates
    for i in partners:
        pl.semaphore_signal(barrier, inc=1, device_id=(i, outer), device_id_type=LOGICAL)
    for d in range(1, 8):
        pl.semaphore_signal(
            barrier, inc=1, device_id=(inner, (outer + d) % 8), device_id_type=LOGICAL
        )

    table[...] = sign_table()
    for load in scale_loads:
        load.wait()
    first = limits(first_buf[...])
    lim1[...] = jnp.concatenate([first, first], axis=0).T
    lim2[...] = jnp.broadcast_to(limits(second_buf[...]), (128, 128)).T

    started = []

    def send(*args):
        copy = remote(*args)
        copy.start()
        started.append(copy)

    def encode(q):
        loads[q].wait()
        weights = table[...]
        for base in range(0, 32, GROUP):
            lhs = jnp.concatenate(
                [gbuf[q, :, (base + k) * 256 : (base + k + 1) * 256].astype(BF16) for k in range(GROUP)],
                axis=0,
            )
            rotated = jnp.dot(lhs, weights, preferred_element_type=F32) * F32(RSQRT)
            for k in range(GROUP):
                for c in range(2):
                    block = 2 * (base + k) + c
                    bound = jnp.broadcast_to(
                        lim1[q * CHUNK_ROWS : (q + 1) * CHUNK_ROWS, block : block + 1],
                        (CHUNK_ROWS, 128),
                    )
                    value = rotated[k * CHUNK_ROWS : (k + 1) * CHUNK_ROWS, c * 128 : (c + 1) * 128]
                    value = jnp.minimum(jnp.maximum(value, -bound), bound)
                    enc[q, c, (base + k) // 8, ((base + k) % 8) // 4, (base + k) % 4] = value.astype(BF16)

    def pair_send(q):
        send(enc.at[q, 1 - core], arecv.at[q], a_send.at[q], a_recv.at[q], sibling)

    def wait_recv(dst, rsem):
        remote(dst, dst, rsem, rsem, sibling).wait_recv()

    def add_pair(q, yy):
        s1[q, yy] = (enc[q, core, yy].astype(F32) + arecv[q, yy].astype(F32)).astype(BF16)

    def ring_one(q):
        wait_recv(arecv.at[q], a_recv.at[q])
        add_pair(q, far_y)
        send(s1.at[q, far_y, 0], m1recv.at[q, 0], m_send.at[q, 0], m1_rsem.at[q, 0], right)
        send(s1.at[q, far_y, 1], m1recv.at[q, 1], m_send.at[q, 1], m1_rsem.at[q, 1], left)
        add_pair(q, right_y)
        send(s1.at[q, right_y, 1], m2recv.at[q, 0], m_send.at[q, 2], m2_rsem.at[q, 0], right)
        add_pair(q, left_y)
        send(s1.at[q, left_y, 0], m2recv.at[q, 1], m_send.at[q, 3], m2_rsem.at[q, 1], left)

    def ring_two(q):
        wait_recv(m1recv.at[q, 0], m1_rsem.at[q, 0])
        m3send[q, 0] = (s1[q, right_y, 0].astype(F32) + m1recv[q, 0].astype(F32)).astype(BF16)
        send(m3send.at[q, 0], m3recv.at[q, 0], m_send.at[q, 4], m3_rsem.at[q, 0], right)
        wait_recv(m1recv.at[q, 1], m1_rsem.at[q, 1])
        m3send[q, 1] = (s1[q, left_y, 1].astype(F32) + m1recv[q, 1].astype(F32)).astype(BF16)
        send(m3send.at[q, 1], m3recv.at[q, 1], m_send.at[q, 5], m3_rsem.at[q, 1], left)

    def run_one(q):
        wait_recv(m2recv.at[q, 0], m2_rsem.at[q, 0])
        wait_recv(m2recv.at[q, 1], m2_rsem.at[q, 1])
        wait_recv(m3recv.at[q, 0], m3_rsem.at[q, 0])
        wait_recv(m3recv.at[q, 1], m3_rsem.at[q, 1])
        for d in (1, 2, 3, 0):
            r = (role + d) % 4
            own = enc[q, core, y, :, r].astype(F32) + arecv[q, y, :, r].astype(F32)
            low = own[0] + m3recv[q, 0, r].astype(F32) + m2recv[q, 1, r].astype(F32)
            high = own[1] + m2recv[q, 0, r].astype(F32) + m3recv[q, 1, r].astype(F32)
            if d == 0:
                s2own[q, 0] = low
                s2own[q, 1] = high
            else:
                s2[q, r, 0] = low.astype(BF16)
                s2[q, r, 1] = high.astype(BF16)
                send(s2.at[q, r], z1recv.at[q, d - 1], z1_send.at[q, d - 1], z1_rsem.at[q, d - 1], mates[d - 1])

    def run_two(q):
        for d in range(3):
            wait_recv(z1recv.at[q, d], z1_rsem.at[q, d])

        def total(part):
            value = s2own[q, part]
            for d in range(3):
                value = value + z1recv[q, d, part].astype(F32)
            return value

        z2send[q] = total(other_run).astype(BF16)
        send(z2send.at[q], z2recv.at[q], z2_send.at[q], z2_rsem.at[q], across)
        zkeep[q] = total(run)

    def group_send(q):
        wait_recv(z2recv.at[q], z2_rsem.at[q])
        bound = lim2[q * CHUNK_ROWS : (q + 1) * CHUNK_ROWS, :]
        value = zkeep[q] + z2recv[q].astype(F32)
        value = jnp.minimum(jnp.maximum(value, -bound), bound).astype(BF16)
        for h in range(CHUNK_ROWS // 16):
            owner = CHUNK_ROWS // 16 * q + h
            fsend[owner] = value[h * 16 : (h + 1) * 16]

            @pl.when(owner != outer)
            def _():
                remote(
                    fsend.at[owner], frecv.at[outer], f_send_sem.at[owner], f_recv_sem.at[outer],
                    inner, owner,
                ).start()

    stages = {
        "e": encode, "a": pair_send, "m": ring_one, "n": ring_two,
        "r": run_one, "s": run_two, "g": group_send,
    }
    waited = False
    for name, q in ORDER:
        if name == "a" and not waited:
            pl.semaphore_wait(barrier, len(partners) + 7)
            waited = True
        stages[name](q)

    for copy in started:
        copy.wait_send()
    total = fsend[outer].astype(F32)
    for d in range(1, 8):
        source = (outer + d) % 8
        wait_recv(frecv.at[source], f_recv_sem.at[source])
        total = total + frecv[source].astype(F32)
    high = total.astype(BF16)
    low = (total - high.astype(F32)).astype(BF16)
    signs = table[0:128, 0:128]
    result = jnp.dot(high, signs, preferred_element_type=F32)
    result = result + jnp.dot(low, signs, preferred_element_type=F32)
    out_ref[...] = result * F32(RSQRT)

    for d in range(1, 8):
        owner = (outer + d) % 8
        remote(
            fsend.at[owner], frecv.at[outer], f_send_sem.at[owner], f_recv_sem.at[outer],
            inner, owner,
        ).wait_send()


def shards(grads, first_exponents, second_exponents):
    rows, columns = grads.shape[2], grads.shape[3]
    first = first_exponents.reshape(rows, columns // 128).T
    second = second_exponents.reshape(1, rows)
    dma = pltpu.SemaphoreType.DMA
    c, r = CHUNKS, CHUNK_ROWS
    return pl.pallas_call(
        kernel,
        out_shape=jax.ShapeDtypeStruct((16, 128), F32),
        in_specs=[
            pl.BlockSpec(memory_space=pltpu.HBM),
            pl.BlockSpec(memory_space=pltpu.HBM),
            pl.BlockSpec(memory_space=pltpu.HBM),
        ],
        out_specs=pl.BlockSpec(memory_space=pltpu.VMEM),
        scratch_shapes=[
            pltpu.VMEM((c, r, columns), F32),
            pltpu.VMEM((columns // 128, rows), jnp.int32),
            pltpu.VMEM((1, rows), jnp.int32),
            pltpu.VMEM((256, 256), BF16),
            pltpu.VMEM((128, 128), F32),
            pltpu.VMEM((128, 128), F32),
            pltpu.VMEM((c, 2, 4, 2, 4, r, 128), BF16),
            pltpu.VMEM((c, 4, 2, 4, r, 128), BF16),
            pltpu.VMEM((c, 4, 2, 4, r, 128), BF16),
            pltpu.VMEM((c, 2, 4, r, 128), BF16),
            pltpu.VMEM((c, 2, 4, r, 128), BF16),
            pltpu.VMEM((c, 2, 4, r, 128), BF16),
            pltpu.VMEM((c, 2, 4, r, 128), BF16),
            pltpu.VMEM((c, 4, 2, r, 128), BF16),
            pltpu.VMEM((c, 2, r, 128), F32),
            pltpu.VMEM((c, 3, 2, r, 128), BF16),
            pltpu.VMEM((c, r, 128), F32),
            pltpu.VMEM((c, r, 128), BF16),
            pltpu.VMEM((c, r, 128), BF16),
            pltpu.VMEM((8, 16, 128), BF16),
            pltpu.VMEM((8, 16, 128), BF16),
            dma((c,)),
            dma((2,)),
            dma((c,)),
            dma((c,)),
            dma((c, 6)),
            dma((c, 2)),
            dma((c, 2)),
            dma((c, 2)),
            dma((c, 3)),
            dma((c, 3)),
            dma((c,)),
            dma((c,)),
            dma((8,)),
            dma((8,)),
        ],
        compiler_params=pltpu.CompilerParams(
            collective_id=0, has_side_effects=True, vmem_limit_bytes=48 * 1024 * 1024
        ),
        name="reduce_scatter",
    )(*(pltpu.with_memory_space_constraint(x, pltpu.HBM) for x in (grads.reshape(rows, columns), first, second)))


def solution(mesh):
    placed = (
        P("inner", "outer", None, None),
        P("inner", "outer", None, None),
        P("outer", None, "inner"),
    )
    return jax.shard_map(
        shards, mesh=mesh, in_specs=placed, out_specs=P("outer", "inner"), check_vma=False
    )
```

```python
import functools
import math

import jax
import jax.numpy as jnp
from jax import lax
from jax.experimental import pallas as pl
from jax.experimental.pallas import tpu as pltpu
from jax.sharding import PartitionSpec as P

SATURATION = 448.0
RSQRT = 1.0 / math.sqrt(128.0)
LOGICAL = pl.DeviceIdType.MESH
CHUNKS = 4
CHUNK_ROWS = 32
GROUP = 8
F32 = jnp.float32
BF16 = jnp.bfloat16


def sign_table():
    row = lax.broadcasted_iota(jnp.int32, (256, 256), 0)
    col = lax.broadcasted_iota(jnp.int32, (256, 256), 1)
    shared = row & col & 127
    shared = shared ^ (shared >> 4)
    shared = shared ^ (shared >> 2)
    shared = shared ^ (shared >> 1)
    signs = (1 - 2 * (shared & 1)).astype(F32)
    return jnp.where((row // 128) == (col // 128), signs, 0.0).astype(BF16)


def limits(exponents):
    return jnp.left_shift(1, exponents + 13).astype(F32) * F32(SATURATION / 8192.0)


def kernel(
    grads_ref, first_ref, second_ref, out_ref,
    gbuf, first_buf, second_buf, table, lim1, lim2, enc, arecv, s1, m1recv, m2recv, m3send, m3recv,
    s2, s2own, z1recv, zkeep, z2send, z2recv, fsend, frecv,
    load_sem, scale_sem, a_send, a_recv, m_send, m1_rsem, m2_rsem, m3_rsem,
    z1_send, z1_rsem, z2_send, z2_rsem, f_send_sem, f_recv_sem,
):
    inner = lax.axis_index("inner")
    outer = lax.axis_index("outer")
    core = inner % 2
    z = (inner // 2) % 8
    y = inner // 16
    run, role = z // 4, z % 4
    other_run = 1 - run

    def inner_of(yy, zz, cc):
        return (yy * 8 + zz) * 2 + cc

    right_y, left_y, far_y = (y + 1) % 4, (y + 3) % 4, (y + 2) % 4
    sibling = inner_of(y, z, 1 - core)
    right = inner_of(right_y, z, core)
    left = inner_of(left_y, z, core)
    across = inner_of(y, other_run * 4 + role, core)
    mates = [inner_of(y, run * 4 + (role + d) % 4, core) for d in (1, 2, 3)]

    def remote(src, dst, ssem, rsem, i, o=None):
        return pltpu.make_async_remote_copy(
            src_ref=src, dst_ref=dst, send_sem=ssem, recv_sem=rsem,
            device_id=(i, outer if o is None else o), device_id_type=LOGICAL,
        )

    def loads(q):
        rows = pl.ds(pl.multiple_of(q * CHUNK_ROWS, CHUNK_ROWS), CHUNK_ROWS)
        return pltpu.make_async_copy(grads_ref.at[rows], gbuf.at[q], load_sem.at[q])

    scale_loads = [
        pltpu.make_async_copy(first_ref, first_buf, scale_sem.at[0]),
        pltpu.make_async_copy(second_ref, second_buf, scale_sem.at[1]),
    ]
    for load in scale_loads + [loads(q) for q in range(CHUNKS)]:
        load.start()

    barrier = pltpu.get_barrier_semaphore()
    partners = [sibling, right, left, across] + mates
    for i in partners:
        pl.semaphore_signal(barrier, inc=1, device_id=(i, outer), device_id_type=LOGICAL)
    for d in range(1, 8):
        pl.semaphore_signal(
            barrier, inc=1, device_id=(inner, (outer + d) % 8), device_id_type=LOGICAL
        )

    table[...] = sign_table()
    for load in scale_loads:
        load.wait()
    first = limits(first_buf[...])
    first = jnp.concatenate([first, first], axis=0).T
    for group in range(4):
        lim1[group] = jnp.concatenate([first[:, 16 * group :], first[:, : 16 * group]], axis=1) if group else first
    lim2[...] = jnp.broadcast_to(limits(second_buf[...]), (128, 128)).T

    def encode(q):
        loads(q).wait()
        rows = pl.ds(pl.multiple_of(q * CHUNK_ROWS, CHUNK_ROWS), CHUNK_ROWS)

        def encode_group(group, carry):
            lhs = jnp.concatenate(
                [
                    gbuf[q, :, pl.ds(pl.multiple_of((group * GROUP + k) * 256, 256), 256)].astype(BF16)
                    for k in range(GROUP)
                ],
                axis=0,
            )
            rotated = jnp.dot(lhs, table[...], preferred_element_type=F32) * F32(RSQRT)
            bounds = lim1[group, rows, :]
            for k in range(GROUP):
                for c in range(2):
                    bound = jnp.broadcast_to(bounds[:, 2 * k + c : 2 * k + c + 1], (CHUNK_ROWS, 128))
                    value = rotated[k * CHUNK_ROWS : (k + 1) * CHUNK_ROWS, c * 128 : (c + 1) * 128]
                    value = jnp.minimum(jnp.maximum(value, -bound), bound)
                    enc[q, c, group, k // 4, k % 4] = value.astype(BF16)
            return carry

        lax.fori_loop(0, 4, encode_group, 0)

    def pair_copy(q):
        return remote(enc.at[q, 1 - core], arecv.at[q], a_send.at[q], a_recv.at[q], sibling)

    def ring_copies(q):
        return [
            remote(s1.at[q, far_y, 0], m1recv.at[q, 0], m_send.at[q, 0], m1_rsem.at[q, 0], right),
            remote(s1.at[q, far_y, 1], m1recv.at[q, 1], m_send.at[q, 1], m1_rsem.at[q, 1], left),
            remote(s1.at[q, right_y, 1], m2recv.at[q, 0], m_send.at[q, 2], m2_rsem.at[q, 0], right),
            remote(s1.at[q, left_y, 0], m2recv.at[q, 1], m_send.at[q, 3], m2_rsem.at[q, 1], left),
            remote(m3send.at[q, 0], m3recv.at[q, 0], m_send.at[q, 4], m3_rsem.at[q, 0], right),
            remote(m3send.at[q, 1], m3recv.at[q, 1], m_send.at[q, 5], m3_rsem.at[q, 1], left),
        ]

    def run_copies(q):
        return [
            remote(
                s2.at[q, (role + d) % 4], z1recv.at[q, d - 1],
                z1_send.at[q, d - 1], z1_rsem.at[q, d - 1], mates[d - 1],
            )
            for d in (1, 2, 3)
        ]

    def across_copy(q):
        return remote(z2send.at[q], z2recv.at[q], z2_send.at[q], z2_rsem.at[q], across)

    def wait_recv(dst, rsem):
        remote(dst, dst, rsem, rsem, sibling).wait_recv()

    def add_pair(q, yy):
        s1[q, yy] = (enc[q, core, yy].astype(F32) + arecv[q, yy].astype(F32)).astype(BF16)

    def ring_one(q):
        copies = ring_copies(q)
        wait_recv(arecv.at[q], a_recv.at[q])
        add_pair(q, far_y)
        copies[0].start()
        copies[1].start()
        add_pair(q, right_y)
        copies[2].start()
        add_pair(q, left_y)
        copies[3].start()

    def ring_two(q):
        copies = ring_copies(q)
        wait_recv(m1recv.at[q, 0], m1_rsem.at[q, 0])
        m3send[q, 0] = (s1[q, right_y, 0].astype(F32) + m1recv[q, 0].astype(F32)).astype(BF16)
        copies[4].start()
        wait_recv(m1recv.at[q, 1], m1_rsem.at[q, 1])
        m3send[q, 1] = (s1[q, left_y, 1].astype(F32) + m1recv[q, 1].astype(F32)).astype(BF16)
        copies[5].start()

    def run_one(q):
        wait_recv(m2recv.at[q, 0], m2_rsem.at[q, 0])
        wait_recv(m2recv.at[q, 1], m2_rsem.at[q, 1])
        wait_recv(m3recv.at[q, 0], m3_rsem.at[q, 0])
        wait_recv(m3recv.at[q, 1], m3_rsem.at[q, 1])
        copies = run_copies(q)
        for d in (1, 2, 3, 0):
            r = (role + d) % 4
            own = enc[q, core, y, :, r].astype(F32) + arecv[q, y, :, r].astype(F32)
            low = own[0] + m3recv[q, 0, r].astype(F32) + m2recv[q, 1, r].astype(F32)
            high = own[1] + m2recv[q, 0, r].astype(F32) + m3recv[q, 1, r].astype(F32)
            if d == 0:
                s2own[q, 0] = low
                s2own[q, 1] = high
            else:
                s2[q, r, 0] = low.astype(BF16)
                s2[q, r, 1] = high.astype(BF16)
                copies[d - 1].start()

    def run_two(q):
        for d in range(3):
            wait_recv(z1recv.at[q, d], z1_rsem.at[q, d])

        def total(part):
            value = s2own[q, part]
            for d in range(3):
                value = value + z1recv[q, d, part].astype(F32)
            return value

        z2send[q] = total(other_run).astype(BF16)
        across_copy(q).start()
        zkeep[q] = total(run)

    def group_send(q):
        wait_recv(z2recv.at[q], z2_rsem.at[q])
        bound = lim2[pl.ds(pl.multiple_of(q * CHUNK_ROWS, CHUNK_ROWS), CHUNK_ROWS), :]
        value = zkeep[q] + z2recv[q].astype(F32)
        value = jnp.minimum(jnp.maximum(value, -bound), bound).astype(BF16)
        for h in range(2):
            owner = 2 * q + h
            fsend[owner] = value[h * 16 : (h + 1) * 16]

            @pl.when(owner != outer)
            def _():
                remote(
                    fsend.at[owner], frecv.at[outer], f_send_sem.at[owner], f_recv_sem.at[outer],
                    inner, owner,
                ).start()

    def each(stage):
        def body(q, carry):
            stage(q)
            return carry

        lax.fori_loop(0, CHUNKS, body, 0)

    def first_stages(q, carry):
        @pl.when(q < CHUNKS)
        def _():
            encode(q)
            pair_copy(q).start()

        @pl.when(q > 0)
        def _():
            ring_one(q - 1)

        return carry

    def sends_done(q):
        for copy in [pair_copy(q), across_copy(q)] + ring_copies(q) + run_copies(q):
            copy.wait_send()

    pl.semaphore_wait(barrier, len(partners) + 7)
    lax.fori_loop(0, CHUNKS + 1, first_stages, 0)
    for stage in (ring_two, run_one, run_two, group_send, sends_done):
        each(stage)

    total = fsend[outer].astype(F32)
    for d in range(1, 8):
        source = (outer + d) % 8
        wait_recv(frecv.at[source], f_recv_sem.at[source])
        total = total + frecv[source].astype(F32)
    high = total.astype(BF16)
    low = (total - high.astype(F32)).astype(BF16)
    signs = table[0:128, 0:128]
    result = jnp.dot(high, signs, preferred_element_type=F32)
    result = result + jnp.dot(low, signs, preferred_element_type=F32)
    out_ref[...] = result * F32(RSQRT)

    for d in range(1, 8):
        owner = (outer + d) % 8
        remote(
            fsend.at[owner], frecv.at[outer], f_send_sem.at[owner], f_recv_sem.at[outer],
            inner, owner,
        ).wait_send()


def shards(grads, first_exponents, second_exponents):
    rows, columns = grads.shape[2], grads.shape[3]
    first = first_exponents.reshape(rows, columns // 128).T
    second = second_exponents.reshape(1, rows)
    dma = pltpu.SemaphoreType.DMA
    c, r = CHUNKS, CHUNK_ROWS
    return pl.pallas_call(
        kernel,
        out_shape=jax.ShapeDtypeStruct((16, 128), F32),
        in_specs=[
            pl.BlockSpec(memory_space=pltpu.HBM),
            pl.BlockSpec(memory_space=pltpu.HBM),
            pl.BlockSpec(memory_space=pltpu.HBM),
        ],
        out_specs=pl.BlockSpec(memory_space=pltpu.VMEM),
        scratch_shapes=[
            pltpu.VMEM((c, r, columns), F32),
            pltpu.VMEM((columns // 128, rows), jnp.int32),
            pltpu.VMEM((1, rows), jnp.int32),
            pltpu.VMEM((256, 256), BF16),
            pltpu.VMEM((4, 128, 128), F32),
            pltpu.VMEM((128, 128), F32),
            pltpu.VMEM((c, 2, 4, 2, 4, r, 128), BF16),
            pltpu.VMEM((c, 4, 2, 4, r, 128), BF16),
            pltpu.VMEM((c, 4, 2, 4, r, 128), BF16),
            pltpu.VMEM((c, 2, 4, r, 128), BF16),
            pltpu.VMEM((c, 2, 4, r, 128), BF16),
            pltpu.VMEM((c, 2, 4, r, 128), BF16),
            pltpu.VMEM((c, 2, 4, r, 128), BF16),
            pltpu.VMEM((c, 4, 2, r, 128), BF16),
            pltpu.VMEM((c, 2, r, 128), F32),
            pltpu.VMEM((c, 3, 2, r, 128), BF16),
            pltpu.VMEM((c, r, 128), F32),
            pltpu.VMEM((c, r, 128), BF16),
            pltpu.VMEM((c, r, 128), BF16),
            pltpu.VMEM((8, 16, 128), BF16),
            pltpu.VMEM((8, 16, 128), BF16),
            dma((c,)),
            dma((2,)),
            dma((c,)),
            dma((c,)),
            dma((c, 6)),
            dma((c, 2)),
            dma((c, 2)),
            dma((c, 2)),
            dma((c, 3)),
            dma((c, 3)),
            dma((c,)),
            dma((c,)),
            dma((8,)),
            dma((8,)),
        ],
        compiler_params=pltpu.CompilerParams(
            collective_id=0, has_side_effects=True, vmem_limit_bytes=48 * 1024 * 1024
        ),
        name="reduce_scatter",
    )(*(pltpu.with_memory_space_constraint(x, pltpu.HBM) for x in (grads.reshape(rows, columns), first, second)))


def solution(mesh):
    placed = (
        P("inner", "outer", None, None),
        P("inner", "outer", None, None),
        P("outer", None, "inner"),
    )
    return jax.shard_map(
        shards, mesh=mesh, in_specs=placed, out_specs=P("outer", "inner"), check_vma=False
    )
```

```python
import math

import jax
import jax.numpy as jnp
from jax import lax
from jax.experimental import pallas as pl
from jax.experimental.pallas import tpu as pltpu
from jax.sharding import PartitionSpec as P

SATURATION = 448.0
RSQRT = 1.0 / math.sqrt(128.0)
LOGICAL = pl.DeviceIdType.MESH
F32 = jnp.float32
BF16 = jnp.bfloat16
CHUNKS = 4
CHUNK_ROWS = 128 // CHUNKS
OWNERS = CHUNK_ROWS // 16
GROUP = 256 // CHUNK_ROWS
ORDER = tuple(
    (item[0], int(item[1:]))
    for line in (
        "e0 a0 e1 a1", "e2 a2 m0 e3", "a3 m1 n0 m2", "n1 m3 r0 n2", "r1 s0 n3 r2", "s1 r3 s2 g0",
        "s3 g1 g2 g3",
    )
    for item in line.split()
)


def sign_table():
    row = lax.broadcasted_iota(jnp.int32, (256, 256), 0)
    col = lax.broadcasted_iota(jnp.int32, (256, 256), 1)
    shared = row & col & 127
    shared = shared ^ (shared >> 4)
    shared = shared ^ (shared >> 2)
    shared = shared ^ (shared >> 1)
    signs = (1 - 2 * (shared & 1)).astype(F32)
    return jnp.where((row // 128) == (col // 128), signs, 0.0).astype(BF16)


def limits(exponents):
    return jnp.left_shift(1, exponents + 13).astype(F32) * F32(SATURATION / 8192.0)


def clip(value, bound):
    return jnp.minimum(jnp.maximum(value, -bound), bound)


def kernel(
    grads_ref, first_ref, second_ref, out_ref,
    gbuf, first_buf, second_buf, table, lim1, lim2, enc, arecv,
    y1send, y1recv, y2send, y2recv, z1send, z1own, z1recv, z2own, z2send, z2recv, fsend, frecv,
    load_sem, scale_sem, send_sem, a_rsem, y1_rsem, y2_rsem, z1_rsem, z2_rsem, f_rsem,
):
    inner = lax.axis_index("inner")
    outer = lax.axis_index("outer")
    core = inner % 2
    z = (inner // 2) % 8
    y = inner // 16
    run, role = z // 4, z % 4
    y_one, y_two, y_far = y + 1 - 2 * (y % 2), 3 - y, (y + 2) % 4

    def inner_of(yy, zz, cc):
        return (yy * 8 + zz) * 2 + cc

    sibling = inner_of(y, z, 1 - core)
    pair_one = inner_of(y_one, z, core)
    pair_two = inner_of(y_two, z, core)
    across = inner_of(y, (1 - run) * 4 + role, core)
    mates = [inner_of(y, run * 4 + (role + d) % 4, core) for d in (1, 2, 3)]

    def remote(src, dst, stage, rsem, i, o=None):
        return pltpu.make_async_remote_copy(
            src_ref=src, dst_ref=dst, send_sem=send_sem.at[stage], recv_sem=rsem,
            device_id=(i, outer if o is None else o), device_id_type=LOGICAL,
        )

    def wait_recv(dst, rsem):
        remote(dst, dst, 0, rsem, sibling).wait_recv()

    def wait_send(like, stage):
        remote(like, like, stage, f_rsem.at[0], sibling).wait_send()

    scale_loads = [
        pltpu.make_async_copy(first_ref, first_buf, scale_sem.at[0]),
        pltpu.make_async_copy(second_ref, second_buf, scale_sem.at[1]),
    ]
    loads = [
        pltpu.make_async_copy(
            grads_ref.at[pl.ds(q * CHUNK_ROWS, CHUNK_ROWS)], gbuf.at[q], load_sem.at[q]
        )
        for q in range(CHUNKS)
    ]
    for load in scale_loads + loads:
        load.start()

    barrier = pltpu.get_barrier_semaphore()
    partners = [sibling, pair_one, pair_two, across] + mates
    for i in partners:
        pl.semaphore_signal(barrier, inc=1, device_id=(i, outer), device_id_type=LOGICAL)
    for d in range(1, 8):
        pl.semaphore_signal(
            barrier, inc=1, device_id=(inner, (outer + d) % 8), device_id_type=LOGICAL
        )

    table[...] = sign_table()
    for load in scale_loads:
        load.wait()
    first = limits(first_buf[...])
    lim1[...] = jnp.concatenate([first, first], axis=0).T
    lim2[...] = jnp.broadcast_to(limits(second_buf[...]), (128, 128)).T

    def encode(q):
        loads[q].wait()
        weights = table[...]
        rows = slice(q * CHUNK_ROWS, (q + 1) * CHUNK_ROWS)
        for base in range(0, 32, GROUP):
            lhs = jnp.concatenate(
                [
                    gbuf[q, :, (base + k) * 256 : (base + k + 1) * 256].astype(BF16)
                    for k in range(GROUP)
                ],
                axis=0,
            )
            rotated = jnp.dot(lhs, weights, preferred_element_type=F32) * F32(RSQRT)
            for k in range(GROUP):
                pair = base + k
                for c in range(2):
                    block = 2 * pair + c
                    bound = jnp.broadcast_to(lim1[rows, block : block + 1], (CHUNK_ROWS, 128))
                    value = rotated[k * CHUNK_ROWS : (k + 1) * CHUNK_ROWS, c * 128 : (c + 1) * 128]
                    enc[q, c, pair // 8, pair % 8 // 4, pair % 4] = clip(value, bound).astype(BF16)

    def pair_send(q):
        remote(enc.at[q, 1 - core], arecv.at[q], 0, a_rsem.at[q], sibling).start()

    def pair_sum(q, yy, half):
        return enc[q, core, yy, half] + arecv[q, yy, half]

    def ring_one(q):
        wait_recv(arecv.at[q], a_rsem.at[q])
        for half, near, to in ((0, y_one, pair_one), (1, y_two, pair_two)):
            y1send[q, half, 0] = pair_sum(q, near, half)
            y1send[q, half, 1] = pair_sum(q, y_far, half)
            remote(y1send.at[q, half], y1recv.at[q, half], 1, y1_rsem.at[q], to).start()

    def ring_two(q):
        wait_recv(y1recv.at[q], y1_rsem.at[q])
        for half, near, to in ((0, y_two, pair_two), (1, y_one, pair_one)):
            value = enc[q, core, near, half].astype(F32) + arecv[q, near, half].astype(F32)
            y2send[q, half] = (value + y1recv[q, half, 1].astype(F32)).astype(BF16)
            remote(y2send.at[q, half], y2recv.at[q, half], 2, y2_rsem.at[q], to).start()

    def run_one(q):
        wait_recv(y2recv.at[q], y2_rsem.at[q])
        for d in (1, 2, 3, 0):
            r = (role + d) % 4
            for half in range(2):
                value = enc[q, core, y, half, r].astype(F32) + arecv[q, y, half, r].astype(F32)
                value = value + y1recv[q, half, 0, r].astype(F32) + y2recv[q, half, r].astype(F32)
                if d:
                    z1send[q, d - 1, half] = value.astype(BF16)
                else:
                    z1own[q, half] = value
            if d:
                remote(z1send.at[q, d - 1], z1recv.at[q, d - 1], 3, z1_rsem.at[q], mates[d - 1]).start()

    def run_two(q):
        wait_recv(z1recv.at[q], z1_rsem.at[q])

        def total(half):
            value = z1own[q, half]
            for d in range(3):
                value = value + z1recv[q, d, half].astype(F32)
            return value

        z2send[q] = total(1 - run).astype(BF16)
        remote(z2send.at[q], z2recv.at[q], 4, z2_rsem.at[q], across).start()
        z2own[q] = total(run)

    def owner_copy(owner):
        return remote(fsend.at[owner], frecv.at[outer], 5, f_rsem.at[0], inner, owner)

    def group_send(q):
        wait_recv(z2recv.at[q], z2_rsem.at[q])
        value = z2own[q] + z2recv[q].astype(F32)
        value = clip(value, lim2[q * CHUNK_ROWS : (q + 1) * CHUNK_ROWS, :]).astype(BF16)
        for h in range(OWNERS):
            owner = OWNERS * q + h
            fsend[owner] = value[h * 16 : (h + 1) * 16]

            @pl.when(owner != outer)
            def _():
                owner_copy(owner).start()

    stages = {
        "e": encode, "a": pair_send, "m": ring_one, "n": ring_two,
        "r": run_one, "s": run_two, "g": group_send,
    }
    for name, q in ORDER:
        if name == "a" and q == 0:
            pl.semaphore_wait(barrier, len(partners) + 7)
        stages[name](q)

    for stage, like in enumerate((arecv, y1send, y2send, z1send, z2send, fsend.at[pl.ds(0, 7)])):
        wait_send(like, stage)
    wait_recv(frecv.at[pl.ds(0, 7)], f_rsem.at[0])
    total = fsend[outer].astype(F32)
    for d in range(1, 8):
        total = total + frecv[(outer + d) % 8].astype(F32)
    high = total.astype(BF16)
    low = (total - high.astype(F32)).astype(BF16)
    signs = table[0:128, 0:128]
    result = jnp.dot(high, signs, preferred_element_type=F32)
    result = result + jnp.dot(low, signs, preferred_element_type=F32)
    out_ref[...] = result * F32(RSQRT)


def shards(grads, first_exponents, second_exponents):
    rows, columns = grads.shape[2], grads.shape[3]
    first = first_exponents.reshape(rows, columns // 128).T
    second = second_exponents.reshape(1, rows)
    operands = (grads.reshape(rows, columns), first, second)
    dma = pltpu.SemaphoreType.DMA
    c, r = CHUNKS, CHUNK_ROWS
    return pl.pallas_call(
        kernel,
        out_shape=jax.ShapeDtypeStruct((16, 128), F32),
        in_specs=[pl.BlockSpec(memory_space=pltpu.HBM)] * 3,
        out_specs=pl.BlockSpec(memory_space=pltpu.VMEM),
        scratch_shapes=[
            pltpu.VMEM((c, r, columns), F32),
            pltpu.VMEM((columns // 128, rows), jnp.int32),
            pltpu.VMEM((1, rows), jnp.int32),
            pltpu.VMEM((256, 256), BF16),
            pltpu.VMEM((128, 128), F32),
            pltpu.VMEM((128, 128), F32),
            pltpu.VMEM((c, 2, 4, 2, 4, r, 128), BF16),
            pltpu.VMEM((c, 4, 2, 4, r, 128), BF16),
            pltpu.VMEM((c, 2, 2, 4, r, 128), BF16),
            pltpu.VMEM((c, 2, 2, 4, r, 128), BF16),
            pltpu.VMEM((c, 2, 4, r, 128), BF16),
            pltpu.VMEM((c, 2, 4, r, 128), BF16),
            pltpu.VMEM((c, 3, 2, r, 128), BF16),
            pltpu.VMEM((c, 2, r, 128), F32),
            pltpu.VMEM((c, 3, 2, r, 128), BF16),
            pltpu.VMEM((c, r, 128), F32),
            pltpu.VMEM((c, r, 128), BF16),
            pltpu.VMEM((c, r, 128), BF16),
            pltpu.VMEM((8, 16, 128), BF16),
            pltpu.VMEM((8, 16, 128), BF16),
            dma((c,)),
            dma((2,)),
            dma((6,)),
            dma((c,)),
            dma((c,)),
            dma((c,)),
            dma((c,)),
            dma((c,)),
            dma((1,)),
        ],
        compiler_params=pltpu.CompilerParams(
            collective_id=0, has_side_effects=True, vmem_limit_bytes=48 * 1024 * 1024
        ),
        name="reduce_scatter",
    )(*(pltpu.with_memory_space_constraint(x, pltpu.HBM) for x in operands))


def solution(mesh):
    placed = (
        P("inner", "outer", None, None),
        P("inner", "outer", None, None),
        P("outer", None, "inner"),
    )
    return jax.shard_map(
        shards, mesh=mesh, in_specs=placed, out_specs=P("outer", "inner"), check_vma=False
    )
```

```python
import math

import jax
import jax.numpy as jnp
from jax import lax
from jax.experimental import pallas as pl
from jax.experimental.pallas import tpu as pltpu
from jax.sharding import PartitionSpec as P

SATURATION = 448.0
RSQRT = 1.0 / math.sqrt(128.0)
LOGICAL = pl.DeviceIdType.MESH
F32 = jnp.float32
BF16 = jnp.bfloat16
CHUNKS = 8
CHUNK_ROWS = 128 // CHUNKS
OWNERS = CHUNK_ROWS // 16
GROUP = 256 // CHUNK_ROWS
ORDER = tuple(
    (item[0], int(item[1:]))
    for line in (
        "e0 a0 e1 a1", "e2 a2 e3 m0", "a3 e4 m1 a4", "e5 m2 n0 a5", "e6 m3 n1 m4",
        "a6 e7 n2 m5", "r0 a7 n3 r1", "m6 n4 r2 n5", "m7 r3 s0 n6", "s1 r4 r5 n7",
        "s2 s3 r6 g0", "g1 s4 r7 s5", "g2 g3 s6 g4", "s7 g5 g6 g7",
    )
    for item in line.split()
)


def sign_table():
    row = lax.broadcasted_iota(jnp.int32, (256, 256), 0)
    col = lax.broadcasted_iota(jnp.int32, (256, 256), 1)
    shared = row & col & 127
    shared = shared ^ (shared >> 4)
    shared = shared ^ (shared >> 2)
    shared = shared ^ (shared >> 1)
    signs = (1 - 2 * (shared & 1)).astype(F32)
    return jnp.where((row // 128) == (col // 128), signs, 0.0).astype(BF16)


def limits(exponents):
    return jnp.left_shift(1, exponents + 13).astype(F32) * F32(SATURATION / 8192.0)


def clip(value, bound):
    return jnp.minimum(jnp.maximum(value, -bound), bound)


def kernel(
    grads_ref, first_ref, second_ref, out_ref,
    gbuf, first_buf, second_buf, table, lim1, lim2, enc, arecv,
    y1send, y1recv, y2send, y2recv, z1send, z1own, z1recv, z2own, z2send, z2recv, fsend, frecv,
    load_sem, scale_sem, send_sem, a_rsem, y1_rsem, y2_rsem, z1_rsem, z2_rsem, f_rsem,
):
    inner = lax.axis_index("inner")
    outer = lax.axis_index("outer")
    core = inner % 2
    z = (inner // 2) % 8
    y = inner // 16
    run, role = z // 4, z % 4
    y_one, y_two, y_far = y + 1 - 2 * (y % 2), 3 - y, (y + 2) % 4

    def inner_of(yy, zz, cc):
        return (yy * 8 + zz) * 2 + cc

    sibling = inner_of(y, z, 1 - core)
    pair_one = inner_of(y_one, z, core)
    pair_two = inner_of(y_two, z, core)
    across = inner_of(y, (1 - run) * 4 + role, core)
    mates = [inner_of(y, run * 4 + (role + d) % 4, core) for d in (1, 2, 3)]

    def remote(src, dst, stage, rsem, i, o=None):
        return pltpu.make_async_remote_copy(
            src_ref=src, dst_ref=dst, send_sem=send_sem.at[stage], recv_sem=rsem,
            device_id=(i, outer if o is None else o), device_id_type=LOGICAL,
        )

    def wait_recv(dst, rsem):
        remote(dst, dst, 0, rsem, sibling).wait_recv()

    def wait_send(like, stage):
        remote(like, like, stage, f_rsem.at[0], sibling).wait_send()

    scale_loads = [
        pltpu.make_async_copy(first_ref, first_buf, scale_sem.at[0]),
        pltpu.make_async_copy(second_ref, second_buf, scale_sem.at[1]),
    ]
    loads = [
        pltpu.make_async_copy(
            grads_ref.at[pl.ds(q * CHUNK_ROWS, CHUNK_ROWS)], gbuf.at[q], load_sem.at[q]
        )
        for q in range(CHUNKS)
    ]
    for load in scale_loads + loads:
        load.start()

    barrier = pltpu.get_barrier_semaphore()
    partners = [sibling, pair_one, pair_two, across] + mates
    for i in partners:
        pl.semaphore_signal(barrier, inc=1, device_id=(i, outer), device_id_type=LOGICAL)
    for d in range(1, 8):
        pl.semaphore_signal(
            barrier, inc=1, device_id=(inner, (outer + d) % 8), device_id_type=LOGICAL
        )

    table[...] = sign_table()
    for load in scale_loads:
        load.wait()
    first = limits(first_buf[...])
    lim1[...] = jnp.concatenate([first, first], axis=0).T.astype(BF16)
    lim2[...] = jnp.broadcast_to(limits(second_buf[...]), (128, 128)).T

    def encode(q):
        loads[q].wait()
        weights = table[...]
        rows = slice(q * CHUNK_ROWS, (q + 1) * CHUNK_ROWS)
        for base in range(0, 32, GROUP):
            lhs = jnp.concatenate(
                [
                    gbuf[q, :, (base + k) * 256 : (base + k + 1) * 256].astype(BF16)
                    for k in range(GROUP)
                ],
                axis=0,
            )
            rotated = jnp.dot(lhs, weights, preferred_element_type=F32) * F32(RSQRT)
            rotated = rotated.astype(BF16)
            for k in range(GROUP):
                pair = base + k
                for c in range(2):
                    block = 2 * pair + c
                    bound = jnp.broadcast_to(lim1[rows, block : block + 1], (CHUNK_ROWS, 128))
                    value = rotated[k * CHUNK_ROWS : (k + 1) * CHUNK_ROWS, c * 128 : (c + 1) * 128]
                    enc[q, c, pair // 8, pair % 8 // 4, pair % 4] = clip(value, bound)

    def pair_send(q):
        remote(enc.at[q, 1 - core], arecv.at[q], 0, a_rsem.at[q], sibling).start()

    def pair_sum(q, yy, half):
        return enc[q, core, yy, half] + arecv[q, yy, half]

    def ring_one(q):
        wait_recv(arecv.at[q], a_rsem.at[q])
        for half, near, to in ((0, y_one, pair_one), (1, y_two, pair_two)):
            y1send[q, half, 0] = pair_sum(q, near, half)
            y1send[q, half, 1] = pair_sum(q, y_far, half)
            remote(y1send.at[q, half], y1recv.at[q, half], 1, y1_rsem.at[q], to).start()

    def ring_two(q):
        wait_recv(y1recv.at[q], y1_rsem.at[q])
        for half, near, to in ((0, y_two, pair_two), (1, y_one, pair_one)):
            value = enc[q, core, near, half].astype(F32) + arecv[q, near, half].astype(F32)
            y2send[q, half] = (value + y1recv[q, half, 1].astype(F32)).astype(BF16)
            remote(y2send.at[q, half], y2recv.at[q, half], 2, y2_rsem.at[q], to).start()

    def run_one(q):
        wait_recv(y2recv.at[q], y2_rsem.at[q])
        for d in (1, 2, 3, 0):
            r = (role + d) % 4
            for half in range(2):
                value = enc[q, core, y, half, r].astype(F32) + arecv[q, y, half, r].astype(F32)
                value = value + y1recv[q, half, 0, r].astype(F32) + y2recv[q, half, r].astype(F32)
                if d:
                    z1send[q, d - 1, half] = value.astype(BF16)
                else:
                    z1own[q, half] = value
            if d:
                remote(z1send.at[q, d - 1], z1recv.at[q, d - 1], 3, z1_rsem.at[q], mates[d - 1]).start()

    def run_two(q):
        wait_recv(z1recv.at[q], z1_rsem.at[q])

        def total(half):
            value = z1own[q, half]
            for d in range(3):
                value = value + z1recv[q, d, half].astype(F32)
            return value

        z2send[q] = total(1 - run).astype(BF16)
        remote(z2send.at[q], z2recv.at[q], 4, z2_rsem.at[q], across).start()
        z2own[q] = total(run)

    def owner_copy(owner):
        return remote(fsend.at[owner], frecv.at[outer], 5, f_rsem.at[0], inner, owner)

    def group_send(q):
        wait_recv(z2recv.at[q], z2_rsem.at[q])
        value = z2own[q] + z2recv[q].astype(F32)
        value = clip(value, lim2[q * CHUNK_ROWS : (q + 1) * CHUNK_ROWS, :]).astype(BF16)
        for h in range(OWNERS):
            owner = OWNERS * q + h
            fsend[owner] = value[h * 16 : (h + 1) * 16]

            @pl.when(owner != outer)
            def _():
                owner_copy(owner).start()

    stages = {
        "e": encode, "a": pair_send, "m": ring_one, "n": ring_two,
        "r": run_one, "s": run_two, "g": group_send,
    }
    for name, q in ORDER:
        if name == "a" and q == 0:
            pl.semaphore_wait(barrier, len(partners) + 7)
        stages[name](q)

    for stage, like in enumerate((arecv, y1send, y2send, z1send, z2send, fsend.at[pl.ds(0, 7)])):
        wait_send(like, stage)
    wait_recv(frecv.at[pl.ds(0, 7)], f_rsem.at[0])
    total = fsend[outer].astype(F32)
    for d in range(1, 8):
        total = total + frecv[(outer + d) % 8].astype(F32)
    high = total.astype(BF16)
    low = (total - high.astype(F32)).astype(BF16)
    signs = table[0:128, 0:128]
    result = jnp.dot(high, signs, preferred_element_type=F32)
    result = result + jnp.dot(low, signs, preferred_element_type=F32)
    out_ref[...] = result * F32(RSQRT)


def shards(grads, first_exponents, second_exponents):
    rows, columns = grads.shape[2], grads.shape[3]
    first = first_exponents.reshape(rows, columns // 128).T
    second = second_exponents.reshape(1, rows)
    operands = (grads.reshape(rows, columns), first, second)
    dma = pltpu.SemaphoreType.DMA
    c, r = CHUNKS, CHUNK_ROWS
    return pl.pallas_call(
        kernel,
        out_shape=jax.ShapeDtypeStruct((16, 128), F32),
        in_specs=[pl.BlockSpec(memory_space=pltpu.HBM)] * 3,
        out_specs=pl.BlockSpec(memory_space=pltpu.VMEM),
        scratch_shapes=[
            pltpu.VMEM((c, r, columns), F32),
            pltpu.VMEM((columns // 128, rows), jnp.int32),
            pltpu.VMEM((1, rows), jnp.int32),
            pltpu.VMEM((256, 256), BF16),
            pltpu.VMEM((128, 128), BF16),
            pltpu.VMEM((128, 128), F32),
            pltpu.VMEM((c, 2, 4, 2, 4, r, 128), BF16),
            pltpu.VMEM((c, 4, 2, 4, r, 128), BF16),
            pltpu.VMEM((c, 2, 2, 4, r, 128), BF16),
            pltpu.VMEM((c, 2, 2, 4, r, 128), BF16),
            pltpu.VMEM((c, 2, 4, r, 128), BF16),
            pltpu.VMEM((c, 2, 4, r, 128), BF16),
            pltpu.VMEM((c, 3, 2, r, 128), BF16),
            pltpu.VMEM((c, 2, r, 128), F32),
            pltpu.VMEM((c, 3, 2, r, 128), BF16),
            pltpu.VMEM((c, r, 128), F32),
            pltpu.VMEM((c, r, 128), BF16),
            pltpu.VMEM((c, r, 128), BF16),
            pltpu.VMEM((8, 16, 128), BF16),
            pltpu.VMEM((8, 16, 128), BF16),
            dma((c,)),
            dma((2,)),
            dma((6,)),
            dma((c,)),
            dma((c,)),
            dma((c,)),
            dma((c,)),
            dma((c,)),
            dma((1,)),
        ],
        compiler_params=pltpu.CompilerParams(
            collective_id=0, has_side_effects=True, vmem_limit_bytes=48 * 1024 * 1024
        ),
        name="reduce_scatter",
    )(*(pltpu.with_memory_space_constraint(x, pltpu.HBM) for x in operands))


def solution(mesh):
    placed = (
        P("inner", "outer", None, None),
        P("inner", "outer", None, None),
        P("outer", None, "inner"),
    )
    return jax.shard_map(
        shards, mesh=mesh, in_specs=placed, out_specs=P("outer", "inner"), check_vma=False
    )
```

```python
import math

import jax
import jax.numpy as jnp
from jax import lax
from jax.experimental import pallas as pl
from jax.experimental.pallas import tpu as pltpu
from jax.sharding import PartitionSpec as P

SATURATION = 448.0
RSQRT = 1.0 / math.sqrt(128.0)
LOGICAL = pl.DeviceIdType.MESH
F32 = jnp.float32
BF16 = jnp.bfloat16
CHUNKS = 8
CHUNK_ROWS = 128 // CHUNKS
OWNERS = CHUNK_ROWS // 16
GROUP = 512 // CHUNK_ROWS
ORDER = tuple(
    (item[0], int(item[1:]))
    for line in (
        "e0 a0 e1 a1", "e2 a2 e3 a3", "l0 e4 a4 e5", "a5 m0 e6 a6", "m1 e7 a7 m2",
        "m3 m4 m5 n0", "n1 m6 n2 m7", "n3 n4 r0 n5", "r1 n6 r2 n7", "r3 r4 r5 s0",
        "r6 s1 r7 s2", "s3 s4 s5 s6", "s7",
    )
    for item in line.split()
)


def sign_table():
    row = lax.broadcasted_iota(jnp.int32, (256, 256), 0)
    col = lax.broadcasted_iota(jnp.int32, (256, 256), 1)
    shared = row & col & 127
    shared = shared ^ (shared >> 4)
    shared = shared ^ (shared >> 2)
    shared = shared ^ (shared >> 1)
    signs = (1 - 2 * (shared & 1)).astype(F32)
    return jnp.where((row // 128) == (col // 128), signs, 0.0).astype(BF16)


def limits(exponents):
    return jnp.left_shift(1, exponents + 13).astype(F32) * F32(SATURATION / 8192.0)


def clip(value, bound):
    return jnp.minimum(jnp.maximum(value, -bound), bound)


def kernel(
    grads_ref, first_ref, second_ref, out_ref,
    gbuf, first_buf, second_buf, table, lim1, lim2, enc, arecv,
    y1send, y1recv, y2send, y2recv, z1send, z1own, z1recv, fsend, frecv, limrecv,
    load_sem, scale_sem, send_sem, a_rsem, y1_rsem, y2_rsem, z1_rsem, l_rsem, f_rsem,
):
    inner = lax.axis_index("inner")
    outer = lax.axis_index("outer")
    core = inner % 2
    z = (inner // 2) % 8
    y = inner // 16
    run, role = z // 4, z % 4
    y_right, y_left, y_far = (y + 1) % 4, (y + 3) % 4, (y + 2) % 4

    def inner_of(yy, zz, cc):
        return (yy * 8 + zz) * 2 + cc

    sibling = inner_of(y, z, 1 - core)
    right = inner_of(y_right, z, core)
    left = inner_of(y_left, z, core)
    across = inner_of(y, (1 - run) * 4 + role, core)
    mates = [inner_of(y, run * 4 + (role + d) % 4, core) for d in (1, 2, 3)]

    def remote(src, dst, stage, rsem, i, o=None):
        return pltpu.make_async_remote_copy(
            src_ref=src, dst_ref=dst, send_sem=send_sem.at[stage], recv_sem=rsem,
            device_id=(i, outer if o is None else o), device_id_type=LOGICAL,
        )

    def wait_recv(dst, rsem):
        remote(dst, dst, 0, rsem, sibling).wait_recv()

    def wait_send(like, stage):
        remote(like, like, stage, f_rsem.at[0], sibling).wait_send()

    scale_loads = [
        pltpu.make_async_copy(first_ref, first_buf, scale_sem.at[0]),
        pltpu.make_async_copy(second_ref, second_buf, scale_sem.at[1]),
    ]
    loads = [
        pltpu.make_async_copy(
            grads_ref.at[pl.ds(q * CHUNK_ROWS, CHUNK_ROWS)], gbuf.at[q], load_sem.at[q]
        )
        for q in range(CHUNKS)
    ]
    for load in scale_loads + loads:
        load.start()

    barrier = pltpu.get_barrier_semaphore()
    partners = [sibling, right, left, across] + mates
    for i in partners:
        pl.semaphore_signal(barrier, inc=1, device_id=(i, outer), device_id_type=LOGICAL)
    for d in range(1, 8):
        for i in (inner, across):
            pl.semaphore_signal(
                barrier, inc=1, device_id=(i, (outer + d) % 8), device_id_type=LOGICAL
            )

    table[...] = sign_table()
    for load in scale_loads:
        load.wait()
    first = limits(first_buf[...])
    lim1[...] = jnp.concatenate([first, first], axis=0).T.astype(BF16)
    second = jnp.broadcast_to(limits(second_buf[...]), (128, 128)).T.astype(BF16)
    for owner in range(8):
        lim2[owner] = second[owner * 16 : (owner + 1) * 16]
    limrecv[outer] = lim2[outer]

    def encode(q):
        loads[q].wait()
        weights = table[...]
        rows = slice(q * CHUNK_ROWS, (q + 1) * CHUNK_ROWS)
        for base in range(0, 32, GROUP):
            lhs = jnp.concatenate(
                [
                    gbuf[q, :, (base + k) * 256 : (base + k + 1) * 256].astype(BF16)
                    for k in range(GROUP)
                ],
                axis=0,
            )
            rotated = jnp.dot(lhs, weights, preferred_element_type=F32) * F32(RSQRT)
            rotated = rotated.astype(BF16)
            for k in range(GROUP):
                pair = base + k
                for c in range(2):
                    block = 2 * pair + c
                    bound = jnp.broadcast_to(lim1[rows, block : block + 1], (CHUNK_ROWS, 128))
                    value = rotated[k * CHUNK_ROWS : (k + 1) * CHUNK_ROWS, c * 128 : (c + 1) * 128]
                    enc[q, c, pair // 8, pair % 8 // 4, pair % 4] = clip(value, bound)

    def pair_send(q):
        remote(enc.at[q, 1 - core], arecv.at[q], 0, a_rsem.at[q], sibling).start()

    def pair_sum(q, yy, half):
        return enc[q, core, yy, half] + arecv[q, yy, half]

    def limit_send(q):
        for d in range(1, 8):
            owner = (outer + d) % 8
            remote(lim2.at[owner], limrecv.at[outer], 4, l_rsem.at[0], inner, owner).start()

    def ring_one(q):
        wait_recv(arecv.at[q], a_rsem.at[q])
        for way, to in ((0, right), (1, left)):
            y1send[q, way] = pair_sum(q, y_far, way)
            remote(y1send.at[q, way], y1recv.at[q, way], 1, y1_rsem.at[q], to).start()
        for way, near, to in ((0, y_right, right), (1, y_left, left)):
            y2send[q, way, 0] = pair_sum(q, near, 1 - way)
            remote(y2send.at[q, way, 0], y2recv.at[q, way, 0], 2, y2_rsem.at[q], to).start()

    def ring_two(q):
        wait_recv(y1recv.at[q], y1_rsem.at[q])
        for way, near, to in ((0, y_right, right), (1, y_left, left)):
            value = enc[q, core, near, way].astype(F32) + arecv[q, near, way].astype(F32)
            y2send[q, way, 1] = (value + y1recv[q, way].astype(F32)).astype(BF16)
            remote(y2send.at[q, way, 1], y2recv.at[q, way, 1], 2, y2_rsem.at[q], to).start()

    def run_one(q):
        wait_recv(y2recv.at[q], y2_rsem.at[q])
        for d in (1, 2, 3, 0):
            r = (role + d) % 4
            for half in range(2):
                value = enc[q, core, y, half, r].astype(F32) + arecv[q, y, half, r].astype(F32)
                value = value + y2recv[q, half, 1, r].astype(F32) + y2recv[q, 1 - half, 0, r].astype(F32)
                if d:
                    z1send[q, d - 1, half] = value.astype(BF16)
                else:
                    z1own[q, half] = value
            if d:
                remote(z1send.at[q, d - 1], z1recv.at[q, d - 1], 3, z1_rsem.at[q], mates[d - 1]).start()

    def run_two(q):
        wait_recv(z1recv.at[q], z1_rsem.at[q])
        for half in range(2):
            value = z1own[q, half]
            for d in range(3):
                value = value + z1recv[q, d, half].astype(F32)
            for h in range(OWNERS):
                owner = OWNERS * q + h
                fsend[half, owner] = value[h * 16 : (h + 1) * 16].astype(BF16)
                here = jnp.logical_and(owner == outer, half == run)

                @pl.when(jnp.logical_not(here))
                def _():
                    remote(
                        fsend.at[half, owner], frecv.at[8 * run + outer], 5, f_rsem.at[0],
                        inner_of(y, 4 * half + role, core), owner,
                    ).start()

    stages = {
        "e": encode, "a": pair_send, "l": limit_send, "m": ring_one, "n": ring_two,
        "r": run_one, "s": run_two,
    }
    for name, q in ORDER:
        if name == "a" and q == 0:
            pl.semaphore_wait(barrier, len(partners) + 14)
        stages[name](q)

    frecv[8 * run + outer] = fsend[run, outer]
    for stage, like in enumerate(
        (arecv, y1send, y2send, z1send, lim2.at[pl.ds(0, 7)], frecv.at[pl.ds(0, 15)])
    ):
        wait_send(like, stage)
    wait_recv(limrecv.at[pl.ds(0, 7)], l_rsem.at[0])
    wait_recv(frecv.at[pl.ds(0, 15)], f_rsem.at[0])
    total = jnp.zeros((16, 128), F32)
    for group in range(8):
        value = frecv[group].astype(F32) + frecv[8 + group].astype(F32)
        total = total + clip(value, limrecv[group].astype(F32))
    high = total.astype(BF16)
    low = (total - high.astype(F32)).astype(BF16)
    signs = table[0:128, 0:128]
    result = jnp.dot(high, signs, preferred_element_type=F32)
    result = result + jnp.dot(low, signs, preferred_element_type=F32)
    out_ref[...] = result * F32(RSQRT)


def shards(grads, first_exponents, second_exponents):
    rows, columns = grads.shape[2], grads.shape[3]
    first = first_exponents.reshape(rows, columns // 128).T
    second = second_exponents.reshape(1, rows)
    operands = (grads.reshape(rows, columns), first, second)
    dma = pltpu.SemaphoreType.DMA
    c, r = CHUNKS, CHUNK_ROWS
    return pl.pallas_call(
        kernel,
        out_shape=jax.ShapeDtypeStruct((16, 128), F32),
        in_specs=[pl.BlockSpec(memory_space=pltpu.HBM)] * 3,
        out_specs=pl.BlockSpec(memory_space=pltpu.VMEM),
        scratch_shapes=[
            pltpu.VMEM((c, r, columns), F32),
            pltpu.VMEM((columns // 128, rows), jnp.int32),
            pltpu.VMEM((1, rows), jnp.int32),
            pltpu.VMEM((256, 256), BF16),
            pltpu.VMEM((128, 128), BF16),
            pltpu.VMEM((8, 16, 128), BF16),
            pltpu.VMEM((c, 2, 4, 2, 4, r, 128), BF16),
            pltpu.VMEM((c, 4, 2, 4, r, 128), BF16),
            pltpu.VMEM((c, 2, 4, r, 128), BF16),
            pltpu.VMEM((c, 2, 4, r, 128), BF16),
            pltpu.VMEM((c, 2, 2, 4, r, 128), BF16),
            pltpu.VMEM((c, 2, 2, 4, r, 128), BF16),
            pltpu.VMEM((c, 3, 2, r, 128), BF16),
            pltpu.VMEM((c, 2, r, 128), F32),
            pltpu.VMEM((c, 3, 2, r, 128), BF16),
            pltpu.VMEM((2, 8, 16, 128), BF16),
            pltpu.VMEM((16, 16, 128), BF16),
            pltpu.VMEM((8, 16, 128), BF16),
            dma((c,)),
            dma((2,)),
            dma((6,)),
            dma((c,)),
            dma((c,)),
            dma((c,)),
            dma((c,)),
            dma((1,)),
            dma((1,)),
        ],
        compiler_params=pltpu.CompilerParams(
            collective_id=0, has_side_effects=True, vmem_limit_bytes=48 * 1024 * 1024
        ),
        name="reduce_scatter",
    )(*(pltpu.with_memory_space_constraint(x, pltpu.HBM) for x in operands))


def solution(mesh):
    placed = (
        P("inner", "outer", None, None),
        P("inner", "outer", None, None),
        P("outer", None, "inner"),
    )
    return jax.shard_map(
        shards, mesh=mesh, in_specs=placed, out_specs=P("outer", "inner"), check_vma=False
    )
```

```python
import math

import jax
import jax.numpy as jnp
from jax import lax
from jax.experimental import pallas as pl
from jax.experimental.pallas import tpu as pltpu
from jax.sharding import PartitionSpec as P

SATURATION = 448.0
RSQRT = 1.0 / math.sqrt(128.0)
LOGICAL = pl.DeviceIdType.MESH
F32 = jnp.float32
BF16 = jnp.bfloat16
CHUNKS = 4
CHUNK_ROWS = 128 // CHUNKS
OWNERS = CHUNK_ROWS // 16
ORDER = tuple(
    (item[0], int(item[1:]))
    for line in (
        "f0 f1 f2 h0", "f3 h1 l0 m0", "m1 h2 m2 h3", "m3 o0 k0 o1", "n0 k1 n1 k2",
        "o2 n2 k3 n3", "o3 r0 r1 r2", "r3 s0 s1 s2", "s3",
    )
    for item in line.split()
)


def sign_table():
    row = lax.broadcasted_iota(jnp.int32, (256, 256), 0)
    col = lax.broadcasted_iota(jnp.int32, (256, 256), 1)
    shared = row & col & 127
    shared = shared ^ (shared >> 4)
    shared = shared ^ (shared >> 2)
    shared = shared ^ (shared >> 1)
    signs = (1 - 2 * (shared & 1)).astype(F32)
    return jnp.where((row // 128) == (col // 128), signs, 0.0).astype(BF16)


def limits(exponents):
    return jnp.left_shift(1, exponents + 13).astype(F32) * F32(SATURATION / 8192.0)


def clip(value, bound):
    return jnp.minimum(jnp.maximum(value, -bound), bound)


def kernel(
    grads_ref, first_ref, second_ref, out_ref,
    gbuf, first_buf, second_buf, table, lim1, lim2, enc, arecv,
    y1send, y1recv, y2send, y2recv, z1send, z1own, z1recv, fsend, frecv, limrecv,
    load_sem, scale_sem, send_sem, a_rsem, y1_rsem, y2_rsem, z1_rsem, l_rsem, f_rsem,
):
    inner = lax.axis_index("inner")
    outer = lax.axis_index("outer")
    core = inner % 2
    z = (inner // 2) % 8
    y = inner // 16
    run, role = z // 4, z % 4
    y_right, y_left, y_far = (y + 1) % 4, (y + 3) % 4, (y + 2) % 4

    def inner_of(yy, zz, cc):
        return (yy * 8 + zz) * 2 + cc

    sibling = inner_of(y, z, 1 - core)
    right = inner_of(y_right, z, core)
    left = inner_of(y_left, z, core)
    across = inner_of(y, (1 - run) * 4 + role, core)
    mates = [inner_of(y, run * 4 + (role + d) % 4, core) for d in (1, 2, 3)]

    def remote(src, dst, stage, rsem, i, o=None):
        return pltpu.make_async_remote_copy(
            src_ref=src, dst_ref=dst, send_sem=send_sem.at[stage], recv_sem=rsem,
            device_id=(i, outer if o is None else o), device_id_type=LOGICAL,
        )

    def wait_recv(dst, rsem):
        remote(dst, dst, 0, rsem, sibling).wait_recv()

    def wait_send(like, stage):
        remote(like, like, stage, f_rsem.at[0], sibling).wait_send()

    scale_loads = [
        pltpu.make_async_copy(first_ref, first_buf, scale_sem.at[0]),
        pltpu.make_async_copy(second_ref, second_buf, scale_sem.at[1]),
    ]
    places = (y_far, y_right, y_left, y)
    parts = {"f": (0,), "h": (1, 2), "o": (3,)}

    def load(q, d):
        columns = pl.ds(pl.multiple_of(places[d] * 2048, 2048), 2048)
        return pltpu.make_async_copy(
            grads_ref.at[pl.ds(q * CHUNK_ROWS, CHUNK_ROWS), columns], gbuf.at[q, d], load_sem.at[q, d]
        )

    for copy in scale_loads:
        copy.start()
    for part in parts.values():
        for q in range(CHUNKS):
            for d in part:
                load(q, d).start()

    barrier = pltpu.get_barrier_semaphore()
    partners = [sibling, right, left, across] + mates
    for i in partners:
        pl.semaphore_signal(barrier, inc=1, device_id=(i, outer), device_id_type=LOGICAL)
    for d in range(1, 8):
        for i in (inner, across):
            pl.semaphore_signal(
                barrier, inc=1, device_id=(i, (outer + d) % 8), device_id_type=LOGICAL
            )

    table[...] = sign_table()
    for copy in scale_loads:
        copy.wait()
    first = jnp.concatenate(
        [first_buf[pl.ds(pl.multiple_of(place * 16, 16), 16), :] for place in places] * 2, axis=0
    )
    lim1[...] = limits(first).T.astype(BF16)
    second = jnp.broadcast_to(limits(second_buf[...]), (128, 128)).T.astype(BF16)
    for owner in range(8):
        lim2[owner] = second[owner * 16 : (owner + 1) * 16]
    limrecv[outer] = lim2[outer]

    def encode(q, part):
        rows = slice(q * CHUNK_ROWS, (q + 1) * CHUNK_ROWS)
        pairs = [(d, k) for d in parts[part] for k in range(8)]
        for d in parts[part]:
            load(q, d).wait()
        lhs = jnp.concatenate(
            [gbuf[q, d, :, k * 256 : (k + 1) * 256].astype(BF16) for d, k in pairs], axis=0
        )
        rotated = jnp.dot(lhs, table[...], preferred_element_type=F32) * F32(RSQRT)
        rotated = rotated.astype(BF16)
        for i, (d, k) in enumerate(pairs):
            for c in range(2):
                lane = 16 * d + 2 * k + c
                bound = jnp.broadcast_to(lim1[rows, lane : lane + 1], (CHUNK_ROWS, 128))
                value = rotated[i * CHUNK_ROWS : (i + 1) * CHUNK_ROWS, c * 128 : (c + 1) * 128]
                enc[q, c, d, k // 4, k % 4] = clip(value, bound)

    def part_copy(q, part):
        span = pl.ds(parts[part][0], len(parts[part]))
        return remote(
            enc.at[q, 1 - core, span], arecv.at[q, span], 0,
            a_rsem.at[q, parts[part][0]], sibling,
        )

    def encode_send(part):
        def stage(q):
            encode(q, part)
            if part == "f" and q == 0:
                pl.semaphore_wait(barrier, len(partners) + 14)
            part_copy(q, part).start()

        return stage

    def pair_sum(q, d, half):
        return enc[q, core, d, half] + arecv[q, d, half]

    def limit_send(q):
        for d in range(1, 8):
            owner = (outer + d) % 8
            remote(lim2.at[owner], limrecv.at[outer], 4, l_rsem.at[0], inner, owner).start()

    def ring_far(q):
        part_copy(q, "f").wait_recv()
        for way, to in ((0, right), (1, left)):
            y1send[q, way] = pair_sum(q, 0, way)
            remote(y1send.at[q, way], y1recv.at[q, way], 1, y1_rsem.at[q], to).start()

    def ring_near(q):
        part_copy(q, "h").wait_recv()
        for way, to in ((0, right), (1, left)):
            y2send[q, way, 0] = pair_sum(q, 1 + way, 1 - way)
            remote(y2send.at[q, way, 0], y2recv.at[q, way, 0], 2, y2_rsem.at[q], to).start()

    def ring_on(q):
        wait_recv(y1recv.at[q], y1_rsem.at[q])
        for way, to in ((0, right), (1, left)):
            value = enc[q, core, 1 + way, way].astype(F32) + arecv[q, 1 + way, way].astype(F32)
            y2send[q, way, 1] = (value + y1recv[q, way].astype(F32)).astype(BF16)
            remote(y2send.at[q, way, 1], y2recv.at[q, way, 1], 2, y2_rsem.at[q], to).start()

    def run_one(q):
        part_copy(q, "o").wait_recv()
        wait_recv(y2recv.at[q], y2_rsem.at[q])
        for d in (1, 2, 3, 0):
            r = (role + d) % 4
            for half in range(2):
                value = enc[q, core, 3, half, r].astype(F32) + arecv[q, 3, half, r].astype(F32)
                value = value + y2recv[q, half, 1, r].astype(F32) + y2recv[q, 1 - half, 0, r].astype(F32)
                if d:
                    z1send[q, d - 1, half] = value.astype(BF16)
                else:
                    z1own[q, half] = value
            if d:
                remote(z1send.at[q, d - 1], z1recv.at[q, d - 1], 3, z1_rsem.at[q], mates[d - 1]).start()

    def run_two(q):
        wait_recv(z1recv.at[q], z1_rsem.at[q])
        for half in range(2):
            value = z1own[q, half]
            for d in range(3):
                value = value + z1recv[q, d, half].astype(F32)
            for h in range(OWNERS):
                owner = OWNERS * q + h
                fsend[half, owner] = value[h * 16 : (h + 1) * 16].astype(BF16)
                here = jnp.logical_and(owner == outer, half == run)

                @pl.when(jnp.logical_not(here))
                def _():
                    remote(
                        fsend.at[half, owner], frecv.at[8 * run + outer], 5, f_rsem.at[0],
                        inner_of(y, 4 * half + role, core), owner,
                    ).start()

    stages = {part: encode_send(part) for part in parts}
    stages.update(l=limit_send, m=ring_far, k=ring_near, n=ring_on, r=run_one, s=run_two)
    for name, q in ORDER:
        stages[name](q)

    frecv[8 * run + outer] = fsend[run, outer]
    for stage, like in enumerate(
        (arecv, y1send, y2send, z1send, lim2.at[pl.ds(0, 7)], frecv.at[pl.ds(0, 15)])
    ):
        wait_send(like, stage)
    wait_recv(limrecv.at[pl.ds(0, 7)], l_rsem.at[0])
    wait_recv(frecv.at[pl.ds(0, 15)], f_rsem.at[0])
    total = jnp.zeros((16, 128), F32)
    for group in range(8):
        value = frecv[group].astype(F32) + frecv[8 + group].astype(F32)
        total = total + clip(value, limrecv[group].astype(F32))
    high = total.astype(BF16)
    low = (total - high.astype(F32)).astype(BF16)
    signs = table[0:128, 0:128]
    result = jnp.dot(high, signs, preferred_element_type=F32)
    result = result + jnp.dot(low, signs, preferred_element_type=F32)
    out_ref[...] = result * F32(RSQRT)


def shards(grads, first_exponents, second_exponents):
    rows, columns = grads.shape[2], grads.shape[3]
    first = first_exponents.reshape(rows, columns // 128).T
    second = second_exponents.reshape(1, rows)
    operands = (grads.reshape(rows, columns), first, second)
    dma = pltpu.SemaphoreType.DMA
    c, r = CHUNKS, CHUNK_ROWS
    return pl.pallas_call(
        kernel,
        out_shape=jax.ShapeDtypeStruct((16, 128), F32),
        in_specs=[pl.BlockSpec(memory_space=pltpu.HBM)] * 3,
        out_specs=pl.BlockSpec(memory_space=pltpu.VMEM),
        scratch_shapes=[
            pltpu.VMEM((c, 4, r, columns // 4), F32),
            pltpu.VMEM((columns // 128, rows), jnp.int32),
            pltpu.VMEM((1, rows), jnp.int32),
            pltpu.VMEM((256, 256), BF16),
            pltpu.VMEM((128, 128), BF16),
            pltpu.VMEM((8, 16, 128), BF16),
            pltpu.VMEM((c, 2, 4, 2, 4, r, 128), BF16),
            pltpu.VMEM((c, 4, 2, 4, r, 128), BF16),
            pltpu.VMEM((c, 2, 4, r, 128), BF16),
            pltpu.VMEM((c, 2, 4, r, 128), BF16),
            pltpu.VMEM((c, 2, 2, 4, r, 128), BF16),
            pltpu.VMEM((c, 2, 2, 4, r, 128), BF16),
            pltpu.VMEM((c, 3, 2, r, 128), BF16),
            pltpu.VMEM((c, 2, r, 128), F32),
            pltpu.VMEM((c, 3, 2, r, 128), BF16),
            pltpu.VMEM((2, 8, 16, 128), BF16),
            pltpu.VMEM((16, 16, 128), BF16),
            pltpu.VMEM((8, 16, 128), BF16),
            dma((c, 4)),
            dma((2,)),
            dma((6,)),
            dma((c, 4)),
            dma((c,)),
            dma((c,)),
            dma((c,)),
            dma((1,)),
            dma((1,)),
        ],
        compiler_params=pltpu.CompilerParams(
            collective_id=0, has_side_effects=True, vmem_limit_bytes=48 * 1024 * 1024
        ),
        name="reduce_scatter",
    )(*(pltpu.with_memory_space_constraint(x, pltpu.HBM) for x in operands))


def solution(mesh):
    placed = (
        P("inner", "outer", None, None),
        P("inner", "outer", None, None),
        P("outer", None, "inner"),
    )
    return jax.shard_map(
        shards, mesh=mesh, in_specs=placed, out_specs=P("outer", "inner"), check_vma=False
    )
```

```python
import math

import jax
import jax.numpy as jnp
from jax import lax
from jax.experimental import pallas as pl
from jax.experimental.pallas import tpu as pltpu
from jax.sharding import PartitionSpec as P

SATURATION = 448.0
RSQRT = 1.0 / math.sqrt(128.0)
LOGICAL = pl.DeviceIdType.MESH
F32 = jnp.float32
BF16 = jnp.bfloat16
CHUNKS = 4
CHUNK_ROWS = 128 // CHUNKS
OWNERS = CHUNK_ROWS // 16
ORDER = tuple(
    (item[0], int(item[1:]))
    for line in (
        "f0 f1 f2 f3", "h0 h1 h2 m0", "m1 h3 m2 m3", "o0 o1 o2 o3", "k0 k1 k2 k3",
        "l0 n0 n1 n2", "n3 r0 r1 r2", "r3 s0 s1 s2", "s3",
    )
    for item in line.split()
)


def sign_table():
    row = lax.broadcasted_iota(jnp.int32, (256, 256), 0)
    col = lax.broadcasted_iota(jnp.int32, (256, 256), 1)
    shared = row & col & 127
    shared = shared ^ (shared >> 4)
    shared = shared ^ (shared >> 2)
    shared = shared ^ (shared >> 1)
    signs = (1 - 2 * (shared & 1)).astype(F32)
    return jnp.where((row // 128) == (col // 128), signs, 0.0).astype(BF16)


def limits(exponents):
    return jnp.left_shift(1, exponents + 13).astype(F32) * F32(SATURATION / 8192.0)


def clip(value, bound):
    return jnp.minimum(jnp.maximum(value, -bound), bound)


def kernel(
    grads_ref, first_ref, second_ref, out_ref,
    gbuf, first_buf, second_buf, table, lim1, lim2, enc, arecv,
    y1send, y1recv, y2send, y2recv, z1send, z1own, z1recv, fsend, frecv, limrecv,
    load_sem, scale_sem, send_sem, a_rsem, y1_rsem, y2_rsem, z1_rsem, l_rsem, f_rsem,
):
    inner = lax.axis_index("inner")
    outer = lax.axis_index("outer")
    core = inner % 2
    z = (inner // 2) % 8
    y = inner // 16
    run, role = z // 4, z % 4
    y_right, y_left, y_far = (y + 1) % 4, (y + 3) % 4, (y + 2) % 4

    def inner_of(yy, zz, cc):
        return (yy * 8 + zz) * 2 + cc

    sibling = inner_of(y, z, 1 - core)
    right = inner_of(y_right, z, core)
    left = inner_of(y_left, z, core)
    across = inner_of(y, (1 - run) * 4 + role, core)
    mates = [inner_of(y, run * 4 + (role + d) % 4, core) for d in (1, 2, 3)]

    def remote(src, dst, stage, rsem, i, o=None):
        return pltpu.make_async_remote_copy(
            src_ref=src, dst_ref=dst, send_sem=send_sem.at[stage], recv_sem=rsem,
            device_id=(i, outer if o is None else o), device_id_type=LOGICAL,
        )

    def wait_recv(dst, rsem):
        remote(dst, dst, 0, rsem, sibling).wait_recv()

    def wait_send(like, stage):
        remote(like, like, stage, f_rsem.at[0], sibling).wait_send()

    scale_loads = [
        pltpu.make_async_copy(first_ref, first_buf, scale_sem.at[0]),
        pltpu.make_async_copy(second_ref, second_buf, scale_sem.at[1]),
    ]
    places = (y_far, y_right, y_left, y)
    parts = {"f": (0,), "h": (1, 2), "o": (3,)}

    def load(q, d):
        columns = pl.ds(pl.multiple_of(places[d] * 2048, 2048), 2048)
        return pltpu.make_async_copy(
            grads_ref.at[pl.ds(q * CHUNK_ROWS, CHUNK_ROWS), columns], gbuf.at[q, d], load_sem.at[q, d]
        )

    def start_loads(part):
        for q in range(CHUNKS):
            for d in parts[part]:
                load(q, d).start()

    for copy in scale_loads:
        copy.start()
    start_loads("f")

    barrier = pltpu.get_barrier_semaphore()
    partners = [sibling, right, left, across] + mates
    for i in partners:
        pl.semaphore_signal(barrier, inc=1, device_id=(i, outer), device_id_type=LOGICAL)
    for d in range(1, 8):
        for i in (inner, across):
            pl.semaphore_signal(
                barrier, inc=1, device_id=(i, (outer + d) % 8), device_id_type=LOGICAL
            )

    start_loads("h")
    start_loads("o")
    table[...] = sign_table()
    for copy in scale_loads:
        copy.wait()
    first = jnp.concatenate(
        [first_buf[pl.ds(pl.multiple_of(place * 16, 16), 16), :] for place in places] * 2, axis=0
    )
    lim1[...] = limits(first).T.astype(BF16)
    second = jnp.broadcast_to(limits(second_buf[...]), (128, 128)).T.astype(BF16)
    for owner in range(8):
        lim2[owner] = second[owner * 16 : (owner + 1) * 16]
    limrecv[outer] = lim2[outer]

    def encode(q, part):
        rows = slice(q * CHUNK_ROWS, (q + 1) * CHUNK_ROWS)
        pairs = [(d, k) for d in parts[part] for k in range(8)]
        for d in parts[part]:
            load(q, d).wait()
        lhs = jnp.concatenate(
            [gbuf[q, d, :, k * 256 : (k + 1) * 256].astype(BF16) for d, k in pairs], axis=0
        )
        rotated = jnp.dot(lhs, table[...], preferred_element_type=F32) * F32(RSQRT)
        rotated = rotated.astype(BF16)
        for i, (d, k) in enumerate(pairs):
            for c in range(2):
                lane = 16 * d + 2 * k + c
                bound = jnp.broadcast_to(lim1[rows, lane : lane + 1], (CHUNK_ROWS, 128))
                value = rotated[i * CHUNK_ROWS : (i + 1) * CHUNK_ROWS, c * 128 : (c + 1) * 128]
                enc[q, c, d, k // 4, k % 4] = clip(value, bound)

    def part_copy(q, part):
        span = pl.ds(parts[part][0], len(parts[part]))
        return remote(
            enc.at[q, 1 - core, span], arecv.at[q, span], 0,
            a_rsem.at[q, parts[part][0]], sibling,
        )

    def encode_send(part):
        def stage(q):
            encode(q, part)
            if part == "f" and q == 0:
                pl.semaphore_wait(barrier, len(partners) + 14)
            part_copy(q, part).start()

        return stage

    def pair_sum(q, d, half):
        return enc[q, core, d, half] + arecv[q, d, half]

    def limit_send(q):
        for d in range(1, 8):
            owner = (outer + d) % 8
            remote(lim2.at[owner], limrecv.at[outer], 4, l_rsem.at[0], inner, owner).start()

    def ring_far(q):
        part_copy(q, "f").wait_recv()
        for way, to in ((0, right), (1, left)):
            y1send[q, way] = pair_sum(q, 0, way)
            remote(y1send.at[q, way], y1recv.at[q, way], 1, y1_rsem.at[q], to).start()

    def ring_near(q):
        part_copy(q, "h").wait_recv()
        for way, to in ((0, right), (1, left)):
            y2send[q, way, 0] = pair_sum(q, 1 + way, 1 - way)
            remote(y2send.at[q, way, 0], y2recv.at[q, way, 0], 2, y2_rsem.at[q], to).start()

    def ring_on(q):
        wait_recv(y1recv.at[q], y1_rsem.at[q])
        for way, to in ((0, right), (1, left)):
            value = enc[q, core, 1 + way, way].astype(F32) + arecv[q, 1 + way, way].astype(F32)
            y2send[q, way, 1] = (value + y1recv[q, way].astype(F32)).astype(BF16)
            remote(y2send.at[q, way, 1], y2recv.at[q, way, 1], 2, y2_rsem.at[q], to).start()

    def run_one(q):
        part_copy(q, "o").wait_recv()
        wait_recv(y2recv.at[q], y2_rsem.at[q])
        for d in (1, 2, 3, 0):
            r = (role + d) % 4
            for half in range(2):
                value = enc[q, core, 3, half, r].astype(F32) + arecv[q, 3, half, r].astype(F32)
                value = value + y2recv[q, half, 1, r].astype(F32) + y2recv[q, 1 - half, 0, r].astype(F32)
                if d:
                    z1send[q, d - 1, half] = value.astype(BF16)
                else:
                    z1own[q, half] = value
            if d:
                remote(z1send.at[q, d - 1], z1recv.at[q, d - 1], 3, z1_rsem.at[q], mates[d - 1]).start()

    def run_two(q):
        wait_recv(z1recv.at[q], z1_rsem.at[q])
        for half in range(2):
            value = z1own[q, half]
            for d in range(3):
                value = value + z1recv[q, d, half].astype(F32)
            for h in range(OWNERS):
                owner = OWNERS * q + h
                fsend[half, owner] = value[h * 16 : (h + 1) * 16].astype(BF16)
                here = jnp.logical_and(owner == outer, half == run)

                @pl.when(jnp.logical_not(here))
                def _():
                    remote(
                        fsend.at[half, owner], frecv.at[8 * run + outer], 5, f_rsem.at[0],
                        inner_of(y, 4 * half + role, core), owner,
                    ).start()

    stages = {part: encode_send(part) for part in parts}
    stages.update(l=limit_send, m=ring_far, k=ring_near, n=ring_on, r=run_one, s=run_two)
    for name, q in ORDER:
        stages[name](q)

    frecv[8 * run + outer] = fsend[run, outer]
    for stage, like in enumerate(
        (arecv, y1send, y2send, z1send, lim2.at[pl.ds(0, 7)], frecv.at[pl.ds(0, 15)])
    ):
        wait_send(like, stage)
    wait_recv(limrecv.at[pl.ds(0, 7)], l_rsem.at[0])
    wait_recv(frecv.at[pl.ds(0, 15)], f_rsem.at[0])
    total = jnp.zeros((16, 128), F32)
    for group in range(8):
        value = frecv[group].astype(F32) + frecv[8 + group].astype(F32)
        total = total + clip(value, limrecv[group].astype(F32))
    high = total.astype(BF16)
    low = (total - high.astype(F32)).astype(BF16)
    signs = table[0:128, 0:128]
    result = jnp.dot(high, signs, preferred_element_type=F32)
    result = result + jnp.dot(low, signs, preferred_element_type=F32)
    out_ref[...] = result * F32(RSQRT)


def shards(grads, first_exponents, second_exponents):
    rows, columns = grads.shape[2], grads.shape[3]
    first = first_exponents.reshape(rows, columns // 128).T
    second = second_exponents.reshape(1, rows)
    operands = (grads.reshape(rows, columns), first, second)
    dma = pltpu.SemaphoreType.DMA
    c, r = CHUNKS, CHUNK_ROWS
    return pl.pallas_call(
        kernel,
        out_shape=jax.ShapeDtypeStruct((16, 128), F32),
        in_specs=[pl.BlockSpec(memory_space=pltpu.HBM)] * 3,
        out_specs=pl.BlockSpec(memory_space=pltpu.VMEM),
        scratch_shapes=[
            pltpu.VMEM((c, 4, r, columns // 4), F32),
            pltpu.VMEM((columns // 128, rows), jnp.int32),
            pltpu.VMEM((1, rows), jnp.int32),
            pltpu.VMEM((256, 256), BF16),
            pltpu.VMEM((128, 128), BF16),
            pltpu.VMEM((8, 16, 128), BF16),
            pltpu.VMEM((c, 2, 4, 2, 4, r, 128), BF16),
            pltpu.VMEM((c, 4, 2, 4, r, 128), BF16),
            pltpu.VMEM((c, 2, 4, r, 128), BF16),
            pltpu.VMEM((c, 2, 4, r, 128), BF16),
            pltpu.VMEM((c, 2, 2, 4, r, 128), BF16),
            pltpu.VMEM((c, 2, 2, 4, r, 128), BF16),
            pltpu.VMEM((c, 3, 2, r, 128), BF16),
            pltpu.VMEM((c, 2, r, 128), F32),
            pltpu.VMEM((c, 3, 2, r, 128), BF16),
            pltpu.VMEM((2, 8, 16, 128), BF16),
            pltpu.VMEM((16, 16, 128), BF16),
            pltpu.VMEM((8, 16, 128), BF16),
            dma((c, 4)),
            dma((2,)),
            dma((6,)),
            dma((c, 4)),
            dma((c,)),
            dma((c,)),
            dma((c,)),
            dma((1,)),
            dma((1,)),
        ],
        compiler_params=pltpu.CompilerParams(
            collective_id=0, has_side_effects=True, vmem_limit_bytes=48 * 1024 * 1024
        ),
        name="reduce_scatter",
    )(*(pltpu.with_memory_space_constraint(x, pltpu.HBM) for x in operands))


def solution(mesh):
    placed = (
        P("inner", "outer", None, None),
        P("inner", "outer", None, None),
        P("outer", None, "inner"),
    )
    return jax.shard_map(
        shards, mesh=mesh, in_specs=placed, out_specs=P("outer", "inner"), check_vma=False
    )
```

```python
import math

import jax
import jax.numpy as jnp
from jax import lax
from jax.experimental import pallas as pl
from jax.experimental.pallas import tpu as pltpu
from jax.sharding import PartitionSpec as P

SATURATION = 448.0
RSQRT = 1.0 / math.sqrt(128.0)
LOGICAL = pl.DeviceIdType.MESH
F32 = jnp.float32
BF16 = jnp.bfloat16
CHUNKS = 4
CHUNK_ROWS = 128 // CHUNKS
OWNERS = CHUNK_ROWS // 16
ORDER = tuple(
    (item[0], int(item[1:]))
    for line in (
        "f0 f1 f2 f3", "h0 h1 m0 m1", "h2 m2 h3 m3", "o0 o1 o2 o3", "l0 n0 k0 n1",
        "k1 n2 k2 n3", "k3 r0 r1 r2", "r3 s0 s1 s2", "s3",
    )
    for item in line.split()
)


def sign_table():
    row = lax.broadcasted_iota(jnp.int32, (256, 256), 0)
    col = lax.broadcasted_iota(jnp.int32, (256, 256), 1)
    shared = row & col & 127
    shared = shared ^ (shared >> 4)
    shared = shared ^ (shared >> 2)
    shared = shared ^ (shared >> 1)
    signs = (1 - 2 * (shared & 1)).astype(F32)
    return jnp.where((row // 128) == (col // 128), signs, 0.0).astype(BF16)


def limits(exponents):
    return jnp.left_shift(1, exponents + 13).astype(F32) * F32(SATURATION / 8192.0)


def clip(value, bound):
    return jnp.minimum(jnp.maximum(value, -bound), bound)


def kernel(
    grads_ref, first_ref, second_ref, out_ref,
    gbuf, first_buf, second_buf, table, lim1, lim2, enc, arecv,
    y1send, y1recv, y2send, y2recv, z1send, z1own, z1recv, fsend, frecv, limrecv,
    load_sem, scale_sem, send_sem, a_rsem, y1_rsem, y2_rsem, z1_rsem, l_rsem, f_rsem,
):
    inner = lax.axis_index("inner")
    outer = lax.axis_index("outer")
    core = inner % 2
    z = (inner // 2) % 8
    y = inner // 16
    run, role = z // 4, z % 4
    y_right, y_left, y_far = (y + 1) % 4, (y + 3) % 4, (y + 2) % 4

    def inner_of(yy, zz, cc):
        return (yy * 8 + zz) * 2 + cc

    sibling = inner_of(y, z, 1 - core)
    right = inner_of(y_right, z, core)
    left = inner_of(y_left, z, core)
    across = inner_of(y, (1 - run) * 4 + role, core)
    mates = [inner_of(y, run * 4 + (role + d) % 4, core) for d in (1, 2, 3)]

    def remote(src, dst, stage, rsem, i, o=None):
        return pltpu.make_async_remote_copy(
            src_ref=src, dst_ref=dst, send_sem=send_sem.at[stage], recv_sem=rsem,
            device_id=(i, outer if o is None else o), device_id_type=LOGICAL,
        )

    def wait_recv(dst, rsem):
        remote(dst, dst, 0, rsem, sibling).wait_recv()

    def wait_send(like, stage):
        remote(like, like, stage, f_rsem.at[0], sibling).wait_send()

    scale_loads = [
        pltpu.make_async_copy(first_ref, first_buf, scale_sem.at[0]),
        pltpu.make_async_copy(second_ref, second_buf, scale_sem.at[1]),
    ]
    places = (y_far, y_right, y_left, y)
    parts = {"f": (0,), "h": (1, 2), "o": (3,)}

    far_z, far_x = 1 - outer // 4, 1 - outer // 2 % 2
    near_z, near_x = outer // 4, outer // 2 % 2
    bands = (2 * far_z + near_x, 2 * far_z + far_x, 2 * near_z + far_x, 2 * near_z + near_x)

    def rows_of(q):
        return pl.ds(pl.multiple_of(bands[q] * CHUNK_ROWS, CHUNK_ROWS), CHUNK_ROWS)

    def load(q, d):
        columns = pl.ds(pl.multiple_of(places[d] * 2048, 2048), 2048)
        return pltpu.make_async_copy(
            grads_ref.at[rows_of(q), columns], gbuf.at[q, d], load_sem.at[q, d]
        )

    def start_loads(part):
        for q in range(CHUNKS):
            for d in parts[part]:
                load(q, d).start()

    for copy in scale_loads:
        copy.start()
    start_loads("f")

    barrier = pltpu.get_barrier_semaphore()
    partners = [sibling, right, left, across] + mates
    for i in partners:
        pl.semaphore_signal(barrier, inc=1, device_id=(i, outer), device_id_type=LOGICAL)
    for d in range(1, 8):
        for i in (inner, across):
            pl.semaphore_signal(
                barrier, inc=1, device_id=(i, (outer + d) % 8), device_id_type=LOGICAL
            )

    start_loads("h")
    start_loads("o")
    table[...] = sign_table()
    for copy in scale_loads:
        copy.wait()
    first = jnp.concatenate(
        [first_buf[pl.ds(pl.multiple_of(place * 16, 16), 16), :] for place in places] * 2, axis=0
    )
    lim1[...] = limits(first).T.astype(BF16)
    second = jnp.broadcast_to(limits(second_buf[...]), (128, 128)).T.astype(BF16)
    for owner in range(8):
        lim2[owner] = second[owner * 16 : (owner + 1) * 16]
    limrecv[outer] = lim2[outer]

    def encode(q, part):
        bounds = lim1[rows_of(q), :]
        pairs = [(d, k) for d in parts[part] for k in range(8)]
        for d in parts[part]:
            load(q, d).wait()
        lhs = jnp.concatenate(
            [gbuf[q, d, :, k * 256 : (k + 1) * 256].astype(BF16) for d, k in pairs], axis=0
        )
        rotated = jnp.dot(lhs, table[...], preferred_element_type=F32) * F32(RSQRT)
        rotated = rotated.astype(BF16)
        for i, (d, k) in enumerate(pairs):
            for c in range(2):
                lane = 16 * d + 2 * k + c
                bound = jnp.broadcast_to(bounds[:, lane : lane + 1], (CHUNK_ROWS, 128))
                value = rotated[i * CHUNK_ROWS : (i + 1) * CHUNK_ROWS, c * 128 : (c + 1) * 128]
                enc[q, c, d, k // 4, k % 4] = clip(value, bound)

    def part_copy(q, part):
        span = pl.ds(parts[part][0], len(parts[part]))
        return remote(
            enc.at[q, 1 - core, span], arecv.at[q, span], 0,
            a_rsem.at[q, parts[part][0]], sibling,
        )

    def encode_send(part):
        def stage(q):
            encode(q, part)
            if part == "f" and q == 0:
                pl.semaphore_wait(barrier, len(partners) + 14)
            part_copy(q, part).start()

        return stage

    def pair_sum(q, d, half):
        return enc[q, core, d, half] + arecv[q, d, half]

    def limit_send(q):
        for d in range(1, 8):
            owner = (outer + d) % 8
            remote(lim2.at[owner], limrecv.at[outer], 4, l_rsem.at[0], inner, owner).start()

    def ring_far(q):
        part_copy(q, "f").wait_recv()
        for way, to in ((0, right), (1, left)):
            y1send[q, way] = pair_sum(q, 0, way)
            remote(y1send.at[q, way], y1recv.at[q, way], 1, y1_rsem.at[q], to).start()

    def ring_near(q):
        for way, to in ((0, right), (1, left)):
            y2send[q, way, 0] = pair_sum(q, 1 + way, 1 - way)
            remote(y2send.at[q, way, 0], y2recv.at[q, way, 0], 2, y2_rsem.at[q], to).start()

    def ring_on(q):
        part_copy(q, "h").wait_recv()
        wait_recv(y1recv.at[q], y1_rsem.at[q])
        for way, to in ((0, right), (1, left)):
            value = enc[q, core, 1 + way, way].astype(F32) + arecv[q, 1 + way, way].astype(F32)
            y2send[q, way, 1] = (value + y1recv[q, way].astype(F32)).astype(BF16)
            remote(y2send.at[q, way, 1], y2recv.at[q, way, 1], 2, y2_rsem.at[q], to).start()

    def run_one(q):
        part_copy(q, "o").wait_recv()
        wait_recv(y2recv.at[q], y2_rsem.at[q])
        for d in (1, 2, 3, 0):
            r = (role + d) % 4
            for half in range(2):
                value = enc[q, core, 3, half, r].astype(F32) + arecv[q, 3, half, r].astype(F32)
                value = value + y2recv[q, half, 1, r].astype(F32) + y2recv[q, 1 - half, 0, r].astype(F32)
                if d:
                    z1send[q, d - 1, half] = value.astype(BF16)
                else:
                    z1own[q, half] = value
            if d:
                remote(z1send.at[q, d - 1], z1recv.at[q, d - 1], 3, z1_rsem.at[q], mates[d - 1]).start()

    def run_two(q):
        wait_recv(z1recv.at[q], z1_rsem.at[q])
        for half in range(2):
            value = z1own[q, half]
            for d in range(3):
                value = value + z1recv[q, d, half].astype(F32)
            for h in range(OWNERS):
                owner = OWNERS * bands[q] + h
                fsend[half, owner] = value[h * 16 : (h + 1) * 16].astype(BF16)
                here = jnp.logical_and(owner == outer, half == run)

                @pl.when(jnp.logical_not(here))
                def _():
                    remote(
                        fsend.at[half, owner], frecv.at[8 * run + outer], 5, f_rsem.at[0],
                        inner_of(y, 4 * half + role, core), owner,
                    ).start()

    stages = {part: encode_send(part) for part in parts}
    stages.update(l=limit_send, m=ring_far, k=ring_near, n=ring_on, r=run_one, s=run_two)
    for name, q in ORDER:
        stages[name](q)

    frecv[8 * run + outer] = fsend[run, outer]
    for stage, like in enumerate(
        (arecv, y1send, y2send, z1send, lim2.at[pl.ds(0, 7)], frecv.at[pl.ds(0, 15)])
    ):
        wait_send(like, stage)
    wait_recv(limrecv.at[pl.ds(0, 7)], l_rsem.at[0])
    wait_recv(frecv.at[pl.ds(0, 15)], f_rsem.at[0])
    total = jnp.zeros((16, 128), F32)
    for group in range(8):
        value = frecv[group].astype(F32) + frecv[8 + group].astype(F32)
        total = total + clip(value, limrecv[group].astype(F32))
    high = total.astype(BF16)
    low = (total - high.astype(F32)).astype(BF16)
    signs = table[0:128, 0:128]
    result = jnp.dot(high, signs, preferred_element_type=F32)
    result = result + jnp.dot(low, signs, preferred_element_type=F32)
    out_ref[...] = result * F32(RSQRT)


def shards(grads, first_exponents, second_exponents):
    rows, columns = grads.shape[2], grads.shape[3]
    first = first_exponents.reshape(rows, columns // 128).T
    second = second_exponents.reshape(1, rows)
    operands = (grads.reshape(rows, columns), first, second)
    dma = pltpu.SemaphoreType.DMA
    c, r = CHUNKS, CHUNK_ROWS
    return pl.pallas_call(
        kernel,
        out_shape=jax.ShapeDtypeStruct((16, 128), F32),
        in_specs=[pl.BlockSpec(memory_space=pltpu.HBM)] * 3,
        out_specs=pl.BlockSpec(memory_space=pltpu.VMEM),
        scratch_shapes=[
            pltpu.VMEM((c, 4, r, columns // 4), F32),
            pltpu.VMEM((columns // 128, rows), jnp.int32),
            pltpu.VMEM((1, rows), jnp.int32),
            pltpu.VMEM((256, 256), BF16),
            pltpu.VMEM((128, 128), BF16),
            pltpu.VMEM((8, 16, 128), BF16),
            pltpu.VMEM((c, 2, 4, 2, 4, r, 128), BF16),
            pltpu.VMEM((c, 4, 2, 4, r, 128), BF16),
            pltpu.VMEM((c, 2, 4, r, 128), BF16),
            pltpu.VMEM((c, 2, 4, r, 128), BF16),
            pltpu.VMEM((c, 2, 2, 4, r, 128), BF16),
            pltpu.VMEM((c, 2, 2, 4, r, 128), BF16),
            pltpu.VMEM((c, 3, 2, r, 128), BF16),
            pltpu.VMEM((c, 2, r, 128), F32),
            pltpu.VMEM((c, 3, 2, r, 128), BF16),
            pltpu.VMEM((2, 8, 16, 128), BF16),
            pltpu.VMEM((16, 16, 128), BF16),
            pltpu.VMEM((8, 16, 128), BF16),
            dma((c, 4)),
            dma((2,)),
            dma((6,)),
            dma((c, 4)),
            dma((c,)),
            dma((c,)),
            dma((c,)),
            dma((1,)),
            dma((1,)),
        ],
        compiler_params=pltpu.CompilerParams(
            collective_id=0, has_side_effects=True, vmem_limit_bytes=48 * 1024 * 1024
        ),
        name="reduce_scatter",
    )(*(pltpu.with_memory_space_constraint(x, pltpu.HBM) for x in operands))


def solution(mesh):
    placed = (
        P("inner", "outer", None, None),
        P("inner", "outer", None, None),
        P("outer", None, "inner"),
    )
    return jax.shard_map(
        shards, mesh=mesh, in_specs=placed, out_specs=P("outer", "inner"), check_vma=False
    )
```

```python
import math

import jax
import jax.numpy as jnp
from jax import lax
from jax.experimental import pallas as pl
from jax.experimental.pallas import tpu as pltpu
from jax.sharding import PartitionSpec as P

SATURATION = 448.0
RSQRT = 1.0 / math.sqrt(128.0)
LOGICAL = pl.DeviceIdType.MESH
F32 = jnp.float32
BF16 = jnp.bfloat16
CHUNKS = 4
CHUNK_ROWS = 64
ORDER = tuple(
    (item[0], int(item[1:]))
    for line in (
        "f0 h0 f1 o0", "f2 h1 m0 m1", "h2 k0 m2 f3", "h3 o1 n0 k1", "n1 m3 o2 o3",
        "k2 n2 k3 r0", "r1 n3 r2 l0", "s0 r3 s1 s2", "s3",
    )
    for item in line.split()
)


def sign_table():
    row = lax.broadcasted_iota(jnp.int32, (256, 256), 0)
    col = lax.broadcasted_iota(jnp.int32, (256, 256), 1)
    shared = row & col & 127
    shared = shared ^ (shared >> 4)
    shared = shared ^ (shared >> 2)
    shared = shared ^ (shared >> 1)
    signs = (1 - 2 * (shared & 1)).astype(F32)
    return jnp.where((row // 128) == (col // 128), signs, 0.0).astype(BF16)


def limits(exponents):
    return jnp.left_shift(1, exponents + 13).astype(F32) * F32(SATURATION / 8192.0)


def clip(value, bound):
    return jnp.minimum(jnp.maximum(value, -bound), bound)


def kernel(
    grads_ref, first_ref, second_ref, out_ref,
    gbuf, first_buf, second_buf, table, lim1, lim2, enc, arecv,
    y1send, y1recv, y2send, y2recv, z1send, z1own, z1recv, fsend, frecv, limrecv,
    load_sem, scale_sem, send_sem, a_rsem, y1_rsem, y2_rsem, z1_rsem, l_rsem, f_rsem,
):
    inner = lax.axis_index("inner")
    outer = lax.axis_index("outer")
    core = inner % 2
    z = (inner // 2) % 8
    y = inner // 16
    run, role = z // 4, z % 4
    y_right, y_left, y_far = (y + 1) % 4, (y + 3) % 4, (y + 2) % 4

    def inner_of(yy, zz, cc):
        return (yy * 8 + zz) * 2 + cc

    sibling = inner_of(y, z, 1 - core)
    right = inner_of(y_right, z, core)
    left = inner_of(y_left, z, core)
    across = inner_of(y, (1 - run) * 4 + role, core)
    mates = [inner_of(y, run * 4 + (role + d) % 4, core) for d in (1, 2, 3)]

    def remote(src, dst, stage, rsem, i, o=None):
        return pltpu.make_async_remote_copy(
            src_ref=src, dst_ref=dst, send_sem=send_sem.at[stage], recv_sem=rsem,
            device_id=(i, outer if o is None else o), device_id_type=LOGICAL,
        )

    def wait_recv(dst, rsem):
        remote(dst, dst, 0, rsem, sibling).wait_recv()

    def wait_send(like, stage):
        remote(like, like, stage, f_rsem.at[0], sibling).wait_send()

    scale_loads = [
        pltpu.make_async_copy(first_ref, first_buf, scale_sem.at[0]),
        pltpu.make_async_copy(second_ref, second_buf, scale_sem.at[1]),
    ]
    places = (y_far, y_right, y_left, y)
    parts = {"f": (0,), "h": (1, 2), "o": (3,)}

    def rows_of(q):
        return pl.ds(q // 2 * CHUNK_ROWS, CHUNK_ROWS)

    def load(q, d):
        columns = pl.ds(pl.multiple_of(places[d] * 2048 + q % 2 * 1024, 1024), 1024)
        return pltpu.make_async_copy(
            grads_ref.at[rows_of(q), columns], gbuf.at[q, d], load_sem.at[q, d]
        )

    def start_loads(q):
        for d in range(4):
            load(q, d).start()

    for copy in scale_loads:
        copy.start()
    start_loads(0)

    lower, first_run = 1 - outer // 4, 1 - run
    klass = lower * first_run
    barrier = pltpu.get_barrier_semaphore()

    def hello(i, o):
        pl.semaphore_signal(barrier, inc=1, device_id=(i, o), device_id_type=LOGICAL)

    def hello_outer(same):
        for d in range(1, 8):
            owner = (outer + d) % 8
            other_lower = 1 - owner // 4
            for i, other in ((inner, other_lower * first_run), (across, other_lower * run)):

                @pl.when((other == klass) if same else (other != klass))
                def _():
                    hello(i, owner)

        @pl.when((lower * run == klass) if same else (lower * run != klass))
        def _():
            hello(across, outer)

    def enter():
        pl.semaphore_wait(barrier, 21 - 12 * klass)
        hello_outer(False)

    def enter_outer():
        @pl.when(klass == 1)
        def _():
            pl.semaphore_wait(barrier, 12)

    for i in [sibling, right, left] + mates:
        hello(i, outer)
    hello_outer(True)

    for q in range(1, CHUNKS):
        start_loads(q)
    table[...] = sign_table()
    for copy in scale_loads:
        copy.wait()
    first = jnp.concatenate(
        [first_buf[pl.ds(pl.multiple_of(place * 16, 16), 16), :] for place in places] * 2, axis=0
    )
    lim1[...] = limits(first).T.astype(BF16)
    second = jnp.broadcast_to(limits(second_buf[...]), (128, 128)).T.astype(BF16)
    for owner in range(8):
        lim2[owner] = second[owner * 16 : (owner + 1) * 16]
    limrecv[outer] = lim2[outer]

    def encode(q, part):
        bounds = lim1[rows_of(q), :]
        pairs = [(d, k) for d in parts[part] for k in range(4)]
        for d in parts[part]:
            load(q, d).wait()
        lhs = jnp.concatenate(
            [gbuf[q, d, :, k * 256 : (k + 1) * 256].astype(BF16) for d, k in pairs], axis=0
        )
        rotated = jnp.dot(lhs, table[...], preferred_element_type=F32) * F32(RSQRT)
        rotated = rotated.astype(BF16)
        for i, (d, k) in enumerate(pairs):
            for c in range(2):
                lane = 16 * d + 8 * (q % 2) + 2 * k + c
                bound = jnp.broadcast_to(bounds[:, lane : lane + 1], (CHUNK_ROWS, 128))
                value = rotated[i * CHUNK_ROWS : (i + 1) * CHUNK_ROWS, c * 128 : (c + 1) * 128]
                enc[q, c, d, k] = clip(value, bound)

    def part_copy(q, part):
        span = pl.ds(parts[part][0], len(parts[part]))
        return remote(
            enc.at[q, 1 - core, span], arecv.at[q, span], 0,
            a_rsem.at[q, parts[part][0]], sibling,
        )

    def encode_send(part):
        def stage(q):
            encode(q, part)
            if part == "f" and q == 0:
                enter()
            part_copy(q, part).start()

        return stage

    def pair_sum(q, d, way):
        two = pl.ds(2 * way, 2)
        return enc[q, core, d, two] + arecv[q, d, two]

    def limit_send(q):
        enter_outer()
        for d in range(1, 8):
            owner = (outer + d) % 8
            remote(lim2.at[owner], limrecv.at[outer], 4, l_rsem.at[0], inner, owner).start()

    def ring_far(q):
        part_copy(q, "f").wait_recv()
        for way, to in ((0, right), (1, left)):
            y1send[q, way] = pair_sum(q, 0, way)
            remote(y1send.at[q, way], y1recv.at[q, way], 1, y1_rsem.at[q], to).start()

    def ring_near(q):
        part_copy(q, "h").wait_recv()
        for way, to in ((0, right), (1, left)):
            y2send[q, way, 0] = pair_sum(q, 1 + way, 1 - way)
            remote(y2send.at[q, way, 0], y2recv.at[q, way, 0], 2, y2_rsem.at[q], to).start()

    def ring_on(q):
        wait_recv(y1recv.at[q], y1_rsem.at[q])
        for way, to in ((0, right), (1, left)):
            two = pl.ds(2 * way, 2)
            value = enc[q, core, 1 + way, two].astype(F32) + arecv[q, 1 + way, two].astype(F32)
            y2send[q, way, 1] = (value + y1recv[q, way].astype(F32)).astype(BF16)
            remote(y2send.at[q, way, 1], y2recv.at[q, way, 1], 2, y2_rsem.at[q], to).start()

    def run_one(q):
        part_copy(q, "o").wait_recv()
        wait_recv(y2recv.at[q], y2_rsem.at[q])
        for d in (1, 2, 3, 0):
            r = (role + d) % 4
            way, place = r // 2, r % 2
            value = enc[q, core, 3, r].astype(F32) + arecv[q, 3, r].astype(F32)
            value = value + y2recv[q, way, 1, place].astype(F32)
            value = value + y2recv[q, 1 - way, 0, place].astype(F32)
            if d:
                z1send[q, d - 1] = value.astype(BF16)
                remote(z1send.at[q, d - 1], z1recv.at[q, d - 1], 3, z1_rsem.at[q], mates[d - 1]).start()
            else:
                z1own[q] = value

    def run_two(q):
        wait_recv(z1recv.at[q], z1_rsem.at[q])
        value = z1own[q]
        for d in range(3):
            value = value + z1recv[q, d].astype(F32)
        value = value.astype(BF16)
        half = q % 2
        for h in range(4):
            owner = q // 2 * 4 + h
            fsend[half, owner] = value[h * 16 : (h + 1) * 16]
            here = jnp.logical_and(owner == outer, half == run)

            @pl.when(jnp.logical_not(here))
            def _():
                remote(
                    fsend.at[half, owner], frecv.at[8 * run + outer], 5, f_rsem.at[0],
                    inner_of(y, 4 * half + role, core), owner,
                ).start()

    stages = {part: encode_send(part) for part in parts}
    stages.update(l=limit_send, m=ring_far, k=ring_near, n=ring_on, r=run_one, s=run_two)
    for name, q in ORDER:
        stages[name](q)

    frecv[8 * run + outer] = fsend[run, outer]
    for stage, like in enumerate(
        (arecv, y1send, y2send, z1send, lim2.at[pl.ds(0, 7)], frecv.at[pl.ds(0, 15)])
    ):
        wait_send(like, stage)
    wait_recv(limrecv.at[pl.ds(0, 7)], l_rsem.at[0])
    wait_recv(frecv.at[pl.ds(0, 15)], f_rsem.at[0])
    total = jnp.zeros((16, 128), F32)
    for group in range(8):
        value = frecv[group].astype(F32) + frecv[8 + group].astype(F32)
        total = total + clip(value, limrecv[group].astype(F32))
    high = total.astype(BF16)
    low = (total - high.astype(F32)).astype(BF16)
    signs = table[0:128, 0:128]
    result = jnp.dot(high, signs, preferred_element_type=F32)
    result = result + jnp.dot(low, signs, preferred_element_type=F32)
    out_ref[...] = result * F32(RSQRT)


def shards(grads, first_exponents, second_exponents):
    rows, columns = grads.shape[2], grads.shape[3]
    first = first_exponents.reshape(rows, columns // 128).T
    second = second_exponents.reshape(1, rows)
    operands = (grads.reshape(rows, columns), first, second)
    dma = pltpu.SemaphoreType.DMA
    c, r = CHUNKS, CHUNK_ROWS
    return pl.pallas_call(
        kernel,
        out_shape=jax.ShapeDtypeStruct((16, 128), F32),
        in_specs=[pl.BlockSpec(memory_space=pltpu.HBM)] * 3,
        out_specs=pl.BlockSpec(memory_space=pltpu.VMEM),
        scratch_shapes=[
            pltpu.VMEM((c, 4, r, 1024), F32),
            pltpu.VMEM((columns // 128, rows), jnp.int32),
            pltpu.VMEM((1, rows), jnp.int32),
            pltpu.VMEM((256, 256), BF16),
            pltpu.VMEM((128, 128), BF16),
            pltpu.VMEM((8, 16, 128), BF16),
            pltpu.VMEM((c, 2, 4, 4, r, 128), BF16),
            pltpu.VMEM((c, 4, 4, r, 128), BF16),
            pltpu.VMEM((c, 2, 2, r, 128), BF16),
            pltpu.VMEM((c, 2, 2, r, 128), BF16),
            pltpu.VMEM((c, 2, 2, 2, r, 128), BF16),
            pltpu.VMEM((c, 2, 2, 2, r, 128), BF16),
            pltpu.VMEM((c, 3, r, 128), BF16),
            pltpu.VMEM((c, r, 128), F32),
            pltpu.VMEM((c, 3, r, 128), BF16),
            pltpu.VMEM((2, 8, 16, 128), BF16),
            pltpu.VMEM((16, 16, 128), BF16),
            pltpu.VMEM((8, 16, 128), BF16),
            dma((c, 4)),
            dma((2,)),
            dma((6,)),
            dma((c, 4)),
            dma((c,)),
            dma((c,)),
            dma((c,)),
            dma((1,)),
            dma((1,)),
        ],
        compiler_params=pltpu.CompilerParams(
            collective_id=0, has_side_effects=True, vmem_limit_bytes=48 * 1024 * 1024
        ),
        name="reduce_scatter",
    )(*(pltpu.with_memory_space_constraint(x, pltpu.HBM) for x in operands))


def solution(mesh):
    placed = (
        P("inner", "outer", None, None),
        P("inner", "outer", None, None),
        P("outer", None, "inner"),
    )
    return jax.shard_map(
        shards, mesh=mesh, in_specs=placed, out_specs=P("outer", "inner"), check_vma=False
    )
```

```python
import math

import jax
import jax.numpy as jnp
from jax import lax
from jax.experimental import pallas as pl
from jax.experimental.pallas import tpu as pltpu
from jax.sharding import PartitionSpec as P

SATURATION = 448.0
RSQRT = 1.0 / math.sqrt(128.0)
LOGICAL = pl.DeviceIdType.MESH
F32 = jnp.float32
BF16 = jnp.bfloat16
CHUNKS = 4
CHUNK_ROWS = 64
ORDER = tuple(
    (item[0], int(item[1:]))
    for line in (
        "f0 h0 f1 o0", "f2 m0 h1 f3", "m1 k0 o1 h2", "n0 h3 m2 k1", "r0 o2 n1 m3",
        "o3 k2 r1 n2", "k3 l0 s0 n3", "r2 s1 r3 s2", "s3",
    )
    for item in line.split()
)


def sign_table():
    row = lax.broadcasted_iota(jnp.int32, (256, 256), 0)
    col = lax.broadcasted_iota(jnp.int32, (256, 256), 1)
    shared = row & col & 127
    shared = shared ^ (shared >> 4)
    shared = shared ^ (shared >> 2)
    shared = shared ^ (shared >> 1)
    signs = (1 - 2 * (shared & 1)).astype(F32)
    return jnp.where((row // 128) == (col // 128), signs, 0.0).astype(BF16)


def spread_table():
    row = lax.broadcasted_iota(jnp.int32, (128, 256), 0)
    col = lax.broadcasted_iota(jnp.int32, (128, 256), 1)
    return jnp.where(row == col // 128, 1.0, 0.0).astype(BF16)


def limits(exponents):
    return jnp.left_shift(1, exponents + 13).astype(F32) * F32(SATURATION / 8192.0)


def clip(value, bound):
    return jnp.minimum(jnp.maximum(value, -bound), bound)


def kernel(
    grads_ref, first_ref, second_ref, out_ref,
    gbuf, first_buf, second_buf, table, spread, lim1, lim2, enc, arecv,
    y1send, y1recv, y2send, y2recv, z1send, z1own, z1recv, fsend, frecv, limrecv,
    load_sem, scale_sem, send_sem, a_rsem, y1_rsem, y2_rsem, z1_rsem, l_rsem, f_rsem,
):
    inner = lax.axis_index("inner")
    outer = lax.axis_index("outer")
    core = inner % 2
    z = (inner // 2) % 8
    y = inner // 16
    run, role = z // 4, z % 4
    y_right, y_left, y_far = (y + 1) % 4, (y + 3) % 4, (y + 2) % 4

    def inner_of(yy, zz, cc):
        return (yy * 8 + zz) * 2 + cc

    sibling = inner_of(y, z, 1 - core)
    right = inner_of(y_right, z, core)
    left = inner_of(y_left, z, core)
    across = inner_of(y, (1 - run) * 4 + role, core)
    mates = [inner_of(y, run * 4 + (role + d) % 4, core) for d in (1, 2, 3)]

    def remote(src, dst, stage, rsem, i, o=None):
        return pltpu.make_async_remote_copy(
            src_ref=src, dst_ref=dst, send_sem=send_sem.at[stage], recv_sem=rsem,
            device_id=(i, outer if o is None else o), device_id_type=LOGICAL,
        )

    def wait_recv(dst, rsem):
        remote(dst, dst, 0, rsem, sibling).wait_recv()

    def wait_send(like, stage):
        remote(like, like, stage, f_rsem.at[0], sibling).wait_send()

    scale_loads = [
        pltpu.make_async_copy(first_ref, first_buf, scale_sem.at[0]),
        pltpu.make_async_copy(second_ref, second_buf, scale_sem.at[1]),
    ]
    places = (y_far, y_right, y_left, y)
    parts = {"f": (0,), "h": (1, 2), "o": (3,)}

    def rows_of(q):
        return pl.ds(q // 2 * CHUNK_ROWS, CHUNK_ROWS)

    def load(q, d):
        columns = pl.ds(pl.multiple_of(places[d] * 2048 + q % 2 * 1024, 1024), 1024)
        return pltpu.make_async_copy(
            grads_ref.at[rows_of(q), columns], gbuf.at[q, d], load_sem.at[q, d]
        )

    def start_loads(q):
        for d in range(4):
            load(q, d).start()

    for copy in scale_loads:
        copy.start()
    start_loads(0)

    lower, first_run = 1 - outer // 4, 1 - run
    klass = lower * first_run
    barrier = pltpu.get_barrier_semaphore()

    def hello(i, o):
        pl.semaphore_signal(barrier, inc=1, device_id=(i, o), device_id_type=LOGICAL)

    def hello_outer(same):
        for d in range(1, 8):
            owner = (outer + d) % 8
            other_lower = 1 - owner // 4
            for i, other in ((inner, other_lower * first_run), (across, other_lower * run)):

                @pl.when((other == klass) if same else (other != klass))
                def _():
                    hello(i, owner)

        @pl.when((lower * run == klass) if same else (lower * run != klass))
        def _():
            hello(across, outer)

    def enter():
        pl.semaphore_wait(barrier, 21 - 12 * klass)
        hello_outer(False)

    def enter_outer():
        @pl.when(klass == 1)
        def _():
            pl.semaphore_wait(barrier, 12)

    for i in [sibling, right, left] + mates:
        hello(i, outer)
    hello_outer(True)

    for q in range(1, CHUNKS):
        start_loads(q)
    table[...] = sign_table()
    spread[...] = spread_table()
    for copy in scale_loads:
        copy.wait()
    first = jnp.concatenate(
        [first_buf[pl.ds(pl.multiple_of(place * 16, 16), 16), :] for place in places] * 2, axis=0
    )
    lim1[...] = limits(first).T
    second = jnp.broadcast_to(limits(second_buf[...]), (128, 128)).T.astype(BF16)
    for owner in range(8):
        lim2[owner] = second[owner * 16 : (owner + 1) * 16]
    limrecv[outer] = lim2[outer]

    def encode(q, part):
        bounds = lim1[rows_of(q), :]
        pairs = [(d, k) for d in parts[part] for k in range(4)]
        for d in parts[part]:
            load(q, d).wait()
        lhs = jnp.concatenate(
            [gbuf[q, d, :, k * 256 : (k + 1) * 256].astype(BF16) for d, k in pairs], axis=0
        )
        lanes = [16 * d + 8 * (q % 2) + 2 * k for d, k in pairs]
        turned = jnp.concatenate(
            [pltpu.roll(bounds, 128 - lane, 1) if lane else bounds for lane in lanes], axis=0
        )
        bound = jnp.dot(turned.astype(BF16), spread[...], preferred_element_type=F32)
        rotated = jnp.dot(lhs, table[...], preferred_element_type=F32) * F32(RSQRT)
        value = clip(rotated, bound).astype(BF16)
        for i, (d, k) in enumerate(pairs):
            for c in range(2):
                enc[q, c, d, k] = value[i * CHUNK_ROWS : (i + 1) * CHUNK_ROWS, c * 128 : (c + 1) * 128]

    def part_copy(q, part):
        span = pl.ds(parts[part][0], len(parts[part]))
        return remote(
            enc.at[q, 1 - core, span], arecv.at[q, span], 0,
            a_rsem.at[q, parts[part][0]], sibling,
        )

    def encode_send(part):
        def stage(q):
            encode(q, part)
            if part == "f" and q == 0:
                enter()
            part_copy(q, part).start()

        return stage

    def pair_sum(q, d, way):
        two = pl.ds(2 * way, 2)
        return enc[q, core, d, two] + arecv[q, d, two]

    def limit_send(q):
        enter_outer()
        for d in range(1, 8):
            owner = (outer + d) % 8
            remote(lim2.at[owner], limrecv.at[outer], 4, l_rsem.at[0], inner, owner).start()

    def ring_far(q):
        part_copy(q, "f").wait_recv()
        for way, to in ((0, right), (1, left)):
            y1send[q, way] = pair_sum(q, 0, way)
            remote(y1send.at[q, way], y1recv.at[q, way], 1, y1_rsem.at[q], to).start()

    def ring_near(q):
        part_copy(q, "h").wait_recv()
        for way, to in ((0, right), (1, left)):
            y2send[q, way, 0] = pair_sum(q, 1 + way, 1 - way)
            remote(y2send.at[q, way, 0], y2recv.at[q, way, 0], 2, y2_rsem.at[q], to).start()

    def ring_on(q):
        wait_recv(y1recv.at[q], y1_rsem.at[q])
        for way, to in ((0, right), (1, left)):
            two = pl.ds(2 * way, 2)
            value = enc[q, core, 1 + way, two].astype(F32) + arecv[q, 1 + way, two].astype(F32)
            y2send[q, way, 1] = (value + y1recv[q, way].astype(F32)).astype(BF16)
            remote(y2send.at[q, way, 1], y2recv.at[q, way, 1], 2, y2_rsem.at[q], to).start()

    def run_one(q):
        part_copy(q, "o").wait_recv()
        wait_recv(y2recv.at[q], y2_rsem.at[q])
        for d in (1, 2, 3, 0):
            r = (role + d) % 4
            way, place = r // 2, r % 2
            value = enc[q, core, 3, r].astype(F32) + arecv[q, 3, r].astype(F32)
            value = value + y2recv[q, way, 1, place].astype(F32)
            value = value + y2recv[q, 1 - way, 0, place].astype(F32)
            if d:
                z1send[q, d - 1] = value.astype(BF16)
                remote(z1send.at[q, d - 1], z1recv.at[q, d - 1], 3, z1_rsem.at[q], mates[d - 1]).start()
            else:
                z1own[q] = value

    def run_two(q):
        wait_recv(z1recv.at[q], z1_rsem.at[q])
        value = z1own[q]
        for d in range(3):
            value = value + z1recv[q, d].astype(F32)
        value = value.astype(BF16)
        half = q % 2
        for h in range(4):
            owner = q // 2 * 4 + h
            fsend[half, owner] = value[h * 16 : (h + 1) * 16]
            here = jnp.logical_and(owner == outer, half == run)

            @pl.when(jnp.logical_not(here))
            def _():
                remote(
                    fsend.at[half, owner], frecv.at[8 * run + outer], 5, f_rsem.at[0],
                    inner_of(y, 4 * half + role, core), owner,
                ).start()

    stages = {part: encode_send(part) for part in parts}
    stages.update(l=limit_send, m=ring_far, k=ring_near, n=ring_on, r=run_one, s=run_two)
    for name, q in ORDER:
        stages[name](q)

    frecv[8 * run + outer] = fsend[run, outer]
    for stage, like in enumerate(
        (arecv, y1send, y2send, z1send, lim2.at[pl.ds(0, 7)], frecv.at[pl.ds(0, 15)])
    ):
        wait_send(like, stage)
    wait_recv(limrecv.at[pl.ds(0, 7)], l_rsem.at[0])
    wait_recv(frecv.at[pl.ds(0, 15)], f_rsem.at[0])
    total = jnp.zeros((16, 128), F32)
    for group in range(8):
        value = frecv[group].astype(F32) + frecv[8 + group].astype(F32)
        total = total + clip(value, limrecv[group].astype(F32))
    high = total.astype(BF16)
    low = (total - high.astype(F32)).astype(BF16)
    signs = table[0:128, 0:128]
    result = jnp.dot(high, signs, preferred_element_type=F32)
    result = result + jnp.dot(low, signs, preferred_element_type=F32)
    out_ref[...] = result * F32(RSQRT)


def shards(grads, first_exponents, second_exponents):
    rows, columns = grads.shape[2], grads.shape[3]
    first = first_exponents.reshape(rows, columns // 128).T
    second = second_exponents.reshape(1, rows)
    operands = (grads.reshape(rows, columns), first, second)
    dma = pltpu.SemaphoreType.DMA
    c, r = CHUNKS, CHUNK_ROWS
    return pl.pallas_call(
        kernel,
        out_shape=jax.ShapeDtypeStruct((16, 128), F32),
        in_specs=[pl.BlockSpec(memory_space=pltpu.HBM)] * 3,
        out_specs=pl.BlockSpec(memory_space=pltpu.VMEM),
        scratch_shapes=[
            pltpu.VMEM((c, 4, r, 1024), F32),
            pltpu.VMEM((columns // 128, rows), jnp.int32),
            pltpu.VMEM((1, rows), jnp.int32),
            pltpu.VMEM((256, 256), BF16),
            pltpu.VMEM((128, 256), BF16),
            pltpu.VMEM((128, 128), F32),
            pltpu.VMEM((8, 16, 128), BF16),
            pltpu.VMEM((c, 2, 4, 4, r, 128), BF16),
            pltpu.VMEM((c, 4, 4, r, 128), BF16),
            pltpu.VMEM((c, 2, 2, r, 128), BF16),
            pltpu.VMEM((c, 2, 2, r, 128), BF16),
            pltpu.VMEM((c, 2, 2, 2, r, 128), BF16),
            pltpu.VMEM((c, 2, 2, 2, r, 128), BF16),
            pltpu.VMEM((c, 3, r, 128), BF16),
            pltpu.VMEM((c, r, 128), F32),
            pltpu.VMEM((c, 3, r, 128), BF16),
            pltpu.VMEM((2, 8, 16, 128), BF16),
            pltpu.VMEM((16, 16, 128), BF16),
            pltpu.VMEM((8, 16, 128), BF16),
            dma((c, 4)),
            dma((2,)),
            dma((6,)),
            dma((c, 4)),
            dma((c,)),
            dma((c,)),
            dma((c,)),
            dma((1,)),
            dma((1,)),
        ],
        compiler_params=pltpu.CompilerParams(
            collective_id=0, has_side_effects=True, vmem_limit_bytes=48 * 1024 * 1024
        ),
        name="reduce_scatter",
    )(*(pltpu.with_memory_space_constraint(x, pltpu.HBM) for x in operands))


def solution(mesh):
    placed = (
        P("inner", "outer", None, None),
        P("inner", "outer", None, None),
        P("outer", None, "inner"),
    )
    return jax.shard_map(
        shards, mesh=mesh, in_specs=placed, out_specs=P("outer", "inner"), check_vma=False
    )
```

```python
import math

import jax
import jax.numpy as jnp
from jax import lax
from jax.experimental import pallas as pl
from jax.experimental.pallas import tpu as pltpu
from jax.sharding import PartitionSpec as P

SATURATION = 448.0
RSQRT = 1.0 / math.sqrt(128.0)
LOGICAL = pl.DeviceIdType.MESH
F32 = jnp.float32
BF16 = jnp.bfloat16
CHUNKS = 4
CHUNK_ROWS = 64
DIRECT = (0, 1)
ORDER = tuple(
    (item[0], int(item[1:]))
    for line in (
        "f0 h0 h1 o0", "f1 h2 f2 f3", "k0 h3 n0 k1", "m2 o1 n1 m3", "r0 o2 k2 o3",
        "n2 k3 r1 n3", "l0 s0 r2 r3", "s1 s2 s3",
    )
    for item in line.split()
)


def sign_table():
    row = lax.broadcasted_iota(jnp.int32, (256, 256), 0)
    col = lax.broadcasted_iota(jnp.int32, (256, 256), 1)
    shared = row & col & 127
    shared = shared ^ (shared >> 4)
    shared = shared ^ (shared >> 2)
    shared = shared ^ (shared >> 1)
    signs = (1 - 2 * (shared & 1)).astype(F32)
    return jnp.where((row // 128) == (col // 128), signs, 0.0).astype(BF16)


def limits(exponents):
    return jnp.left_shift(1, exponents + 13).astype(F32) * F32(SATURATION / 8192.0)


def clip(value, bound):
    return jnp.minimum(jnp.maximum(value, -bound), bound)


def kernel(
    grads_ref, first_ref, second_ref, out_ref,
    gbuf, first_buf, second_buf, table, lim1, lim2, enc, arecv,
    y1send, y1recv, y2send, y2recv, z1send, z1own, z1recv, xrecv, fsend, frecv, limrecv,
    load_sem, scale_sem, send_sem, a_rsem, y1_rsem, y2_rsem, z1_rsem, l_rsem, f_rsem,
):
    inner = lax.axis_index("inner")
    outer = lax.axis_index("outer")
    core = inner % 2
    z = (inner // 2) % 8
    y = inner // 16
    run, role = z // 4, z % 4
    y_right, y_left, y_far = (y + 1) % 4, (y + 3) % 4, (y + 2) % 4

    def inner_of(yy, zz, cc):
        return (yy * 8 + zz) * 2 + cc

    sibling = inner_of(y, z, 1 - core)
    right = inner_of(y_right, z, core)
    left = inner_of(y_left, z, core)
    beside = [inner_of(y_right, z, 1 - core), inner_of(y_left, z, 1 - core)]
    across = inner_of(y, (1 - run) * 4 + role, core)
    mates = [inner_of(y, run * 4 + (role + d) % 4, core) for d in (1, 2, 3)]

    def remote(src, dst, stage, rsem, i, o=None):
        return pltpu.make_async_remote_copy(
            src_ref=src, dst_ref=dst, send_sem=send_sem.at[stage], recv_sem=rsem,
            device_id=(i, outer if o is None else o), device_id_type=LOGICAL,
        )

    def wait_recv(dst, rsem):
        remote(dst, dst, 0, rsem, sibling).wait_recv()

    def wait_send(like, stage):
        remote(like, like, stage, f_rsem.at[0], sibling).wait_send()

    scale_loads = [
        pltpu.make_async_copy(first_ref, first_buf, scale_sem.at[0]),
        pltpu.make_async_copy(second_ref, second_buf, scale_sem.at[1]),
    ]
    places = (y_far, y_right, y_left, y)
    parts = {"f": (0,), "h": (1, 2), "o": (3,)}

    def rows_of(q):
        return pl.ds(q // 2 * CHUNK_ROWS, CHUNK_ROWS)

    def load(q, d):
        columns = pl.ds(pl.multiple_of(places[d] * 2048 + q % 2 * 1024, 1024), 1024)
        return pltpu.make_async_copy(
            grads_ref.at[rows_of(q), columns], gbuf.at[q, d], load_sem.at[q, d]
        )

    def start_loads(q):
        for d in range(4):
            load(q, d).start()

    for copy in scale_loads:
        copy.start()
    start_loads(0)

    lower, first_run = 1 - outer // 4, 1 - run
    klass = lower * first_run
    barrier = pltpu.get_barrier_semaphore()

    def hello(i, o):
        pl.semaphore_signal(barrier, inc=1, device_id=(i, o), device_id_type=LOGICAL)

    def hello_outer(same):
        for d in range(1, 8):
            owner = (outer + d) % 8
            other_lower = 1 - owner // 4
            for i, other in ((inner, other_lower * first_run), (across, other_lower * run)):

                @pl.when((other == klass) if same else (other != klass))
                def _():
                    hello(i, owner)

        @pl.when((lower * run == klass) if same else (lower * run != klass))
        def _():
            hello(across, outer)

    def enter():
        pl.semaphore_wait(barrier, 23 - 12 * klass)
        hello_outer(False)

    def enter_outer():
        @pl.when(klass == 1)
        def _():
            pl.semaphore_wait(barrier, 12)

    for i in [sibling, right, left] + beside + mates:
        hello(i, outer)
    hello_outer(True)

    start_loads(1)
    table[...] = sign_table()
    for copy in scale_loads:
        copy.wait()
    first = jnp.concatenate(
        [first_buf[pl.ds(pl.multiple_of(place * 16, 16), 16), :] for place in places] * 2, axis=0
    )
    lim1[...] = limits(first).T.astype(BF16)
    second = jnp.broadcast_to(limits(second_buf[...]), (128, 128)).T.astype(BF16)
    for owner in range(8):
        lim2[owner] = second[owner * 16 : (owner + 1) * 16]
    limrecv[outer] = lim2[outer]

    def encode(q, part):
        bounds = lim1[rows_of(q), :]
        pairs = [(d, k) for d in parts[part] for k in range(4)]
        for d in parts[part]:
            load(q, d).wait()
        if part == "h" and q + 2 < CHUNKS:
            start_loads(q + 2)
        lhs = jnp.concatenate(
            [gbuf[q, d, :, k * 256 : (k + 1) * 256].astype(BF16) for d, k in pairs], axis=0
        )
        rotated = jnp.dot(lhs, table[...], preferred_element_type=F32) * F32(RSQRT)
        rotated = rotated.astype(BF16)
        for i, (d, k) in enumerate(pairs):
            for c in range(2):
                lane = 16 * d + 8 * (q % 2) + 2 * k + c
                bound = jnp.broadcast_to(bounds[:, lane : lane + 1], (CHUNK_ROWS, 128))
                value = rotated[i * CHUNK_ROWS : (i + 1) * CHUNK_ROWS, c * 128 : (c + 1) * 128]
                enc[q, c, d, k] = clip(value, bound)

    def part_copy(q, part):
        span = pl.ds(parts[part][0], len(parts[part]))
        return remote(
            enc.at[q, 1 - core, span], arecv.at[q, span], 7 if q in DIRECT else 0,
            a_rsem.at[q, parts[part][0]], sibling,
        )

    def direct_copy(q, way, c):
        two = pl.ds(2 * way, 2)
        target = inner_of((y_right, y_left)[way], z, c)
        return remote(enc.at[q, c, 0, two], xrecv.at[q, core, way], 6, y1_rsem.at[q], target)

    def encode_send(part):
        def stage(q):
            encode(q, part)
            if part == "f" and q == 0:
                enter()
            if part == "f" and q in DIRECT:
                for way in range(2):
                    for c in range(2):
                        direct_copy(q, way, c).start()
            else:
                part_copy(q, part).start()

        return stage

    def pair_sum(q, d, way):
        two = pl.ds(2 * way, 2)
        return enc[q, core, d, two] + arecv[q, d, two]

    def limit_send(q):
        enter_outer()
        for d in range(1, 8):
            owner = (outer + d) % 8
            remote(lim2.at[owner], limrecv.at[outer], 4, l_rsem.at[0], inner, owner).start()

    def ring_far(q):
        if q in DIRECT:
            return
        part_copy(q, "f").wait_recv()
        for way, to in ((0, right), (1, left)):
            y1send[q, way] = pair_sum(q, 0, way)
            remote(y1send.at[q, way], y1recv.at[q, way], 1, y1_rsem.at[q], to).start()

    def ring_near(q):
        part_copy(q, "h").wait_recv()
        for way, to in ((0, right), (1, left)):
            y2send[q, way, 0] = pair_sum(q, 1 + way, 1 - way)
            remote(y2send.at[q, way, 0], y2recv.at[q, way, 0], 2, y2_rsem.at[q], to).start()

    def ring_on(q):
        wait_recv(xrecv.at[q] if q in DIRECT else y1recv.at[q], y1_rsem.at[q])
        for way, to in ((0, right), (1, left)):
            two = pl.ds(2 * way, 2)
            value = enc[q, core, 1 + way, two].astype(F32) + arecv[q, 1 + way, two].astype(F32)
            if q in DIRECT:
                value = value + xrecv[q, 0, way].astype(F32) + xrecv[q, 1, way].astype(F32)
            else:
                value = value + y1recv[q, way].astype(F32)
            y2send[q, way, 1] = value.astype(BF16)
            remote(y2send.at[q, way, 1], y2recv.at[q, way, 1], 2, y2_rsem.at[q], to).start()

    def run_one(q):
        part_copy(q, "o").wait_recv()
        wait_recv(y2recv.at[q], y2_rsem.at[q])
        for d in (1, 2, 3, 0):
            r = (role + d) % 4
            way, place = r // 2, r % 2
            value = enc[q, core, 3, r].astype(F32) + arecv[q, 3, r].astype(F32)
            value = value + y2recv[q, way, 1, place].astype(F32)
            value = value + y2recv[q, 1 - way, 0, place].astype(F32)
            if d:
                z1send[q, d - 1] = value.astype(BF16)
                remote(z1send.at[q, d - 1], z1recv.at[q, d - 1], 3, z1_rsem.at[q], mates[d - 1]).start()
            else:
                z1own[q] = value

    def run_two(q):
        wait_recv(z1recv.at[q], z1_rsem.at[q])
        value = z1own[q]
        for d in range(3):
            value = value + z1recv[q, d].astype(F32)
        value = value.astype(BF16)
        half = q % 2
        for h in range(4):
            owner = q // 2 * 4 + h
            fsend[half, owner] = value[h * 16 : (h + 1) * 16]
            here = jnp.logical_and(owner == outer, half == run)

            @pl.when(jnp.logical_not(here))
            def _():
                remote(
                    fsend.at[half, owner], frecv.at[8 * run + outer], 5, f_rsem.at[0],
                    inner_of(y, 4 * half + role, core), owner,
                ).start()

    first_pair, pairs = len(DIRECT), CHUNKS - len(DIRECT)
    stages = {part: encode_send(part) for part in parts}
    stages.update(l=limit_send, m=ring_far, k=ring_near, n=ring_on, r=run_one, s=run_two)
    for name, q in ORDER:
        stages[name](q)

    frecv[8 * run + outer] = fsend[run, outer]
    for stage, like in enumerate(
        (y1send.at[pl.ds(first_pair, pairs)], y2send, z1send, lim2.at[pl.ds(0, 7)], frecv.at[pl.ds(0, 15)])
    ):
        wait_send(like, stage + 1)
    wait_send(xrecv, 6)
    wait_send(arecv.at[pl.ds(first_pair, pairs)], 0)
    wait_send(arecv.at[pl.ds(0, len(DIRECT)), pl.ds(1, 3)], 7)
    wait_recv(limrecv.at[pl.ds(0, 7)], l_rsem.at[0])
    wait_recv(frecv.at[pl.ds(0, 15)], f_rsem.at[0])
    total = jnp.zeros((16, 128), F32)
    for group in range(8):
        value = frecv[group].astype(F32) + frecv[8 + group].astype(F32)
        total = total + clip(value, limrecv[group].astype(F32))
    high = total.astype(BF16)
    low = (total - high.astype(F32)).astype(BF16)
    signs = table[0:128, 0:128]
    result = jnp.dot(high, signs, preferred_element_type=F32)
    result = result + jnp.dot(low, signs, preferred_element_type=F32)
    out_ref[...] = result * F32(RSQRT)


def shards(grads, first_exponents, second_exponents):
    rows, columns = grads.shape[2], grads.shape[3]
    first = first_exponents.reshape(rows, columns // 128).T
    second = second_exponents.reshape(1, rows)
    operands = (grads.reshape(rows, columns), first, second)
    dma = pltpu.SemaphoreType.DMA
    c, r = CHUNKS, CHUNK_ROWS
    return pl.pallas_call(
        kernel,
        out_shape=jax.ShapeDtypeStruct((16, 128), F32),
        in_specs=[pl.BlockSpec(memory_space=pltpu.HBM)] * 3,
        out_specs=pl.BlockSpec(memory_space=pltpu.VMEM),
        scratch_shapes=[
            pltpu.VMEM((c, 4, r, 1024), F32),
            pltpu.VMEM((columns // 128, rows), jnp.int32),
            pltpu.VMEM((1, rows), jnp.int32),
            pltpu.VMEM((256, 256), BF16),
            pltpu.VMEM((128, 128), BF16),
            pltpu.VMEM((8, 16, 128), BF16),
            pltpu.VMEM((c, 2, 4, 4, r, 128), BF16),
            pltpu.VMEM((c, 4, 4, r, 128), BF16),
            pltpu.VMEM((c, 2, 2, r, 128), BF16),
            pltpu.VMEM((c, 2, 2, r, 128), BF16),
            pltpu.VMEM((c, 2, 2, 2, r, 128), BF16),
            pltpu.VMEM((c, 2, 2, 2, r, 128), BF16),
            pltpu.VMEM((c, 3, r, 128), BF16),
            pltpu.VMEM((c, r, 128), F32),
            pltpu.VMEM((c, 3, r, 128), BF16),
            pltpu.VMEM((len(DIRECT), 2, 2, 2, r, 128), BF16),
            pltpu.VMEM((2, 8, 16, 128), BF16),
            pltpu.VMEM((16, 16, 128), BF16),
            pltpu.VMEM((8, 16, 128), BF16),
            dma((c, 4)),
            dma((2,)),
            dma((8,)),
            dma((c, 4)),
            dma((c,)),
            dma((c,)),
            dma((c,)),
            dma((1,)),
            dma((1,)),
        ],
        compiler_params=pltpu.CompilerParams(
            collective_id=0, has_side_effects=True, vmem_limit_bytes=48 * 1024 * 1024
        ),
        name="reduce_scatter",
    )(*(pltpu.with_memory_space_constraint(x, pltpu.HBM) for x in operands))


def solution(mesh):
    placed = (
        P("inner", "outer", None, None),
        P("inner", "outer", None, None),
        P("outer", None, "inner"),
    )
    return jax.shard_map(
        shards, mesh=mesh, in_specs=placed, out_specs=P("outer", "inner"), check_vma=False
    )
```

```python
import math

import jax
import jax.numpy as jnp
from jax import lax
from jax.experimental import pallas as pl
from jax.experimental.pallas import tpu as pltpu
from jax.sharding import PartitionSpec as P

SATURATION = 448.0
RSQRT = 1.0 / math.sqrt(128.0)
LOGICAL = pl.DeviceIdType.MESH
F32 = jnp.float32
BF16 = jnp.bfloat16
CHUNKS = 4
CHUNK_ROWS = 64
HALF = (0, 1, 1, 0)
DIRECT = (0, 1)
ORDER = tuple(
    (item[0], int(item[1:]))
    for line in (
        "f0 h0 h1 o0", "f1 h2 f2 f3", "k0 h3 n0 k1", "m2 o1 n1 m3", "r0 o2 k2 o3",
        "n2 k3 r1 n3", "l0 s0 r2 r3", "s1 s2 s3",
    )
    for item in line.split()
)


def sign_table():
    row = lax.broadcasted_iota(jnp.int32, (256, 256), 0)
    col = lax.broadcasted_iota(jnp.int32, (256, 256), 1)
    shared = row & col & 127
    shared = shared ^ (shared >> 4)
    shared = shared ^ (shared >> 2)
    shared = shared ^ (shared >> 1)
    signs = (1 - 2 * (shared & 1)).astype(F32)
    return jnp.where((row // 128) == (col // 128), signs, 0.0).astype(BF16)


def limits(exponents):
    return jnp.left_shift(1, exponents + 13).astype(F32) * F32(SATURATION / 8192.0)


def clip(value, bound):
    return jnp.minimum(jnp.maximum(value, -bound), bound)


def kernel(
    grads_ref, first_ref, second_ref, out_ref,
    gbuf, first_buf, second_buf, table, lim1, lim2, enc, arecv,
    y1send, y1recv, y2send, y2recv, z1send, z1own, z1recv, xrecv, fsend, frecv, limrecv,
    load_sem, scale_sem, send_sem, a_rsem, y1_rsem, y2_rsem, z1_rsem, l_rsem, f_rsem,
):
    inner = lax.axis_index("inner")
    outer = lax.axis_index("outer")
    core = inner % 2
    z = (inner // 2) % 8
    y = inner // 16
    run, role = z // 4, z % 4
    y_right, y_left, y_far = (y + 1) % 4, (y + 3) % 4, (y + 2) % 4

    def inner_of(yy, zz, cc):
        return (yy * 8 + zz) * 2 + cc

    sibling = inner_of(y, z, 1 - core)
    right = inner_of(y_right, z, core)
    left = inner_of(y_left, z, core)
    beside = [inner_of(y_right, z, 1 - core), inner_of(y_left, z, 1 - core)]
    across = inner_of(y, (1 - run) * 4 + role, core)
    mates = [inner_of(y, run * 4 + (role + d) % 4, core) for d in (1, 2, 3)]

    def remote(src, dst, stage, rsem, i, o=None):
        return pltpu.make_async_remote_copy(
            src_ref=src, dst_ref=dst, send_sem=send_sem.at[stage], recv_sem=rsem,
            device_id=(i, outer if o is None else o), device_id_type=LOGICAL,
        )

    def wait_recv(dst, rsem):
        remote(dst, dst, 0, rsem, sibling).wait_recv()

    def wait_send(like, stage):
        remote(like, like, stage, f_rsem.at[0], sibling).wait_send()

    scale_loads = [
        pltpu.make_async_copy(first_ref, first_buf, scale_sem.at[0]),
        pltpu.make_async_copy(second_ref, second_buf, scale_sem.at[1]),
    ]
    places = (y_far, y_right, y_left, y)
    parts = {"f": (0,), "h": (1, 2), "o": (3,)}

    def rows_of(q):
        return pl.ds(q // 2 * CHUNK_ROWS, CHUNK_ROWS)

    def load(q, d):
        columns = pl.ds(pl.multiple_of(places[d] * 2048 + HALF[q] * 1024, 1024), 1024)
        return pltpu.make_async_copy(
            grads_ref.at[rows_of(q), columns], gbuf.at[q, d], load_sem.at[q, d]
        )

    def start_loads(q):
        for d in range(4):
            load(q, d).start()

    for copy in scale_loads:
        copy.start()
    start_loads(0)

    lower, first_run = 1 - outer // 4, 1 - run
    klass = lower * first_run
    barrier = pltpu.get_barrier_semaphore()

    def hello(i, o):
        pl.semaphore_signal(barrier, inc=1, device_id=(i, o), device_id_type=LOGICAL)

    def hello_outer(same):
        for d in range(1, 8):
            owner = (outer + d) % 8
            other_lower = 1 - owner // 4
            for i, other in ((inner, other_lower * first_run), (across, other_lower * run)):

                @pl.when((other == klass) if same else (other != klass))
                def _():
                    hello(i, owner)

        @pl.when((lower * run == klass) if same else (lower * run != klass))
        def _():
            hello(across, outer)

    def enter():
        pl.semaphore_wait(barrier, 23 - 12 * klass)
        hello_outer(False)

    def enter_outer():
        @pl.when(klass == 1)
        def _():
            pl.semaphore_wait(barrier, 12)

    for i in [sibling, right, left] + beside + mates:
        hello(i, outer)
    hello_outer(True)

    start_loads(1)
    table[...] = sign_table()
    for copy in scale_loads:
        copy.wait()
    first = jnp.concatenate(
        [first_buf[pl.ds(pl.multiple_of(place * 16, 16), 16), :] for place in places] * 2, axis=0
    )
    lim1[...] = limits(first).T.astype(BF16)
    second = jnp.broadcast_to(limits(second_buf[...]), (128, 128)).T.astype(BF16)
    for owner in range(8):
        lim2[owner] = second[owner * 16 : (owner + 1) * 16]
    limrecv[outer] = lim2[outer]

    def encode(q, part):
        bounds = lim1[rows_of(q), :]
        pairs = [(d, k) for d in parts[part] for k in range(4)]
        for d in parts[part]:
            load(q, d).wait()
        if part == "h" and q + 2 < CHUNKS:
            start_loads(q + 2)
        lhs = jnp.concatenate(
            [gbuf[q, d, :, k * 256 : (k + 1) * 256].astype(BF16) for d, k in pairs], axis=0
        )
        rotated = jnp.dot(lhs, table[...], preferred_element_type=F32) * F32(RSQRT)
        rotated = rotated.astype(BF16)
        for i, (d, k) in enumerate(pairs):
            for c in range(2):
                lane = 16 * d + 8 * HALF[q] + 2 * k + c
                bound = jnp.broadcast_to(bounds[:, lane : lane + 1], (CHUNK_ROWS, 128))
                value = rotated[i * CHUNK_ROWS : (i + 1) * CHUNK_ROWS, c * 128 : (c + 1) * 128]
                enc[q, c, d, k] = clip(value, bound)

    def part_copy(q, part):
        span = pl.ds(parts[part][0], len(parts[part]))
        return remote(
            enc.at[q, 1 - core, span], arecv.at[q, span], 7 if q in DIRECT else 0,
            a_rsem.at[q, parts[part][0]], sibling,
        )

    def direct_copy(q, way, c):
        two = pl.ds(2 * way, 2)
        target = inner_of((y_right, y_left)[way], z, c)
        return remote(enc.at[q, c, 0, two], xrecv.at[q, core, way], 6, y1_rsem.at[q], target)

    def encode_send(part):
        def stage(q):
            encode(q, part)
            if part == "f" and q == 0:
                enter()
            if part == "f" and q in DIRECT:
                for way in range(2):
                    for c in range(2):
                        direct_copy(q, way, c).start()
            else:
                part_copy(q, part).start()

        return stage

    def pair_sum(q, d, way):
        two = pl.ds(2 * way, 2)
        return enc[q, core, d, two] + arecv[q, d, two]

    def limit_send(q):
        enter_outer()
        for d in range(1, 8):
            owner = (outer + d) % 8
            remote(lim2.at[owner], limrecv.at[outer], 4, l_rsem.at[0], inner, owner).start()

    def ring_far(q):
        if q in DIRECT:
            return
        part_copy(q, "f").wait_recv()
        for way, to in ((0, right), (1, left)):
            y1send[q, way] = pair_sum(q, 0, way)
            remote(y1send.at[q, way], y1recv.at[q, way], 1, y1_rsem.at[q], to).start()

    def ring_near(q):
        part_copy(q, "h").wait_recv()
        for way, to in ((0, right), (1, left)):
            y2send[q, way, 0] = pair_sum(q, 1 + way, 1 - way)
            remote(y2send.at[q, way, 0], y2recv.at[q, way, 0], 2, y2_rsem.at[q], to).start()

    def ring_on(q):
        wait_recv(xrecv.at[q] if q in DIRECT else y1recv.at[q], y1_rsem.at[q])
        for way, to in ((0, right), (1, left)):
            two = pl.ds(2 * way, 2)
            value = enc[q, core, 1 + way, two].astype(F32) + arecv[q, 1 + way, two].astype(F32)
            if q in DIRECT:
                value = value + xrecv[q, 0, way].astype(F32) + xrecv[q, 1, way].astype(F32)
            else:
                value = value + y1recv[q, way].astype(F32)
            y2send[q, way, 1] = value.astype(BF16)
            remote(y2send.at[q, way, 1], y2recv.at[q, way, 1], 2, y2_rsem.at[q], to).start()

    def run_one(q):
        part_copy(q, "o").wait_recv()
        wait_recv(y2recv.at[q], y2_rsem.at[q])
        for d in (1, 2, 3, 0):
            r = (role + d) % 4
            way, place = r // 2, r % 2
            value = enc[q, core, 3, r].astype(F32) + arecv[q, 3, r].astype(F32)
            value = value + y2recv[q, way, 1, place].astype(F32)
            value = value + y2recv[q, 1 - way, 0, place].astype(F32)
            if d:
                z1send[q, d - 1] = value.astype(BF16)
                remote(z1send.at[q, d - 1], z1recv.at[q, d - 1], 3, z1_rsem.at[q], mates[d - 1]).start()
            else:
                z1own[q] = value

    def run_two(q):
        wait_recv(z1recv.at[q], z1_rsem.at[q])
        value = z1own[q]
        for d in range(3):
            value = value + z1recv[q, d].astype(F32)
        value = value.astype(BF16)
        half = HALF[q]
        for h in range(4):
            owner = q // 2 * 4 + h
            fsend[half, owner] = value[h * 16 : (h + 1) * 16]
            here = jnp.logical_and(owner == outer, half == run)

            @pl.when(jnp.logical_not(here))
            def _():
                remote(
                    fsend.at[half, owner], frecv.at[8 * run + outer], 5, f_rsem.at[0],
                    inner_of(y, 4 * half + role, core), owner,
                ).start()

    first_pair, pairs = len(DIRECT), CHUNKS - len(DIRECT)
    stages = {part: encode_send(part) for part in parts}
    stages.update(l=limit_send, m=ring_far, k=ring_near, n=ring_on, r=run_one, s=run_two)
    for name, q in ORDER:
        stages[name](q)

    frecv[8 * run + outer] = fsend[run, outer]
    for stage, like in enumerate(
        (y1send.at[pl.ds(first_pair, pairs)], y2send, z1send, lim2.at[pl.ds(0, 7)], frecv.at[pl.ds(0, 15)])
    ):
        wait_send(like, stage + 1)
    wait_send(xrecv, 6)
    wait_send(arecv.at[pl.ds(first_pair, pairs)], 0)
    wait_send(arecv.at[pl.ds(0, len(DIRECT)), pl.ds(1, 3)], 7)
    wait_recv(limrecv.at[pl.ds(0, 7)], l_rsem.at[0])
    wait_recv(frecv.at[pl.ds(0, 15)], f_rsem.at[0])
    total = jnp.zeros((16, 128), F32)
    for group in range(8):
        value = frecv[group].astype(F32) + frecv[8 + group].astype(F32)
        total = total + clip(value, limrecv[group].astype(F32))
    high = total.astype(BF16)
    low = (total - high.astype(F32)).astype(BF16)
    signs = table[0:128, 0:128]
    result = jnp.dot(high, signs, preferred_element_type=F32)
    result = result + jnp.dot(low, signs, preferred_element_type=F32)
    out_ref[...] = result * F32(RSQRT)


def shards(grads, first_exponents, second_exponents):
    rows, columns = grads.shape[2], grads.shape[3]
    first = first_exponents.reshape(rows, columns // 128).T
    second = second_exponents.reshape(1, rows)
    operands = (grads.reshape(rows, columns), first, second)
    dma = pltpu.SemaphoreType.DMA
    c, r = CHUNKS, CHUNK_ROWS
    return pl.pallas_call(
        kernel,
        out_shape=jax.ShapeDtypeStruct((16, 128), F32),
        in_specs=[pl.BlockSpec(memory_space=pltpu.HBM)] * 3,
        out_specs=pl.BlockSpec(memory_space=pltpu.VMEM),
        scratch_shapes=[
            pltpu.VMEM((c, 4, r, 1024), F32),
            pltpu.VMEM((columns // 128, rows), jnp.int32),
            pltpu.VMEM((1, rows), jnp.int32),
            pltpu.VMEM((256, 256), BF16),
            pltpu.VMEM((128, 128), BF16),
            pltpu.VMEM((8, 16, 128), BF16),
            pltpu.VMEM((c, 2, 4, 4, r, 128), BF16),
            pltpu.VMEM((c, 4, 4, r, 128), BF16),
            pltpu.VMEM((c, 2, 2, r, 128), BF16),
            pltpu.VMEM((c, 2, 2, r, 128), BF16),
            pltpu.VMEM((c, 2, 2, 2, r, 128), BF16),
            pltpu.VMEM((c, 2, 2, 2, r, 128), BF16),
            pltpu.VMEM((c, 3, r, 128), BF16),
            pltpu.VMEM((c, r, 128), F32),
            pltpu.VMEM((c, 3, r, 128), BF16),
            pltpu.VMEM((len(DIRECT), 2, 2, 2, r, 128), BF16),
            pltpu.VMEM((2, 8, 16, 128), BF16),
            pltpu.VMEM((16, 16, 128), BF16),
            pltpu.VMEM((8, 16, 128), BF16),
            dma((c, 4)),
            dma((2,)),
            dma((8,)),
            dma((c, 4)),
            dma((c,)),
            dma((c,)),
            dma((c,)),
            dma((1,)),
            dma((1,)),
        ],
        compiler_params=pltpu.CompilerParams(
            collective_id=0, has_side_effects=True, vmem_limit_bytes=48 * 1024 * 1024
        ),
        name="reduce_scatter",
    )(*(pltpu.with_memory_space_constraint(x, pltpu.HBM) for x in operands))


def solution(mesh):
    placed = (
        P("inner", "outer", None, None),
        P("inner", "outer", None, None),
        P("outer", None, "inner"),
    )
    return jax.shard_map(
        shards, mesh=mesh, in_specs=placed, out_specs=P("outer", "inner"), check_vma=False
    )
```

```python
import math

import jax
import jax.numpy as jnp
from jax import lax
from jax.experimental import pallas as pl
from jax.experimental.pallas import tpu as pltpu
from jax.sharding import PartitionSpec as P

SATURATION = 448.0
RSQRT = 1.0 / math.sqrt(128.0)
LOGICAL = pl.DeviceIdType.MESH
F32 = jnp.float32
BF16 = jnp.bfloat16
CHUNKS = 4
CHUNK_ROWS = 64
HALF = (0, 1, 1, 0)
DIRECT = (0, 1)
ORDER = tuple(
    (item[0], int(item[1:]))
    for line in (
        "f0 h0 h1 o0", "f1 h2 f2 f3", "k0 h3 n0 k1", "m2 o1 n1 m3", "l0 r0 o2 k2",
        "o3 n2 k3 r1", "n3 s0 r2 r3", "s1 s2 s3",
    )
    for item in line.split()
)


def sign_table():
    row = lax.broadcasted_iota(jnp.int32, (256, 256), 0)
    col = lax.broadcasted_iota(jnp.int32, (256, 256), 1)
    shared = row & col & 127
    shared = shared ^ (shared >> 4)
    shared = shared ^ (shared >> 2)
    shared = shared ^ (shared >> 1)
    signs = (1 - 2 * (shared & 1)).astype(F32)
    return jnp.where((row // 128) == (col // 128), signs, 0.0).astype(BF16)


def limits(exponents):
    return jnp.left_shift(1, exponents + 13).astype(F32) * F32(SATURATION / 8192.0)


def clip(value, bound):
    return jnp.minimum(jnp.maximum(value, -bound), bound)


def kernel(
    grads_ref, first_ref, second_ref, out_ref,
    gbuf, first_buf, second_buf, table, lim1, lim2, enc, arecv,
    y1send, y1recv, y2send, y2recv, z1send, z1own, z1recv, xrecv, fsend, frecv, limrecv,
    load_sem, scale_sem, send_sem, a_rsem, y1_rsem, y2_rsem, z1_rsem, l_rsem, f_rsem,
):
    inner = lax.axis_index("inner")
    outer = lax.axis_index("outer")
    core = inner % 2
    z = (inner // 2) % 8
    y = inner // 16
    run, role = z // 4, z % 4
    y_right, y_left, y_far = (y + 1) % 4, (y + 3) % 4, (y + 2) % 4

    def inner_of(yy, zz, cc):
        return (yy * 8 + zz) * 2 + cc

    sibling = inner_of(y, z, 1 - core)
    right = inner_of(y_right, z, core)
    left = inner_of(y_left, z, core)
    beside = [inner_of(y_right, z, 1 - core), inner_of(y_left, z, 1 - core)]
    across = inner_of(y, (1 - run) * 4 + role, core)
    mates = [inner_of(y, run * 4 + (role + d) % 4, core) for d in (1, 2, 3)]

    def remote(src, dst, stage, rsem, i, o=None):
        return pltpu.make_async_remote_copy(
            src_ref=src, dst_ref=dst, send_sem=send_sem.at[stage], recv_sem=rsem,
            device_id=(i, outer if o is None else o), device_id_type=LOGICAL,
        )

    def wait_recv(dst, rsem):
        remote(dst, dst, 0, rsem, sibling).wait_recv()

    def wait_send(like, stage):
        remote(like, like, stage, f_rsem.at[0], sibling).wait_send()

    scale_loads = [
        pltpu.make_async_copy(first_ref, first_buf, scale_sem.at[0]),
        pltpu.make_async_copy(second_ref, second_buf, scale_sem.at[1]),
    ]
    places = (y_far, y_right, y_left, y)
    parts = {"f": (0,), "h": (1, 2), "o": (3,)}

    def rows_of(q):
        return pl.ds(q // 2 * CHUNK_ROWS, CHUNK_ROWS)

    def load(q, d):
        columns = pl.ds(pl.multiple_of(places[d] * 2048 + HALF[q] * 1024, 1024), 1024)
        return pltpu.make_async_copy(
            grads_ref.at[rows_of(q), columns], gbuf.at[q, d], load_sem.at[q, d]
        )

    def start_loads(q):
        for d in range(4):
            load(q, d).start()

    for copy in scale_loads:
        copy.start()
    start_loads(0)

    lower, first_run = 1 - outer // 4, 1 - run
    klass = lower * first_run
    barrier = pltpu.get_barrier_semaphore()

    def hello(i, o):
        pl.semaphore_signal(barrier, inc=1, device_id=(i, o), device_id_type=LOGICAL)

    def hello_outer(same):
        for d in range(1, 8):
            owner = (outer + d) % 8
            other_lower = 1 - owner // 4
            for i, other in ((inner, other_lower * first_run), (across, other_lower * run)):

                @pl.when((other == klass) if same else (other != klass))
                def _():
                    hello(i, owner)

        @pl.when((lower * run == klass) if same else (lower * run != klass))
        def _():
            hello(across, outer)

    def enter():
        pl.semaphore_wait(barrier, 23 - 12 * klass)

    def enter_outer():
        @pl.when(klass == 1)
        def _():
            pl.semaphore_wait(barrier, 12)

    for i in [sibling, right, left] + beside + mates:
        hello(i, outer)
    hello_outer(True)

    start_loads(1)
    table[...] = sign_table()
    for copy in scale_loads:
        copy.wait()
    first = jnp.concatenate(
        [first_buf[pl.ds(pl.multiple_of(place * 16, 16), 16), :] for place in places] * 2, axis=0
    )
    lim1[...] = limits(first).T.astype(BF16)
    second = jnp.broadcast_to(limits(second_buf[...]), (128, 128)).T.astype(BF16)
    for owner in range(8):
        lim2[owner] = second[owner * 16 : (owner + 1) * 16]
    limrecv[outer] = lim2[outer]

    def encode(q, part):
        bounds = lim1[rows_of(q), :]
        pairs = [(d, k) for d in parts[part] for k in range(4)]
        for d in parts[part]:
            load(q, d).wait()
        if part == "h" and q + 2 < CHUNKS:
            start_loads(q + 2)
        lhs = jnp.concatenate(
            [gbuf[q, d, :, k * 256 : (k + 1) * 256].astype(BF16) for d, k in pairs], axis=0
        )
        rotated = jnp.dot(lhs, table[...], preferred_element_type=F32) * F32(RSQRT)
        rotated = rotated.astype(BF16)
        for i, (d, k) in enumerate(pairs):
            for c in range(2):
                lane = 16 * d + 8 * HALF[q] + 2 * k + c
                bound = jnp.broadcast_to(bounds[:, lane : lane + 1], (CHUNK_ROWS, 128))
                value = rotated[i * CHUNK_ROWS : (i + 1) * CHUNK_ROWS, c * 128 : (c + 1) * 128]
                enc[q, c, d, k] = clip(value, bound)

    def part_copy(q, part):
        span = pl.ds(parts[part][0], len(parts[part]))
        return remote(
            enc.at[q, 1 - core, span], arecv.at[q, span], 7 if q in DIRECT else 0,
            a_rsem.at[q, parts[part][0]], sibling,
        )

    def direct_copy(q, way, c):
        two = pl.ds(2 * way, 2)
        target = inner_of((y_right, y_left)[way], z, c)
        return remote(enc.at[q, c, 0, two], xrecv.at[q, core, way], 6, y1_rsem.at[q], target)

    def encode_send(part):
        def stage(q):
            encode(q, part)
            if part == "f" and q == 0:
                enter()
            if part == "f" and q in DIRECT:
                for way in range(2):
                    for c in range(2):
                        direct_copy(q, way, c).start()
            else:
                part_copy(q, part).start()
            if part == "f" and q == 0:
                hello_outer(False)

        return stage

    def pair_sum(q, d, way):
        two = pl.ds(2 * way, 2)
        return enc[q, core, d, two] + arecv[q, d, two]

    def limit_send(q):
        enter_outer()
        for d in range(1, 8):
            owner = (outer + d) % 8
            remote(lim2.at[owner], limrecv.at[outer], 4, l_rsem.at[0], inner, owner).start()

    def ring_far(q):
        if q in DIRECT:
            return
        part_copy(q, "f").wait_recv()
        for way, to in ((0, right), (1, left)):
            y1send[q, way] = pair_sum(q, 0, way)
            remote(y1send.at[q, way], y1recv.at[q, way], 1, y1_rsem.at[q], to).start()

    def ring_near(q):
        part_copy(q, "h").wait_recv()
        for way, to in ((0, right), (1, left)):
            y2send[q, way, 0] = pair_sum(q, 1 + way, 1 - way)
            remote(y2send.at[q, way, 0], y2recv.at[q, way, 0], 2, y2_rsem.at[q], to).start()

    def ring_on(q):
        wait_recv(xrecv.at[q] if q in DIRECT else y1recv.at[q], y1_rsem.at[q])
        for way, to in ((0, right), (1, left)):
            two = pl.ds(2 * way, 2)
            value = enc[q, core, 1 + way, two].astype(F32) + arecv[q, 1 + way, two].astype(F32)
            if q in DIRECT:
                value = value + xrecv[q, 0, way].astype(F32) + xrecv[q, 1, way].astype(F32)
            else:
                value = value + y1recv[q, way].astype(F32)
            y2send[q, way, 1] = value.astype(BF16)
            remote(y2send.at[q, way, 1], y2recv.at[q, way, 1], 2, y2_rsem.at[q], to).start()

    def run_one(q):
        part_copy(q, "o").wait_recv()
        wait_recv(y2recv.at[q], y2_rsem.at[q])
        for d in (1, 2, 3, 0):
            r = (role + d) % 4
            way, place = r // 2, r % 2
            value = enc[q, core, 3, r].astype(F32) + arecv[q, 3, r].astype(F32)
            value = value + y2recv[q, way, 1, place].astype(F32)
            value = value + y2recv[q, 1 - way, 0, place].astype(F32)
            if d:
                z1send[q, d - 1] = value.astype(BF16)
                remote(z1send.at[q, d - 1], z1recv.at[q, d - 1], 3, z1_rsem.at[q], mates[d - 1]).start()
            else:
                z1own[q] = value

    def run_two(q):
        wait_recv(z1recv.at[q], z1_rsem.at[q])
        value = z1own[q]
        for d in range(3):
            value = value + z1recv[q, d].astype(F32)
        value = value.astype(BF16)
        half = HALF[q]
        for h in range(4):
            owner = q // 2 * 4 + h
            fsend[half, owner] = value[h * 16 : (h + 1) * 16]
            here = jnp.logical_and(owner == outer, half == run)

            @pl.when(jnp.logical_not(here))
            def _():
                remote(
                    fsend.at[half, owner], frecv.at[8 * run + outer], 5, f_rsem.at[0],
                    inner_of(y, 4 * half + role, core), owner,
                ).start()

    first_pair, pairs = len(DIRECT), CHUNKS - len(DIRECT)
    stages = {part: encode_send(part) for part in parts}
    stages.update(l=limit_send, m=ring_far, k=ring_near, n=ring_on, r=run_one, s=run_two)
    for name, q in ORDER:
        stages[name](q)

    frecv[8 * run + outer] = fsend[run, outer]
    for stage, like in enumerate(
        (y1send.at[pl.ds(first_pair, pairs)], y2send, z1send, lim2.at[pl.ds(0, 7)], frecv.at[pl.ds(0, 15)])
    ):
        wait_send(like, stage + 1)
    wait_send(xrecv, 6)
    wait_send(arecv.at[pl.ds(first_pair, pairs)], 0)
    wait_send(arecv.at[pl.ds(0, len(DIRECT)), pl.ds(1, 3)], 7)
    wait_recv(limrecv.at[pl.ds(0, 7)], l_rsem.at[0])
    wait_recv(frecv.at[pl.ds(0, 15)], f_rsem.at[0])
    total = jnp.zeros((16, 128), F32)
    for group in range(8):
        value = frecv[group].astype(F32) + frecv[8 + group].astype(F32)
        total = total + clip(value, limrecv[group].astype(F32))
    high = total.astype(BF16)
    low = (total - high.astype(F32)).astype(BF16)
    signs = table[0:128, 0:128]
    result = jnp.dot(high, signs, preferred_element_type=F32)
    result = result + jnp.dot(low, signs, preferred_element_type=F32)
    out_ref[...] = result * F32(RSQRT)


def shards(grads, first_exponents, second_exponents):
    rows, columns = grads.shape[2], grads.shape[3]
    first = first_exponents.reshape(rows, columns // 128).T
    second = second_exponents.reshape(1, rows)
    operands = (grads.reshape(rows, columns), first, second)
    dma = pltpu.SemaphoreType.DMA
    c, r = CHUNKS, CHUNK_ROWS
    return pl.pallas_call(
        kernel,
        out_shape=jax.ShapeDtypeStruct((16, 128), F32),
        in_specs=[pl.BlockSpec(memory_space=pltpu.HBM)] * 3,
        out_specs=pl.BlockSpec(memory_space=pltpu.VMEM),
        scratch_shapes=[
            pltpu.VMEM((c, 4, r, 1024), F32),
            pltpu.VMEM((columns // 128, rows), jnp.int32),
            pltpu.VMEM((1, rows), jnp.int32),
            pltpu.VMEM((256, 256), BF16),
            pltpu.VMEM((128, 128), BF16),
            pltpu.VMEM((8, 16, 128), BF16),
            pltpu.VMEM((c, 2, 4, 4, r, 128), BF16),
            pltpu.VMEM((c, 4, 4, r, 128), BF16),
            pltpu.VMEM((c, 2, 2, r, 128), BF16),
            pltpu.VMEM((c, 2, 2, r, 128), BF16),
            pltpu.VMEM((c, 2, 2, 2, r, 128), BF16),
            pltpu.VMEM((c, 2, 2, 2, r, 128), BF16),
            pltpu.VMEM((c, 3, r, 128), BF16),
            pltpu.VMEM((c, r, 128), F32),
            pltpu.VMEM((c, 3, r, 128), BF16),
            pltpu.VMEM((len(DIRECT), 2, 2, 2, r, 128), BF16),
            pltpu.VMEM((2, 8, 16, 128), BF16),
            pltpu.VMEM((16, 16, 128), BF16),
            pltpu.VMEM((8, 16, 128), BF16),
            dma((c, 4)),
            dma((2,)),
            dma((8,)),
            dma((c, 4)),
            dma((c,)),
            dma((c,)),
            dma((c,)),
            dma((1,)),
            dma((1,)),
        ],
        compiler_params=pltpu.CompilerParams(
            collective_id=0, has_side_effects=True, vmem_limit_bytes=48 * 1024 * 1024
        ),
        name="reduce_scatter",
    )(*(pltpu.with_memory_space_constraint(x, pltpu.HBM) for x in operands))


def solution(mesh):
    placed = (
        P("inner", "outer", None, None),
        P("inner", "outer", None, None),
        P("outer", None, "inner"),
    )
    return jax.shard_map(
        shards, mesh=mesh, in_specs=placed, out_specs=P("outer", "inner"), check_vma=False
    )
```

```python
import math

import jax
import jax.numpy as jnp
from jax import lax
from jax.experimental import pallas as pl
from jax.experimental.pallas import tpu as pltpu
from jax.sharding import PartitionSpec as P

SATURATION = 448.0
RSQRT = 1.0 / math.sqrt(128.0)
LOGICAL = pl.DeviceIdType.MESH
F32 = jnp.float32
BF16 = jnp.bfloat16
CHUNKS = 4
CHUNK_ROWS = 64
HALF = (0, 1, 1, 0)
DIRECT = (0, 1)
ORDER = tuple(
    (item[0], int(item[1:]))
    for line in (
        "f0 h0 h1 o0", "f1 h2 f2 f3", "p0 k0 h3 n0", "k1 m2 o1 n1", "m3 l0 r0 o2",
        "k2 o3 n2 k3", "r1 n3 s0 r2", "r3 s1 s2 s3",
    )
    for item in line.split()
)


def sign_table():
    row = lax.broadcasted_iota(jnp.int32, (256, 256), 0)
    col = lax.broadcasted_iota(jnp.int32, (256, 256), 1)
    shared = row & col & 127
    shared = shared ^ (shared >> 4)
    shared = shared ^ (shared >> 2)
    shared = shared ^ (shared >> 1)
    signs = (1 - 2 * (shared & 1)).astype(F32)
    return jnp.where((row // 128) == (col // 128), signs, 0.0).astype(BF16)


def limits(exponents):
    return jnp.left_shift(1, exponents + 13).astype(F32) * F32(SATURATION / 8192.0)


def clip(value, bound):
    return jnp.minimum(jnp.maximum(value, -bound), bound)


def kernel(
    grads_ref, first_ref, second_ref, out_ref,
    gbuf, first_buf, second_buf, table, lim1, lim2, enc, arecv,
    y1send, y1recv, y2send, y2recv, z1send, z1own, z1recv, xrecv, fsend, frecv, limrecv,
    load_sem, scale_sem, send_sem, a_rsem, y1_rsem, y2_rsem, z1_rsem, l_rsem, f_rsem,
):
    inner = lax.axis_index("inner")
    outer = lax.axis_index("outer")
    core = inner % 2
    z = (inner // 2) % 8
    y = inner // 16
    run, role = z // 4, z % 4
    y_right, y_left, y_far = (y + 1) % 4, (y + 3) % 4, (y + 2) % 4

    def inner_of(yy, zz, cc):
        return (yy * 8 + zz) * 2 + cc

    sibling = inner_of(y, z, 1 - core)
    right = inner_of(y_right, z, core)
    left = inner_of(y_left, z, core)
    beside = [inner_of(y_right, z, 1 - core), inner_of(y_left, z, 1 - core)]
    across = inner_of(y, (1 - run) * 4 + role, core)
    mates = [inner_of(y, run * 4 + (role + d) % 4, core) for d in (1, 2, 3)]

    def remote(src, dst, stage, rsem, i, o=None):
        return pltpu.make_async_remote_copy(
            src_ref=src, dst_ref=dst, send_sem=send_sem.at[stage], recv_sem=rsem,
            device_id=(i, outer if o is None else o), device_id_type=LOGICAL,
        )

    def wait_recv(dst, rsem):
        remote(dst, dst, 0, rsem, sibling).wait_recv()

    def wait_send(like, stage):
        remote(like, like, stage, f_rsem.at[0], sibling).wait_send()

    scale_loads = [
        pltpu.make_async_copy(first_ref, first_buf, scale_sem.at[0]),
        pltpu.make_async_copy(second_ref, second_buf, scale_sem.at[1]),
    ]
    places = (y_far, y_right, y_left, y)
    parts = {"f": (0,), "h": (1, 2), "o": (3,)}

    def rows_of(q):
        return pl.ds(q // 2 * CHUNK_ROWS, CHUNK_ROWS)

    def load(q, d):
        columns = pl.ds(pl.multiple_of(places[d] * 2048 + HALF[q] * 1024, 1024), 1024)
        return pltpu.make_async_copy(
            grads_ref.at[rows_of(q), columns], gbuf.at[q, d], load_sem.at[q, d]
        )

    def start_loads(q):
        for d in range(4):
            load(q, d).start()

    for copy in scale_loads:
        copy.start()
    start_loads(0)

    lower, first_run = 1 - outer // 4, 1 - run
    klass = lower * first_run
    barrier = pltpu.get_barrier_semaphore()

    def hello(i, o):
        pl.semaphore_signal(barrier, inc=1, device_id=(i, o), device_id_type=LOGICAL)

    def hello_first():
        for i in [sibling, right, left] + beside + mates:
            hello(i, outer)
        for d in range(1, 4):
            hello(inner, outer // 4 * 4 + (outer + d) % 4)

        @pl.when(klass == 0)
        def _():
            other = lower * inner + (1 - lower) * (first_run * across + run * inner)
            for j in range(4):
                hello(across, 4 + j)
                hello(other, 4 * lower + j)

    def hello_second(q):
        @pl.when(klass == 1)
        def _():
            for j in range(4):
                hello(across, j)
                hello(across, 4 + j)
                hello(inner, 4 + j)

        @pl.when(klass == 0)
        def _():
            early = lower * across + (1 - lower) * (first_run * inner + run * across)
            for j in range(4):
                hello(early, j)

    def enter():
        pl.semaphore_wait(barrier, 23 - 12 * klass)

    def enter_outer():
        @pl.when(klass == 1)
        def _():
            pl.semaphore_wait(barrier, 12)

    hello_first()

    start_loads(1)
    table[...] = sign_table()
    for copy in scale_loads:
        copy.wait()
    first = jnp.concatenate(
        [first_buf[pl.ds(pl.multiple_of(place * 16, 16), 16), :] for place in places] * 2, axis=0
    )
    lim1[...] = limits(first).T.astype(BF16)
    second = jnp.broadcast_to(limits(second_buf[...]), (128, 128)).T.astype(BF16)
    for owner in range(8):
        lim2[owner] = second[owner * 16 : (owner + 1) * 16]
    limrecv[outer] = lim2[outer]

    def encode(q, part):
        bounds = lim1[rows_of(q), :]
        pairs = [(d, k) for d in parts[part] for k in range(4)]
        for d in parts[part]:
            load(q, d).wait()
        if part == "h" and q + 2 < CHUNKS:
            start_loads(q + 2)
        lhs = jnp.concatenate(
            [gbuf[q, d, :, k * 256 : (k + 1) * 256].astype(BF16) for d, k in pairs], axis=0
        )
        rotated = jnp.dot(lhs, table[...], preferred_element_type=F32) * F32(RSQRT)
        rotated = rotated.astype(BF16)
        for i, (d, k) in enumerate(pairs):
            for c in range(2):
                lane = 16 * d + 8 * HALF[q] + 2 * k + c
                bound = jnp.broadcast_to(bounds[:, lane : lane + 1], (CHUNK_ROWS, 128))
                value = rotated[i * CHUNK_ROWS : (i + 1) * CHUNK_ROWS, c * 128 : (c + 1) * 128]
                enc[q, c, d, k] = clip(value, bound)

    def part_copy(q, part):
        span = pl.ds(parts[part][0], len(parts[part]))
        return remote(
            enc.at[q, 1 - core, span], arecv.at[q, span], 7 if q in DIRECT else 0,
            a_rsem.at[q, parts[part][0]], sibling,
        )

    def direct_copy(q, way, c):
        two = pl.ds(2 * way, 2)
        target = inner_of((y_right, y_left)[way], z, c)
        return remote(enc.at[q, c, 0, two], xrecv.at[q, core, way], 6, y1_rsem.at[q], target)

    def encode_send(part):
        def stage(q):
            encode(q, part)
            if part == "f" and q == 0:
                enter()
            if part == "f" and q in DIRECT:
                for way in range(2):
                    for c in range(2):
                        direct_copy(q, way, c).start()
            else:
                part_copy(q, part).start()

        return stage

    def pair_sum(q, d, way):
        two = pl.ds(2 * way, 2)
        return enc[q, core, d, two] + arecv[q, d, two]

    def limit_send(q):
        enter_outer()
        for d in range(1, 8):
            owner = (outer + d) % 8
            remote(lim2.at[owner], limrecv.at[outer], 4, l_rsem.at[0], inner, owner).start()

    def ring_far(q):
        if q in DIRECT:
            return
        part_copy(q, "f").wait_recv()
        for way, to in ((0, right), (1, left)):
            y1send[q, way] = pair_sum(q, 0, way)
            remote(y1send.at[q, way], y1recv.at[q, way], 1, y1_rsem.at[q], to).start()

    def ring_near(q):
        part_copy(q, "h").wait_recv()
        for way, to in ((0, right), (1, left)):
            y2send[q, way, 0] = pair_sum(q, 1 + way, 1 - way)
            remote(y2send.at[q, way, 0], y2recv.at[q, way, 0], 2, y2_rsem.at[q], to).start()

    def ring_on(q):
        wait_recv(xrecv.at[q] if q in DIRECT else y1recv.at[q], y1_rsem.at[q])
        for way, to in ((0, right), (1, left)):
            two = pl.ds(2 * way, 2)
            value = enc[q, core, 1 + way, two].astype(F32) + arecv[q, 1 + way, two].astype(F32)
            if q in DIRECT:
                value = value + xrecv[q, 0, way].astype(F32) + xrecv[q, 1, way].astype(F32)
            else:
                value = value + y1recv[q, way].astype(F32)
            y2send[q, way, 1] = value.astype(BF16)
            remote(y2send.at[q, way, 1], y2recv.at[q, way, 1], 2, y2_rsem.at[q], to).start()

    def run_one(q):
        part_copy(q, "o").wait_recv()
        wait_recv(y2recv.at[q], y2_rsem.at[q])
        for d in (1, 2, 3, 0):
            r = (role + d) % 4
            way, place = r // 2, r % 2
            value = enc[q, core, 3, r].astype(F32) + arecv[q, 3, r].astype(F32)
            value = value + y2recv[q, way, 1, place].astype(F32)
            value = value + y2recv[q, 1 - way, 0, place].astype(F32)
            if d:
                z1send[q, d - 1] = value.astype(BF16)
                remote(z1send.at[q, d - 1], z1recv.at[q, d - 1], 3, z1_rsem.at[q], mates[d - 1]).start()
            else:
                z1own[q] = value

    def run_two(q):
        wait_recv(z1recv.at[q], z1_rsem.at[q])
        value = z1own[q]
        for d in range(3):
            value = value + z1recv[q, d].astype(F32)
        value = value.astype(BF16)
        half = HALF[q]
        for h in range(4):
            owner = q // 2 * 4 + h
            fsend[half, owner] = value[h * 16 : (h + 1) * 16]
            here = jnp.logical_and(owner == outer, half == run)

            @pl.when(jnp.logical_not(here))
            def _():
                remote(
                    fsend.at[half, owner], frecv.at[8 * run + outer], 5, f_rsem.at[0],
                    inner_of(y, 4 * half + role, core), owner,
                ).start()

    first_pair, pairs = len(DIRECT), CHUNKS - len(DIRECT)
    stages = {part: encode_send(part) for part in parts}
    stages.update(p=hello_second, l=limit_send, m=ring_far, k=ring_near, n=ring_on, r=run_one, s=run_two)
    for name, q in ORDER:
        stages[name](q)

    frecv[8 * run + outer] = fsend[run, outer]
    for stage, like in enumerate(
        (y1send.at[pl.ds(first_pair, pairs)], y2send, z1send, lim2.at[pl.ds(0, 7)], frecv.at[pl.ds(0, 15)])
    ):
        wait_send(like, stage + 1)
    wait_send(xrecv, 6)
    wait_send(arecv.at[pl.ds(first_pair, pairs)], 0)
    wait_send(arecv.at[pl.ds(0, len(DIRECT)), pl.ds(1, 3)], 7)
    wait_recv(limrecv.at[pl.ds(0, 7)], l_rsem.at[0])
    wait_recv(frecv.at[pl.ds(0, 15)], f_rsem.at[0])
    total = jnp.zeros((16, 128), F32)
    for group in range(8):
        value = frecv[group].astype(F32) + frecv[8 + group].astype(F32)
        total = total + clip(value, limrecv[group].astype(F32))
    high = total.astype(BF16)
    low = (total - high.astype(F32)).astype(BF16)
    signs = table[0:128, 0:128]
    result = jnp.dot(high, signs, preferred_element_type=F32)
    result = result + jnp.dot(low, signs, preferred_element_type=F32)
    out_ref[...] = result * F32(RSQRT)


def shards(grads, first_exponents, second_exponents):
    rows, columns = grads.shape[2], grads.shape[3]
    first = first_exponents.reshape(rows, columns // 128).T
    second = second_exponents.reshape(1, rows)
    operands = (grads.reshape(rows, columns), first, second)
    dma = pltpu.SemaphoreType.DMA
    c, r = CHUNKS, CHUNK_ROWS
    return pl.pallas_call(
        kernel,
        out_shape=jax.ShapeDtypeStruct((16, 128), F32),
        in_specs=[pl.BlockSpec(memory_space=pltpu.HBM)] * 3,
        out_specs=pl.BlockSpec(memory_space=pltpu.VMEM),
        scratch_shapes=[
            pltpu.VMEM((c, 4, r, 1024), F32),
            pltpu.VMEM((columns // 128, rows), jnp.int32),
            pltpu.VMEM((1, rows), jnp.int32),
            pltpu.VMEM((256, 256), BF16),
            pltpu.VMEM((128, 128), BF16),
            pltpu.VMEM((8, 16, 128), BF16),
            pltpu.VMEM((c, 2, 4, 4, r, 128), BF16),
            pltpu.VMEM((c, 4, 4, r, 128), BF16),
            pltpu.VMEM((c, 2, 2, r, 128), BF16),
            pltpu.VMEM((c, 2, 2, r, 128), BF16),
            pltpu.VMEM((c, 2, 2, 2, r, 128), BF16),
            pltpu.VMEM((c, 2, 2, 2, r, 128), BF16),
            pltpu.VMEM((c, 3, r, 128), BF16),
            pltpu.VMEM((c, r, 128), F32),
            pltpu.VMEM((c, 3, r, 128), BF16),
            pltpu.VMEM((len(DIRECT), 2, 2, 2, r, 128), BF16),
            pltpu.VMEM((2, 8, 16, 128), BF16),
            pltpu.VMEM((16, 16, 128), BF16),
            pltpu.VMEM((8, 16, 128), BF16),
            dma((c, 4)),
            dma((2,)),
            dma((8,)),
            dma((c, 4)),
            dma((c,)),
            dma((c,)),
            dma((c,)),
            dma((1,)),
            dma((1,)),
        ],
        compiler_params=pltpu.CompilerParams(
            collective_id=0, has_side_effects=True, vmem_limit_bytes=48 * 1024 * 1024
        ),
        name="reduce_scatter",
    )(*(pltpu.with_memory_space_constraint(x, pltpu.HBM) for x in operands))


def solution(mesh):
    placed = (
        P("inner", "outer", None, None),
        P("inner", "outer", None, None),
        P("outer", None, "inner"),
    )
    return jax.shard_map(
        shards, mesh=mesh, in_specs=placed, out_specs=P("outer", "inner"), check_vma=False
    )
```

```python
import math

import jax
import jax.numpy as jnp
from jax import lax
from jax.experimental import pallas as pl
from jax.experimental.pallas import tpu as pltpu
from jax.sharding import PartitionSpec as P

SATURATION = 448.0
RSQRT = 1.0 / math.sqrt(128.0)
LOGICAL = pl.DeviceIdType.MESH
F32 = jnp.float32
BF16 = jnp.bfloat16
CHUNKS = 4
CHUNK_ROWS = 64
HALF = (0, 1, 1, 0)
DIRECT = (0, 1)
ORDER = tuple(
    (item[0], int(item[1:]))
    for line in (
        "f0 h0 o0 h1", "f1 h2 f2 f3", "p0 k0 h3 n0", "k1 m2 n1 m3", "l0 r0 k2 n2",
        "k3 r1 n3 s0", "r2 r3 s1 s2", "s3",
    )
    for item in line.split()
)


def sign_table():
    row = lax.broadcasted_iota(jnp.int32, (256, 256), 0)
    col = lax.broadcasted_iota(jnp.int32, (256, 256), 1)
    shared = row & col & 127
    shared = shared ^ (shared >> 4)
    shared = shared ^ (shared >> 2)
    shared = shared ^ (shared >> 1)
    signs = (1 - 2 * (shared & 1)).astype(F32)
    return jnp.where((row // 128) == (col // 128), signs, 0.0).astype(BF16)


def limits(exponents):
    return jnp.left_shift(1, exponents + 13).astype(F32) * F32(SATURATION / 8192.0)


def clip(value, bound):
    return jnp.minimum(jnp.maximum(value, -bound), bound)


def kernel(
    grads_ref, first_ref, second_ref, out_ref,
    gbuf, first_buf, second_buf, table, lim1, lim2, enc, arecv,
    y1send, y1recv, y2send, y2recv, z1send, z1own, z1recv, xrecv, fsend, frecv, limrecv,
    load_sem, scale_sem, send_sem, a_rsem, y1_rsem, y2_rsem, z1_rsem, l_rsem, f_rsem,
):
    inner = lax.axis_index("inner")
    outer = lax.axis_index("outer")
    core = inner % 2
    z = (inner // 2) % 8
    y = inner // 16
    run, role = z // 4, z % 4
    y_right, y_left, y_far = (y + 1) % 4, (y + 3) % 4, (y + 2) % 4

    def inner_of(yy, zz, cc):
        return (yy * 8 + zz) * 2 + cc

    sibling = inner_of(y, z, 1 - core)
    right = inner_of(y_right, z, core)
    left = inner_of(y_left, z, core)
    beside = [inner_of(y_right, z, 1 - core), inner_of(y_left, z, 1 - core)]
    across = inner_of(y, (1 - run) * 4 + role, core)
    mates = [inner_of(y, run * 4 + (role + d) % 4, core) for d in (1, 2, 3)]

    def remote(src, dst, stage, rsem, i, o=None):
        return pltpu.make_async_remote_copy(
            src_ref=src, dst_ref=dst, send_sem=send_sem.at[stage], recv_sem=rsem,
            device_id=(i, outer if o is None else o), device_id_type=LOGICAL,
        )

    def wait_recv(dst, rsem):
        remote(dst, dst, 0, rsem, sibling).wait_recv()

    def wait_send(like, stage):
        remote(like, like, stage, f_rsem.at[0], sibling).wait_send()

    scale_loads = [
        pltpu.make_async_copy(first_ref, first_buf, scale_sem.at[0]),
        pltpu.make_async_copy(second_ref, second_buf, scale_sem.at[1]),
    ]
    places = (y_far, y_right, y_left, y)

    def places_of(q, part):
        return {"f": (0,), "h": (1, 2, 3) if q else (1, 2), "o": (3,)}[part]

    def rows_of(q):
        return pl.ds(q // 2 * CHUNK_ROWS, CHUNK_ROWS)

    def load(q, d):
        columns = pl.ds(pl.multiple_of(places[d] * 2048 + HALF[q] * 1024, 1024), 1024)
        return pltpu.make_async_copy(
            grads_ref.at[rows_of(q), columns], gbuf.at[q, d], load_sem.at[q, d]
        )

    def start_loads(q):
        for d in range(4):
            load(q, d).start()

    for copy in scale_loads:
        copy.start()
    start_loads(0)

    lower, first_run = 1 - outer // 4, 1 - run
    klass = lower * first_run
    barrier = pltpu.get_barrier_semaphore()

    def hello(i, o):
        pl.semaphore_signal(barrier, inc=1, device_id=(i, o), device_id_type=LOGICAL)

    def hello_first():
        for i in [sibling, right, left] + beside + mates:
            hello(i, outer)
        for d in range(1, 4):
            hello(inner, outer // 4 * 4 + (outer + d) % 4)

        @pl.when(klass == 0)
        def _():
            other = lower * inner + (1 - lower) * (first_run * across + run * inner)
            for j in range(4):
                hello(across, 4 + j)
                hello(other, 4 * lower + j)

    def hello_second(q):
        second = jnp.broadcast_to(limits(second_buf[...]), (128, 128)).T.astype(BF16)
        for owner in range(8):
            lim2[owner] = second[owner * 16 : (owner + 1) * 16]
        limrecv[outer] = lim2[outer]

        @pl.when(klass == 1)
        def _():
            for j in range(4):
                hello(across, j)
                hello(across, 4 + j)
                hello(inner, 4 + j)

        @pl.when(klass == 0)
        def _():
            early = lower * across + (1 - lower) * (first_run * inner + run * across)
            for j in range(4):
                hello(early, j)

    def enter():
        pl.semaphore_wait(barrier, 23 - 12 * klass)

    def enter_outer():
        @pl.when(klass == 1)
        def _():
            pl.semaphore_wait(barrier, 12)

    hello_first()

    table[...] = sign_table()
    for copy in scale_loads:
        copy.wait()
    first = jnp.concatenate(
        [first_buf[pl.ds(pl.multiple_of(place * 16, 16), 16), :] for place in places] * 2, axis=0
    )
    lim1[...] = limits(first).T.astype(BF16)

    def encode(q, part):
        bounds = lim1[rows_of(q), :]
        pairs = [(d, k) for d in places_of(q, part) for k in range(4)]
        for d in places_of(q, part):
            load(q, d).wait()
        if part == "h" and q + 2 < CHUNKS:
            start_loads(q + 2)
        lhs = jnp.concatenate(
            [gbuf[q, d, :, k * 256 : (k + 1) * 256].astype(BF16) for d, k in pairs], axis=0
        )
        rotated = jnp.dot(lhs, table[...], preferred_element_type=F32) * F32(RSQRT)
        rotated = rotated.astype(BF16)
        for i, (d, k) in enumerate(pairs):
            for c in range(2):
                lane = 16 * d + 8 * HALF[q] + 2 * k + c
                bound = jnp.broadcast_to(bounds[:, lane : lane + 1], (CHUNK_ROWS, 128))
                value = rotated[i * CHUNK_ROWS : (i + 1) * CHUNK_ROWS, c * 128 : (c + 1) * 128]
                enc[q, c, d, k] = clip(value, bound)

    def part_copy(q, part):
        places = places_of(q, part)
        span = pl.ds(places[0], len(places))
        return remote(
            enc.at[q, 1 - core, span], arecv.at[q, span], 7 if q in DIRECT else 0,
            a_rsem.at[q, places[0]], sibling,
        )

    def direct_copy(q, way, c):
        two = pl.ds(2 * way, 2)
        target = inner_of((y_right, y_left)[way], z, c)
        return remote(enc.at[q, c, 0, two], xrecv.at[q, core, way], 6, y1_rsem.at[q], target)

    def encode_send(part):
        def stage(q):
            encode(q, part)
            if part == "f" and q == 0:
                enter()
            if part == "f" and q in DIRECT:
                for way in range(2):
                    for c in range(2):
                        direct_copy(q, way, c).start()
            else:
                part_copy(q, part).start()
            if part == "f" and q == 0:
                start_loads(1)

        return stage

    def pair_sum(q, d, way):
        two = pl.ds(2 * way, 2)
        return enc[q, core, d, two] + arecv[q, d, two]

    def limit_send(q):
        enter_outer()
        for d in range(1, 8):
            owner = (outer + d) % 8
            remote(lim2.at[owner], limrecv.at[outer], 4, l_rsem.at[0], inner, owner).start()

    def ring_far(q):
        if q in DIRECT:
            return
        part_copy(q, "f").wait_recv()
        for way, to in ((0, right), (1, left)):
            y1send[q, way] = pair_sum(q, 0, way)
            remote(y1send.at[q, way], y1recv.at[q, way], 1, y1_rsem.at[q], to).start()

    def ring_near(q):
        part_copy(q, "h").wait_recv()
        for way, to in ((0, right), (1, left)):
            y2send[q, way, 0] = pair_sum(q, 1 + way, 1 - way)
            remote(y2send.at[q, way, 0], y2recv.at[q, way, 0], 2, y2_rsem.at[q], to).start()

    def ring_on(q):
        wait_recv(xrecv.at[q] if q in DIRECT else y1recv.at[q], y1_rsem.at[q])
        for way, to in ((0, right), (1, left)):
            two = pl.ds(2 * way, 2)
            value = enc[q, core, 1 + way, two].astype(F32) + arecv[q, 1 + way, two].astype(F32)
            if q in DIRECT:
                value = value + xrecv[q, 0, way].astype(F32) + xrecv[q, 1, way].astype(F32)
            else:
                value = value + y1recv[q, way].astype(F32)
            y2send[q, way, 1] = value.astype(BF16)
            remote(y2send.at[q, way, 1], y2recv.at[q, way, 1], 2, y2_rsem.at[q], to).start()

    def run_one(q):
        if q == 0:
            part_copy(q, "o").wait_recv()
        wait_recv(y2recv.at[q], y2_rsem.at[q])
        for d in (1, 2, 3, 0):
            r = (role + d) % 4
            way, place = r // 2, r % 2
            value = enc[q, core, 3, r].astype(F32) + arecv[q, 3, r].astype(F32)
            value = value + y2recv[q, way, 1, place].astype(F32)
            value = value + y2recv[q, 1 - way, 0, place].astype(F32)
            if d:
                z1send[q, d - 1] = value.astype(BF16)
                remote(z1send.at[q, d - 1], z1recv.at[q, d - 1], 3, z1_rsem.at[q], mates[d - 1]).start()
            else:
                z1own[q] = value

    def run_two(q):
        wait_recv(z1recv.at[q], z1_rsem.at[q])
        value = z1own[q]
        for d in range(3):
            value = value + z1recv[q, d].astype(F32)
        value = value.astype(BF16)
        half = HALF[q]
        for h in range(4):
            owner = q // 2 * 4 + h
            fsend[half, owner] = value[h * 16 : (h + 1) * 16]
            here = jnp.logical_and(owner == outer, half == run)

            @pl.when(jnp.logical_not(here))
            def _():
                remote(
                    fsend.at[half, owner], frecv.at[8 * run + outer], 5, f_rsem.at[0],
                    inner_of(y, 4 * half + role, core), owner,
                ).start()

    first_pair, pairs = len(DIRECT), CHUNKS - len(DIRECT)
    stages = {part: encode_send(part) for part in "fho"}
    stages.update(p=hello_second, l=limit_send, m=ring_far, k=ring_near, n=ring_on, r=run_one, s=run_two)
    for name, q in ORDER:
        stages[name](q)

    frecv[8 * run + outer] = fsend[run, outer]
    for stage, like in enumerate(
        (y1send.at[pl.ds(first_pair, pairs)], y2send, z1send, lim2.at[pl.ds(0, 7)], frecv.at[pl.ds(0, 15)])
    ):
        wait_send(like, stage + 1)
    wait_send(xrecv, 6)
    wait_send(arecv.at[pl.ds(first_pair, pairs)], 0)
    wait_send(arecv.at[pl.ds(0, len(DIRECT)), pl.ds(1, 3)], 7)
    wait_recv(limrecv.at[pl.ds(0, 7)], l_rsem.at[0])
    wait_recv(frecv.at[pl.ds(0, 15)], f_rsem.at[0])
    total = jnp.zeros((16, 128), F32)
    for group in range(8):
        value = frecv[group].astype(F32) + frecv[8 + group].astype(F32)
        total = total + clip(value, limrecv[group].astype(F32))
    high = total.astype(BF16)
    low = (total - high.astype(F32)).astype(BF16)
    signs = table[0:128, 0:128]
    result = jnp.dot(high, signs, preferred_element_type=F32)
    result = result + jnp.dot(low, signs, preferred_element_type=F32)
    out_ref[...] = result * F32(RSQRT)


def shards(grads, first_exponents, second_exponents):
    rows, columns = grads.shape[2], grads.shape[3]
    first = first_exponents.reshape(rows, columns // 128).T
    second = second_exponents.reshape(1, rows)
    operands = (grads.reshape(rows, columns), first, second)
    dma = pltpu.SemaphoreType.DMA
    c, r = CHUNKS, CHUNK_ROWS
    return pl.pallas_call(
        kernel,
        out_shape=jax.ShapeDtypeStruct((16, 128), F32),
        in_specs=[pl.BlockSpec(memory_space=pltpu.HBM)] * 3,
        out_specs=pl.BlockSpec(memory_space=pltpu.VMEM),
        scratch_shapes=[
            pltpu.VMEM((c, 4, r, 1024), F32),
            pltpu.VMEM((columns // 128, rows), jnp.int32),
            pltpu.VMEM((1, rows), jnp.int32),
            pltpu.VMEM((256, 256), BF16),
            pltpu.VMEM((128, 128), BF16),
            pltpu.VMEM((8, 16, 128), BF16),
            pltpu.VMEM((c, 2, 4, 4, r, 128), BF16),
            pltpu.VMEM((c, 4, 4, r, 128), BF16),
            pltpu.VMEM((c, 2, 2, r, 128), BF16),
            pltpu.VMEM((c, 2, 2, r, 128), BF16),
            pltpu.VMEM((c, 2, 2, 2, r, 128), BF16),
            pltpu.VMEM((c, 2, 2, 2, r, 128), BF16),
            pltpu.VMEM((c, 3, r, 128), BF16),
            pltpu.VMEM((c, r, 128), F32),
            pltpu.VMEM((c, 3, r, 128), BF16),
            pltpu.VMEM((len(DIRECT), 2, 2, 2, r, 128), BF16),
            pltpu.VMEM((2, 8, 16, 128), BF16),
            pltpu.VMEM((16, 16, 128), BF16),
            pltpu.VMEM((8, 16, 128), BF16),
            dma((c, 4)),
            dma((2,)),
            dma((8,)),
            dma((c, 4)),
            dma((c,)),
            dma((c,)),
            dma((c,)),
            dma((1,)),
            dma((1,)),
        ],
        compiler_params=pltpu.CompilerParams(
            collective_id=0, has_side_effects=True, vmem_limit_bytes=48 * 1024 * 1024
        ),
        name="reduce_scatter",
    )(*(pltpu.with_memory_space_constraint(x, pltpu.HBM) for x in operands))


def solution(mesh):
    placed = (
        P("inner", "outer", None, None),
        P("inner", "outer", None, None),
        P("outer", None, "inner"),
    )
    return jax.shard_map(
        shards, mesh=mesh, in_specs=placed, out_specs=P("outer", "inner"), check_vma=False
    )
```

```python
import math

import jax
import jax.numpy as jnp
from jax import lax
from jax.experimental import pallas as pl
from jax.experimental.pallas import tpu as pltpu
from jax.sharding import PartitionSpec as P

SATURATION = 448.0
RSQRT = 1.0 / math.sqrt(128.0)
LOGICAL = pl.DeviceIdType.MESH
F32 = jnp.float32
BF16 = jnp.bfloat16
CHUNKS = 4
CHUNK_ROWS = 64
HALF = (0, 1, 1, 0)
DIRECT = (0, 1)
ORDER = tuple(
    (item[0], int(item[1:]))
    for line in (
        "f0 h0 h1 o0", "f1 h2 f2 f3", "p0 k0 h3 n0", "k1 m2 o1 n1", "m3 l0 r0 o2",
        "k2 o3 n2 k3", "r1 n3 s0 r2", "r3 s1 s2 s3",
    )
    for item in line.split()
)


def sign_table():
    row = lax.broadcasted_iota(jnp.int32, (256, 256), 0)
    col = lax.broadcasted_iota(jnp.int32, (256, 256), 1)
    shared = row & col & 127
    shared = shared ^ (shared >> 4)
    shared = shared ^ (shared >> 2)
    shared = shared ^ (shared >> 1)
    signs = (1 - 2 * (shared & 1)).astype(F32)
    return jnp.where((row // 128) == (col // 128), signs, 0.0).astype(BF16)


def limits(exponents):
    return jnp.left_shift(1, exponents + 13).astype(F32) * F32(SATURATION / 8192.0)


def clip(value, bound):
    return jnp.minimum(jnp.maximum(value, -bound), bound)


def kernel(
    grads_ref, first_ref, second_ref, out_ref,
    gbuf, first_buf, second_buf, table, lim1, lim2, enc, arecv,
    y1send, y1recv, y2send, y2recv, z1send, z1own, z1recv, xrecv, fsend, frecv, limrecv,
    load_sem, scale_sem, send_sem, a_rsem, y1_rsem, y2_rsem, z1_rsem, l_rsem, f_rsem,
):
    inner = lax.axis_index("inner")
    outer = lax.axis_index("outer")
    core = inner % 2
    z = (inner // 2) % 8
    y = inner // 16
    run, role = z // 4, z % 4
    y_right, y_left, y_far = (y + 1) % 4, (y + 3) % 4, (y + 2) % 4

    def inner_of(yy, zz, cc):
        return (yy * 8 + zz) * 2 + cc

    sibling = inner_of(y, z, 1 - core)
    right = inner_of(y_right, z, core)
    left = inner_of(y_left, z, core)
    beside = [inner_of(y_right, z, 1 - core), inner_of(y_left, z, 1 - core)]
    across = inner_of(y, (1 - run) * 4 + role, core)
    mates = [inner_of(y, run * 4 + (role + d) % 4, core) for d in (1, 2, 3)]

    def remote(src, dst, stage, rsem, i, o=None):
        return pltpu.make_async_remote_copy(
            src_ref=src, dst_ref=dst, send_sem=send_sem.at[stage], recv_sem=rsem,
            device_id=(i, outer if o is None else o), device_id_type=LOGICAL,
        )

    def wait_recv(dst, rsem):
        remote(dst, dst, 0, rsem, sibling).wait_recv()

    def wait_send(like, stage):
        remote(like, like, stage, f_rsem.at[0], sibling).wait_send()

    scale_loads = [
        pltpu.make_async_copy(first_ref, first_buf, scale_sem.at[0]),
        pltpu.make_async_copy(second_ref, second_buf, scale_sem.at[1]),
    ]
    places = (y_far, y_right, y_left, y)
    parts = {"f": (0,), "h": (1, 2), "o": (3,)}

    def rows_of(q):
        return pl.ds(q // 2 * CHUNK_ROWS, CHUNK_ROWS)

    def load(q, d):
        columns = pl.ds(pl.multiple_of(places[d] * 2048 + HALF[q] * 1024, 1024), 1024)
        return pltpu.make_async_copy(
            grads_ref.at[rows_of(q), columns], gbuf.at[q, d], load_sem.at[q, d]
        )

    def start_loads(q):
        for d in range(4):
            load(q, d).start()

    for copy in scale_loads:
        copy.start()
    load(0, 0).start()

    lower, first_run = 1 - outer // 4, 1 - run
    klass = lower * first_run
    barrier = pltpu.get_barrier_semaphore()

    def hello(i, o):
        pl.semaphore_signal(barrier, inc=1, device_id=(i, o), device_id_type=LOGICAL)

    def hello_first():
        for i in [sibling, right, left] + beside + mates:
            hello(i, outer)
        for d in range(1, 4):
            hello(inner, outer // 4 * 4 + (outer + d) % 4)

        @pl.when(klass == 0)
        def _():
            other = lower * inner + (1 - lower) * (first_run * across + run * inner)
            for j in range(4):
                hello(across, 4 + j)
                hello(other, 4 * lower + j)

    def hello_second(q):
        @pl.when(klass == 1)
        def _():
            for j in range(4):
                hello(across, j)
                hello(across, 4 + j)
                hello(inner, 4 + j)

        @pl.when(klass == 0)
        def _():
            early = lower * across + (1 - lower) * (first_run * inner + run * across)
            for j in range(4):
                hello(early, j)

    def enter():
        pl.semaphore_wait(barrier, 23 - 12 * klass)

    def enter_outer():
        @pl.when(klass == 1)
        def _():
            pl.semaphore_wait(barrier, 12)

    hello_first()
    for d in (1, 2, 3):
        load(0, d).start()

    start_loads(1)
    table[...] = sign_table()
    for copy in scale_loads:
        copy.wait()
    first = jnp.concatenate(
        [first_buf[pl.ds(pl.multiple_of(place * 16, 16), 16), :] for place in places] * 2, axis=0
    )
    lim1[...] = limits(first).T.astype(BF16)

    def encode(q, part):
        bounds = lim1[rows_of(q), :]
        pairs = [(d, k) for d in parts[part] for k in range(4)]
        for d in parts[part]:
            load(q, d).wait()
        if part == "h" and q + 2 < CHUNKS:
            start_loads(q + 2)
        lhs = jnp.concatenate(
            [gbuf[q, d, :, k * 256 : (k + 1) * 256].astype(BF16) for d, k in pairs], axis=0
        )
        rotated = jnp.dot(lhs, table[...], preferred_element_type=F32) * F32(RSQRT)
        rotated = rotated.astype(BF16)
        for i, (d, k) in enumerate(pairs):
            for c in range(2):
                lane = 16 * d + 8 * HALF[q] + 2 * k + c
                bound = jnp.broadcast_to(bounds[:, lane : lane + 1], (CHUNK_ROWS, 128))
                value = rotated[i * CHUNK_ROWS : (i + 1) * CHUNK_ROWS, c * 128 : (c + 1) * 128]
                enc[q, c, d, k] = clip(value, bound)

    def part_copy(q, part):
        span = pl.ds(parts[part][0], len(parts[part]))
        return remote(
            enc.at[q, 1 - core, span], arecv.at[q, span], 7 if q in DIRECT else 0,
            a_rsem.at[q, parts[part][0]], sibling,
        )

    def direct_copy(q, way, c):
        two = pl.ds(2 * way, 2)
        target = inner_of((y_right, y_left)[way], z, c)
        return remote(enc.at[q, c, 0, two], xrecv.at[q, core, way], 6, y1_rsem.at[q], target)

    def encode_send(part):
        def stage(q):
            encode(q, part)
            if part == "f" and q == 0:
                enter()
            if part == "f" and q in DIRECT:
                for way in range(2):
                    for c in range(2):
                        direct_copy(q, way, c).start()
            else:
                part_copy(q, part).start()

        return stage

    def pair_sum(q, d, way):
        two = pl.ds(2 * way, 2)
        return enc[q, core, d, two] + arecv[q, d, two]

    def limit_send(q):
        second = jnp.broadcast_to(limits(second_buf[...]), (128, 128)).T.astype(BF16)
        for owner in range(8):
            lim2[owner] = second[owner * 16 : (owner + 1) * 16]
        limrecv[outer] = lim2[outer]
        enter_outer()
        for d in range(1, 8):
            owner = (outer + d) % 8
            remote(lim2.at[owner], limrecv.at[outer], 4, l_rsem.at[0], inner, owner).start()

    def ring_far(q):
        if q in DIRECT:
            return
        part_copy(q, "f").wait_recv()
        for way, to in ((0, right), (1, left)):
            y1send[q, way] = pair_sum(q, 0, way)
            remote(y1send.at[q, way], y1recv.at[q, way], 1, y1_rsem.at[q], to).start()

    def ring_near(q):
        part_copy(q, "h").wait_recv()
        for way, to in ((0, right), (1, left)):
            y2send[q, way, 0] = pair_sum(q, 1 + way, 1 - way)
            remote(y2send.at[q, way, 0], y2recv.at[q, way, 0], 2, y2_rsem.at[q], to).start()

    def ring_on(q):
        wait_recv(xrecv.at[q] if q in DIRECT else y1recv.at[q], y1_rsem.at[q])
        for way, to in ((0, right), (1, left)):
            two = pl.ds(2 * way, 2)
            value = enc[q, core, 1 + way, two].astype(F32) + arecv[q, 1 + way, two].astype(F32)
            if q in DIRECT:
                value = value + xrecv[q, 0, way].astype(F32) + xrecv[q, 1, way].astype(F32)
            else:
                value = value + y1recv[q, way].astype(F32)
            y2send[q, way, 1] = value.astype(BF16)
            remote(y2send.at[q, way, 1], y2recv.at[q, way, 1], 2, y2_rsem.at[q], to).start()

    def run_one(q):
        part_copy(q, "o").wait_recv()
        wait_recv(y2recv.at[q], y2_rsem.at[q])
        for d in (1, 2, 3, 0):
            r = (role + d) % 4
            way, place = r // 2, r % 2
            value = enc[q, core, 3, r].astype(F32) + arecv[q, 3, r].astype(F32)
            value = value + y2recv[q, way, 1, place].astype(F32)
            value = value + y2recv[q, 1 - way, 0, place].astype(F32)
            if d:
                z1send[q, d - 1] = value.astype(BF16)
                remote(z1send.at[q, d - 1], z1recv.at[q, d - 1], 3, z1_rsem.at[q], mates[d - 1]).start()
            else:
                z1own[q] = value

    def run_two(q):
        wait_recv(z1recv.at[q], z1_rsem.at[q])
        value = z1own[q]
        for d in range(3):
            value = value + z1recv[q, d].astype(F32)
        value = value.astype(BF16)
        half = HALF[q]
        for h in range(4):
            owner = q // 2 * 4 + h
            fsend[half, owner] = value[h * 16 : (h + 1) * 16]
            here = jnp.logical_and(owner == outer, half == run)

            @pl.when(jnp.logical_not(here))
            def _():
                remote(
                    fsend.at[half, owner], frecv.at[8 * run + outer], 5, f_rsem.at[0],
                    inner_of(y, 4 * half + role, core), owner,
                ).start()

    first_pair, pairs = len(DIRECT), CHUNKS - len(DIRECT)
    stages = {part: encode_send(part) for part in parts}
    stages.update(p=hello_second, l=limit_send, m=ring_far, k=ring_near, n=ring_on, r=run_one, s=run_two)
    for name, q in ORDER:
        stages[name](q)

    frecv[8 * run + outer] = fsend[run, outer]
    for stage, like in enumerate(
        (y1send.at[pl.ds(first_pair, pairs)], y2send, z1send, lim2.at[pl.ds(0, 7)], frecv.at[pl.ds(0, 15)])
    ):
        wait_send(like, stage + 1)
    wait_send(xrecv, 6)
    wait_send(arecv.at[pl.ds(first_pair, pairs)], 0)
    wait_send(arecv.at[pl.ds(0, len(DIRECT)), pl.ds(1, 3)], 7)
    wait_recv(limrecv.at[pl.ds(0, 7)], l_rsem.at[0])
    wait_recv(frecv.at[pl.ds(0, 15)], f_rsem.at[0])
    total = jnp.zeros((16, 128), F32)
    for group in range(8):
        value = frecv[group].astype(F32) + frecv[8 + group].astype(F32)
        total = total + clip(value, limrecv[group].astype(F32))
    high = total.astype(BF16)
    low = (total - high.astype(F32)).astype(BF16)
    signs = table[0:128, 0:128]
    result = jnp.dot(high, signs, preferred_element_type=F32)
    result = result + jnp.dot(low, signs, preferred_element_type=F32)
    out_ref[...] = result * F32(RSQRT)


def shards(grads, first_exponents, second_exponents):
    rows, columns = grads.shape[2], grads.shape[3]
    first = first_exponents.reshape(rows, columns // 128).T
    second = second_exponents.reshape(1, rows)
    operands = (grads.reshape(rows, columns), first, second)
    dma = pltpu.SemaphoreType.DMA
    c, r = CHUNKS, CHUNK_ROWS
    return pl.pallas_call(
        kernel,
        out_shape=jax.ShapeDtypeStruct((16, 128), F32),
        in_specs=[pl.BlockSpec(memory_space=pltpu.HBM)] * 3,
        out_specs=pl.BlockSpec(memory_space=pltpu.VMEM),
        scratch_shapes=[
            pltpu.VMEM((c, 4, r, 1024), F32),
            pltpu.VMEM((columns // 128, rows), jnp.int32),
            pltpu.VMEM((1, rows), jnp.int32),
            pltpu.VMEM((256, 256), BF16),
            pltpu.VMEM((128, 128), BF16),
            pltpu.VMEM((8, 16, 128), BF16),
            pltpu.VMEM((c, 2, 4, 4, r, 128), BF16),
            pltpu.VMEM((c, 4, 4, r, 128), BF16),
            pltpu.VMEM((c, 2, 2, r, 128), BF16),
            pltpu.VMEM((c, 2, 2, r, 128), BF16),
            pltpu.VMEM((c, 2, 2, 2, r, 128), BF16),
            pltpu.VMEM((c, 2, 2, 2, r, 128), BF16),
            pltpu.VMEM((c, 3, r, 128), BF16),
            pltpu.VMEM((c, r, 128), F32),
            pltpu.VMEM((c, 3, r, 128), BF16),
            pltpu.VMEM((len(DIRECT), 2, 2, 2, r, 128), BF16),
            pltpu.VMEM((2, 8, 16, 128), BF16),
            pltpu.VMEM((16, 16, 128), BF16),
            pltpu.VMEM((8, 16, 128), BF16),
            dma((c, 4)),
            dma((2,)),
            dma((8,)),
            dma((c, 4)),
            dma((c,)),
            dma((c,)),
            dma((c,)),
            dma((1,)),
            dma((1,)),
        ],
        compiler_params=pltpu.CompilerParams(
            collective_id=0, has_side_effects=True, vmem_limit_bytes=48 * 1024 * 1024
        ),
        name="reduce_scatter",
    )(*(pltpu.with_memory_space_constraint(x, pltpu.HBM) for x in operands))


def solution(mesh):
    placed = (
        P("inner", "outer", None, None),
        P("inner", "outer", None, None),
        P("outer", None, "inner"),
    )
    return jax.shard_map(
        shards, mesh=mesh, in_specs=placed, out_specs=P("outer", "inner"), check_vma=False
    )
```

```python
import math

import jax
import jax.numpy as jnp
from jax import lax
from jax.experimental import pallas as pl
from jax.experimental.pallas import tpu as pltpu
from jax.sharding import PartitionSpec as P

SATURATION = 448.0
RSQRT = 1.0 / math.sqrt(128.0)
LOGICAL = pl.DeviceIdType.MESH
F32 = jnp.float32
BF16 = jnp.bfloat16
CHUNKS = 4
CHUNK_ROWS = 64
HALF = (0, 1, 1, 0)
DIRECT = (0, 1)
ORDER = tuple(
    (item[0], int(item[1:]))
    for line in (
        "f0 h0 h1 f1", "h2 f2 f3 p0", "k0 n0 o0 h3", "k1 m2 o1 n1", "m3 l0 r0 o2",
        "k2 o3 n2 k3", "r1 n3 s0 r2", "r3 s1 s2 s3",
    )
    for item in line.split()
)


def sign_table():
    row = lax.broadcasted_iota(jnp.int32, (256, 256), 0)
    col = lax.broadcasted_iota(jnp.int32, (256, 256), 1)
    shared = row & col & 127
    shared = shared ^ (shared >> 4)
    shared = shared ^ (shared >> 2)
    shared = shared ^ (shared >> 1)
    signs = (1 - 2 * (shared & 1)).astype(F32)
    return jnp.where((row // 128) == (col // 128), signs, 0.0).astype(BF16)


def limits(exponents):
    return jnp.left_shift(1, exponents + 13).astype(F32) * F32(SATURATION / 8192.0)


def clip(value, bound):
    return jnp.minimum(jnp.maximum(value, -bound), bound)


def kernel(
    grads_ref, first_ref, second_ref, out_ref,
    gbuf, first_buf, second_buf, table, lim1, lim2, enc, arecv,
    y1send, y1recv, y2send, y2recv, z1send, z1own, z1recv, xrecv, fsend, frecv, limrecv,
    load_sem, scale_sem, send_sem, a_rsem, y1_rsem, y2_rsem, z1_rsem, l_rsem, f_rsem,
):
    inner = lax.axis_index("inner")
    outer = lax.axis_index("outer")
    core = inner % 2
    z = (inner // 2) % 8
    y = inner // 16
    run, role = z // 4, z % 4
    y_right, y_left, y_far = (y + 1) % 4, (y + 3) % 4, (y + 2) % 4

    def inner_of(yy, zz, cc):
        return (yy * 8 + zz) * 2 + cc

    sibling = inner_of(y, z, 1 - core)
    right = inner_of(y_right, z, core)
    left = inner_of(y_left, z, core)
    beside = [inner_of(y_right, z, 1 - core), inner_of(y_left, z, 1 - core)]
    across = inner_of(y, (1 - run) * 4 + role, core)
    mates = [inner_of(y, run * 4 + (role + d) % 4, core) for d in (1, 2, 3)]

    def remote(src, dst, stage, rsem, i, o=None):
        return pltpu.make_async_remote_copy(
            src_ref=src, dst_ref=dst, send_sem=send_sem.at[stage], recv_sem=rsem,
            device_id=(i, outer if o is None else o), device_id_type=LOGICAL,
        )

    def wait_recv(dst, rsem):
        remote(dst, dst, 0, rsem, sibling).wait_recv()

    def wait_send(like, stage):
        remote(like, like, stage, f_rsem.at[0], sibling).wait_send()

    scale_loads = [
        pltpu.make_async_copy(first_ref, first_buf, scale_sem.at[0]),
        pltpu.make_async_copy(second_ref, second_buf, scale_sem.at[1]),
    ]
    places = (y_far, y_right, y_left, y)
    parts = {"f": (0,), "h": (1, 2), "o": (3,)}

    def rows_of(q):
        return pl.ds(q // 2 * CHUNK_ROWS, CHUNK_ROWS)

    def load(q, d):
        columns = pl.ds(pl.multiple_of(places[d] * 2048 + HALF[q] * 1024, 1024), 1024)
        return pltpu.make_async_copy(
            grads_ref.at[rows_of(q), columns], gbuf.at[q, d], load_sem.at[q, d]
        )

    def start_loads(q):
        for d in range(4):
            load(q, d).start()

    for copy in scale_loads:
        copy.start()
    load(0, 0).start()

    lower, first_run = 1 - outer // 4, 1 - run
    klass = lower * first_run
    barrier = pltpu.get_barrier_semaphore()

    def hello(i, o):
        pl.semaphore_signal(barrier, inc=1, device_id=(i, o), device_id_type=LOGICAL)

    def hello_first():
        for i in [sibling, right, left] + beside + mates:
            hello(i, outer)
        for d in range(1, 4):
            hello(inner, outer // 4 * 4 + (outer + d) % 4)

        @pl.when(klass == 0)
        def _():
            other = lower * inner + (1 - lower) * (first_run * across + run * inner)
            for j in range(4):
                hello(across, 4 + j)
                hello(other, 4 * lower + j)

    def hello_second(q):
        @pl.when(klass == 1)
        def _():
            for j in range(4):
                hello(across, j)
                hello(across, 4 + j)
                hello(inner, 4 + j)

        @pl.when(klass == 0)
        def _():
            early = lower * across + (1 - lower) * (first_run * inner + run * across)
            for j in range(4):
                hello(early, j)

    def enter():
        pl.semaphore_wait(barrier, 23 - 12 * klass)

    def enter_outer():
        @pl.when(klass == 1)
        def _():
            pl.semaphore_wait(barrier, 12)

    hello_first()
    for d in (1, 2, 3):
        load(0, d).start()

    start_loads(1)
    table[...] = sign_table()
    for copy in scale_loads:
        copy.wait()
    first = jnp.concatenate(
        [first_buf[pl.ds(pl.multiple_of(place * 16, 16), 16), :] for place in places] * 2, axis=0
    )
    lim1[...] = limits(first).T.astype(BF16)

    def encode(q, part):
        bounds = lim1[rows_of(q), :]
        pairs = [(d, k) for d in parts[part] for k in range(4)]
        for d in parts[part]:
            load(q, d).wait()
        if part == "h" and q + 2 < CHUNKS:
            start_loads(q + 2)
        lhs = jnp.concatenate(
            [gbuf[q, d, :, k * 256 : (k + 1) * 256].astype(BF16) for d, k in pairs], axis=0
        )
        rotated = jnp.dot(lhs, table[...], preferred_element_type=F32) * F32(RSQRT)
        rotated = rotated.astype(BF16)
        for i, (d, k) in enumerate(pairs):
            for c in range(2):
                lane = 16 * d + 8 * HALF[q] + 2 * k + c
                bound = jnp.broadcast_to(bounds[:, lane : lane + 1], (CHUNK_ROWS, 128))
                value = rotated[i * CHUNK_ROWS : (i + 1) * CHUNK_ROWS, c * 128 : (c + 1) * 128]
                enc[q, c, d, k] = clip(value, bound)

    def part_copy(q, part):
        span = pl.ds(parts[part][0], len(parts[part]))
        return remote(
            enc.at[q, 1 - core, span], arecv.at[q, span], 7 if q in DIRECT else 0,
            a_rsem.at[q, parts[part][0]], sibling,
        )

    def direct_copy(q, way, c):
        two = pl.ds(2 * way, 2)
        target = inner_of((y_right, y_left)[way], z, c)
        return remote(enc.at[q, c, 0, two], xrecv.at[q, core, way], 6, y1_rsem.at[q], target)

    def encode_send(part):
        def stage(q):
            encode(q, part)
            if part == "f" and q == 0:
                enter()
            if part == "f" and q in DIRECT:
                for way in range(2):
                    for c in range(2):
                        direct_copy(q, way, c).start()
            else:
                part_copy(q, part).start()

        return stage

    def pair_sum(q, d, way):
        two = pl.ds(2 * way, 2)
        return enc[q, core, d, two] + arecv[q, d, two]

    def limit_send(q):
        second = jnp.broadcast_to(limits(second_buf[...]), (128, 128)).T.astype(BF16)
        for owner in range(8):
            lim2[owner] = second[owner * 16 : (owner + 1) * 16]
        limrecv[outer] = lim2[outer]
        enter_outer()
        for d in range(1, 8):
            owner = (outer + d) % 8
            remote(lim2.at[owner], limrecv.at[outer], 4, l_rsem.at[0], inner, owner).start()

    def ring_far(q):
        if q in DIRECT:
            return
        part_copy(q, "f").wait_recv()
        for way, to in ((0, right), (1, left)):
            y1send[q, way] = pair_sum(q, 0, way)
            remote(y1send.at[q, way], y1recv.at[q, way], 1, y1_rsem.at[q], to).start()

    def ring_near(q):
        part_copy(q, "h").wait_recv()
        for way, to in ((0, right), (1, left)):
            y2send[q, way, 0] = pair_sum(q, 1 + way, 1 - way)
            remote(y2send.at[q, way, 0], y2recv.at[q, way, 0], 2, y2_rsem.at[q], to).start()

    def ring_on(q):
        wait_recv(xrecv.at[q] if q in DIRECT else y1recv.at[q], y1_rsem.at[q])
        for way, to in ((0, right), (1, left)):
            two = pl.ds(2 * way, 2)
            value = enc[q, core, 1 + way, two].astype(F32) + arecv[q, 1 + way, two].astype(F32)
            if q in DIRECT:
                value = value + xrecv[q, 0, way].astype(F32) + xrecv[q, 1, way].astype(F32)
            else:
                value = value + y1recv[q, way].astype(F32)
            y2send[q, way, 1] = value.astype(BF16)
            remote(y2send.at[q, way, 1], y2recv.at[q, way, 1], 2, y2_rsem.at[q], to).start()

    def run_one(q):
        part_copy(q, "o").wait_recv()
        wait_recv(y2recv.at[q], y2_rsem.at[q])
        for d in (1, 2, 3, 0):
            r = (role + d) % 4
            way, place = r // 2, r % 2
            value = enc[q, core, 3, r].astype(F32) + arecv[q, 3, r].astype(F32)
            value = value + y2recv[q, way, 1, place].astype(F32)
            value = value + y2recv[q, 1 - way, 0, place].astype(F32)
            if d:
                z1send[q, d - 1] = value.astype(BF16)
                remote(z1send.at[q, d - 1], z1recv.at[q, d - 1], 3, z1_rsem.at[q], mates[d - 1]).start()
            else:
                z1own[q] = value

    def run_two(q):
        wait_recv(z1recv.at[q], z1_rsem.at[q])
        value = z1own[q]
        for d in range(3):
            value = value + z1recv[q, d].astype(F32)
        value = value.astype(BF16)
        half = HALF[q]
        for h in range(4):
            owner = q // 2 * 4 + h
            fsend[half, owner] = value[h * 16 : (h + 1) * 16]
            here = jnp.logical_and(owner == outer, half == run)

            @pl.when(jnp.logical_not(here))
            def _():
                remote(
                    fsend.at[half, owner], frecv.at[8 * run + outer], 5, f_rsem.at[0],
                    inner_of(y, 4 * half + role, core), owner,
                ).start()

    first_pair, pairs = len(DIRECT), CHUNKS - len(DIRECT)
    stages = {part: encode_send(part) for part in parts}
    stages.update(p=hello_second, l=limit_send, m=ring_far, k=ring_near, n=ring_on, r=run_one, s=run_two)
    for name, q in ORDER:
        stages[name](q)

    frecv[8 * run + outer] = fsend[run, outer]
    for stage, like in enumerate(
        (y1send.at[pl.ds(first_pair, pairs)], y2send, z1send, lim2.at[pl.ds(0, 7)], frecv.at[pl.ds(0, 15)])
    ):
        wait_send(like, stage + 1)
    wait_send(xrecv, 6)
    wait_send(arecv.at[pl.ds(first_pair, pairs)], 0)
    wait_send(arecv.at[pl.ds(0, len(DIRECT)), pl.ds(1, 3)], 7)
    wait_recv(limrecv.at[pl.ds(0, 7)], l_rsem.at[0])
    wait_recv(frecv.at[pl.ds(0, 15)], f_rsem.at[0])
    total = jnp.zeros((16, 128), F32)
    for group in range(8):
        value = frecv[group].astype(F32) + frecv[8 + group].astype(F32)
        total = total + clip(value, limrecv[group].astype(F32))
    high = total.astype(BF16)
    low = (total - high.astype(F32)).astype(BF16)
    signs = table[0:128, 0:128]
    result = jnp.dot(high, signs, preferred_element_type=F32)
    result = result + jnp.dot(low, signs, preferred_element_type=F32)
    out_ref[...] = result * F32(RSQRT)


def shards(grads, first_exponents, second_exponents):
    rows, columns = grads.shape[2], grads.shape[3]
    first = first_exponents.reshape(rows, columns // 128).T
    second = second_exponents.reshape(1, rows)
    operands = (grads.reshape(rows, columns), first, second)
    dma = pltpu.SemaphoreType.DMA
    c, r = CHUNKS, CHUNK_ROWS
    return pl.pallas_call(
        kernel,
        out_shape=jax.ShapeDtypeStruct((16, 128), F32),
        in_specs=[pl.BlockSpec(memory_space=pltpu.HBM)] * 3,
        out_specs=pl.BlockSpec(memory_space=pltpu.VMEM),
        scratch_shapes=[
            pltpu.VMEM((c, 4, r, 1024), F32),
            pltpu.VMEM((columns // 128, rows), jnp.int32),
            pltpu.VMEM((1, rows), jnp.int32),
            pltpu.VMEM((256, 256), BF16),
            pltpu.VMEM((128, 128), BF16),
            pltpu.VMEM((8, 16, 128), BF16),
            pltpu.VMEM((c, 2, 4, 4, r, 128), BF16),
            pltpu.VMEM((c, 4, 4, r, 128), BF16),
            pltpu.VMEM((c, 2, 2, r, 128), BF16),
            pltpu.VMEM((c, 2, 2, r, 128), BF16),
            pltpu.VMEM((c, 2, 2, 2, r, 128), BF16),
            pltpu.VMEM((c, 2, 2, 2, r, 128), BF16),
            pltpu.VMEM((c, 3, r, 128), BF16),
            pltpu.VMEM((c, r, 128), F32),
            pltpu.VMEM((c, 3, r, 128), BF16),
            pltpu.VMEM((len(DIRECT), 2, 2, 2, r, 128), BF16),
            pltpu.VMEM((2, 8, 16, 128), BF16),
            pltpu.VMEM((16, 16, 128), BF16),
            pltpu.VMEM((8, 16, 128), BF16),
            dma((c, 4)),
            dma((2,)),
            dma((8,)),
            dma((c, 4)),
            dma((c,)),
            dma((c,)),
            dma((c,)),
            dma((1,)),
            dma((1,)),
        ],
        compiler_params=pltpu.CompilerParams(
            collective_id=0, has_side_effects=True, vmem_limit_bytes=48 * 1024 * 1024
        ),
        name="reduce_scatter",
    )(*(pltpu.with_memory_space_constraint(x, pltpu.HBM) for x in operands))


def solution(mesh):
    placed = (
        P("inner", "outer", None, None),
        P("inner", "outer", None, None),
        P("outer", None, "inner"),
    )
    return jax.shard_map(
        shards, mesh=mesh, in_specs=placed, out_specs=P("outer", "inner"), check_vma=False
    )
```

```python
import math

import jax
import jax.numpy as jnp
from jax import lax
from jax.experimental import pallas as pl
from jax.experimental.pallas import tpu as pltpu
from jax.sharding import PartitionSpec as P

SATURATION = 448.0
RSQRT = 1.0 / math.sqrt(128.0)
LOGICAL = pl.DeviceIdType.MESH
F32 = jnp.float32
BF16 = jnp.bfloat16
CHUNKS = 4
CHUNK_ROWS = 64
HALF = (0, 1, 1, 0)
DIRECT = (0, 1)
ORDER = tuple(
    (item[0], int(item[1:]))
    for line in (
        "f0 h0 h1 f1", "h2 f2 f3 p0", "k0 n0 o0 h3", "k1 m2 o1 n1", "m3 l0 r0 o2",
        "k2 o3 n2 k3", "r1 n3 s0 r2", "r3 s1 s2 s3",
    )
    for item in line.split()
)


def sign_table():
    row = lax.broadcasted_iota(jnp.int32, (256, 256), 0)
    col = lax.broadcasted_iota(jnp.int32, (256, 256), 1)
    shared = row & col & 127
    shared = shared ^ (shared >> 4)
    shared = shared ^ (shared >> 2)
    shared = shared ^ (shared >> 1)
    signs = (1 - 2 * (shared & 1)).astype(F32)
    return jnp.where((row // 128) == (col // 128), signs, 0.0).astype(BF16)


def limits(exponents):
    return jnp.left_shift(1, exponents + 13).astype(F32) * F32(SATURATION / 8192.0)


def clip(value, bound):
    return jnp.minimum(jnp.maximum(value, -bound), bound)


def kernel(
    grads_ref, first_ref, second_ref, out_ref,
    gbuf, first_buf, second_buf, table, lim1, lim2, enc, arecv,
    y1send, y1recv, y2send, y2recv, z1send, z1own, z1recv, xrecv, fsend, frecv, limrecv,
    load_sem, scale_sem, send_sem, a_rsem, y1_rsem, y2_rsem, z1_rsem, l_rsem, f_rsem,
):
    inner = lax.axis_index("inner")
    outer = lax.axis_index("outer")
    core = inner % 2
    z = (inner // 2) % 8
    y = inner // 16
    run, role = z // 4, z % 4
    y_right, y_left, y_far = (y + 1) % 4, (y + 3) % 4, (y + 2) % 4

    def inner_of(yy, zz, cc):
        return (yy * 8 + zz) * 2 + cc

    sibling = inner_of(y, z, 1 - core)
    right = inner_of(y_right, z, core)
    left = inner_of(y_left, z, core)
    beside = [inner_of(y_right, z, 1 - core), inner_of(y_left, z, 1 - core)]
    across = inner_of(y, (1 - run) * 4 + role, core)
    mates = [inner_of(y, run * 4 + (role + d) % 4, core) for d in (1, 2, 3)]

    def remote(src, dst, stage, rsem, i, o=None):
        return pltpu.make_async_remote_copy(
            src_ref=src, dst_ref=dst, send_sem=send_sem.at[stage], recv_sem=rsem,
            device_id=(i, outer if o is None else o), device_id_type=LOGICAL,
        )

    def wait_recv(dst, rsem):
        remote(dst, dst, 0, rsem, sibling).wait_recv()

    def wait_send(like, stage):
        remote(like, like, stage, f_rsem.at[0], sibling).wait_send()

    scale_loads = [
        pltpu.make_async_copy(first_ref, first_buf, scale_sem.at[0]),
        pltpu.make_async_copy(second_ref, second_buf, scale_sem.at[1]),
    ]
    places = (y_far, y_right, y_left, y)
    parts = {"f": (0,), "h": (1, 2), "o": (3,)}

    def rows_of(q):
        return pl.ds(q // 2 * CHUNK_ROWS, CHUNK_ROWS)

    def load(q, d):
        columns = pl.ds(pl.multiple_of(places[d] * 2048 + HALF[q] * 1024, 1024), 1024)
        return pltpu.make_async_copy(
            grads_ref.at[rows_of(q), columns], gbuf.at[q, d], load_sem.at[q, d]
        )

    def start_loads(q):
        for d in range(4):
            load(q, d).start()

    for copy in scale_loads:
        copy.start()
    load(0, 0).start()

    lower, first_run = 1 - outer // 4, 1 - run
    klass = lower * first_run
    barrier = pltpu.get_barrier_semaphore()

    def hello(i, o):
        pl.semaphore_signal(barrier, inc=1, device_id=(i, o), device_id_type=LOGICAL)

    def hello_first():
        for i in [sibling, right, left] + beside + mates:
            hello(i, outer)
        for d in range(1, 4):
            hello(inner, outer // 4 * 4 + (outer + d) % 4)

        @pl.when(klass == 0)
        def _():
            other = lower * inner + (1 - lower) * (first_run * across + run * inner)
            for j in range(4):
                hello(across, 4 + j)
                hello(other, 4 * lower + j)

    def hello_second(q):
        @pl.when(klass == 1)
        def _():
            for j in range(4):
                hello(across, j)
                hello(across, 4 + j)
                hello(inner, 4 + j)

        @pl.when(klass == 0)
        def _():
            early = lower * across + (1 - lower) * (first_run * inner + run * across)
            for j in range(4):
                hello(early, j)

    def enter():
        pl.semaphore_wait(barrier, 23 - 12 * klass)

    def enter_outer():
        @pl.when(klass == 1)
        def _():
            pl.semaphore_wait(barrier, 12)

    hello_first()
    for d in (1, 2, 3):
        load(0, d).start()

    start_loads(1)
    table[...] = sign_table()
    for copy in scale_loads:
        copy.wait()
    first = jnp.concatenate(
        [first_buf[pl.ds(pl.multiple_of(place * 16, 16), 16), :] for place in places] * 2, axis=0
    )
    lim1[...] = limits(first).T.astype(BF16)

    def encode(q, part):
        bounds = lim1[rows_of(q), :]
        pairs = [(d, k) for d in parts[part] for k in range(4)]
        for d in parts[part]:
            load(q, d).wait()
        if part == "h" and q + 2 < CHUNKS:
            start_loads(q + 2)
        lhs = jnp.concatenate(
            [gbuf[q, d, :, k * 256 : (k + 1) * 256].astype(BF16) for d, k in pairs], axis=0
        )
        rotated = jnp.dot(lhs, table[...], preferred_element_type=F32) * F32(RSQRT)
        rotated = rotated.astype(BF16)
        for i, (d, k) in enumerate(pairs):
            for c in range(2):
                lane = 16 * d + 8 * HALF[q] + 2 * k + c
                bound = jnp.broadcast_to(bounds[:, lane : lane + 1], (CHUNK_ROWS, 128))
                value = rotated[i * CHUNK_ROWS : (i + 1) * CHUNK_ROWS, c * 128 : (c + 1) * 128]
                enc[q, c, d, k] = clip(value, bound)

    def part_copy(q, part):
        span = pl.ds(parts[part][0], len(parts[part]))
        return remote(
            enc.at[q, 1 - core, span], arecv.at[q, span], 7 if q in DIRECT else 0,
            a_rsem.at[q, parts[part][0]], sibling,
        )

    def direct_copy(q, way, c):
        two = pl.ds(2 * way, 2)
        target = inner_of((y_right, y_left)[way], z, c)
        return remote(enc.at[q, c, 0, two], xrecv.at[q, core, way], 6, y1_rsem.at[q], target)

    def encode_send(part):
        def stage(q):
            encode(q, part)
            if part == "f" and q == 0:
                enter()
            if part == "f" and q in DIRECT:
                for way in range(2):
                    for c in range(2):
                        direct_copy(q, way, c).start()
            else:
                part_copy(q, part).start()

        return stage

    def pair_sum(q, d, way):
        two = pl.ds(2 * way, 2)
        return enc[q, core, d, two] + arecv[q, d, two]

    def limit_send(q):
        second = jnp.broadcast_to(limits(second_buf[...]), (128, 128)).T.astype(BF16)
        for owner in range(8):
            lim2[owner] = second[owner * 16 : (owner + 1) * 16]
        limrecv[outer] = lim2[outer]
        enter_outer()
        for d in range(1, 8):
            owner = (outer + d) % 8
            remote(lim2.at[owner], limrecv.at[outer], 4, l_rsem.at[0], inner, owner).start()

    def ring_far(q):
        if q in DIRECT:
            return
        part_copy(q, "f").wait_recv()
        for way, to in ((0, right), (1, left)):
            y1send[q, way] = pair_sum(q, 0, way)
            remote(y1send.at[q, way], y1recv.at[q, way], 1, y1_rsem.at[q], to).start()

    def ring_near(q):
        part_copy(q, "h").wait_recv()
        for way in range(2):
            y2send[q, way, 0] = pair_sum(q, 1 + way, 1 - way)

    def ring_on(q):
        wait_recv(xrecv.at[q] if q in DIRECT else y1recv.at[q], y1_rsem.at[q])
        for way, to in ((0, right), (1, left)):
            two = pl.ds(2 * way, 2)
            value = enc[q, core, 1 + way, two].astype(F32) + arecv[q, 1 + way, two].astype(F32)
            if q in DIRECT:
                value = value + xrecv[q, 0, way].astype(F32) + xrecv[q, 1, way].astype(F32)
            else:
                value = value + y1recv[q, way].astype(F32)
            y2send[q, way, 1] = value.astype(BF16)
            remote(y2send.at[q, way], y2recv.at[q, way], 2, y2_rsem.at[q], to).start()

    def run_one(q):
        part_copy(q, "o").wait_recv()
        wait_recv(y2recv.at[q], y2_rsem.at[q])
        for d in (1, 2, 3, 0):
            r = (role + d) % 4
            way, place = r // 2, r % 2
            value = enc[q, core, 3, r].astype(F32) + arecv[q, 3, r].astype(F32)
            value = value + y2recv[q, way, 1, place].astype(F32)
            value = value + y2recv[q, 1 - way, 0, place].astype(F32)
            if d:
                z1send[q, d - 1] = value.astype(BF16)
                remote(z1send.at[q, d - 1], z1recv.at[q, d - 1], 3, z1_rsem.at[q], mates[d - 1]).start()
            else:
                z1own[q] = value

    def run_two(q):
        wait_recv(z1recv.at[q], z1_rsem.at[q])
        value = z1own[q]
        for d in range(3):
            value = value + z1recv[q, d].astype(F32)
        value = value.astype(BF16)
        half = HALF[q]
        band = q // 2
        for h in range(4):
            fsend[half, band * 4 + h] = value[h * 16 : (h + 1) * 16]

        def owner_copy(h):
            owner = band * 4 + (outer + h) % 4
            return remote(
                fsend.at[half, owner], frecv.at[8 * run + outer], 5, f_rsem.at[0],
                inner_of(y, 4 * half + role, core), owner,
            )

        for h in range(1, 4):
            owner_copy(h).start()
        here = jnp.logical_and(outer // 4 == band, half == run)

        @pl.when(jnp.logical_not(here))
        def _():
            owner_copy(0).start()

    first_pair, pairs = len(DIRECT), CHUNKS - len(DIRECT)
    stages = {part: encode_send(part) for part in parts}
    stages.update(p=hello_second, l=limit_send, m=ring_far, k=ring_near, n=ring_on, r=run_one, s=run_two)
    for name, q in ORDER:
        stages[name](q)

    frecv[8 * run + outer] = fsend[run, outer]
    for stage, like in enumerate(
        (y1send.at[pl.ds(first_pair, pairs)], y2send, z1send, lim2.at[pl.ds(0, 7)], frecv.at[pl.ds(0, 15)])
    ):
        wait_send(like, stage + 1)
    wait_send(xrecv, 6)
    wait_send(arecv.at[pl.ds(first_pair, pairs)], 0)
    wait_send(arecv.at[pl.ds(0, len(DIRECT)), pl.ds(1, 3)], 7)
    wait_recv(limrecv.at[pl.ds(0, 7)], l_rsem.at[0])
    wait_recv(frecv.at[pl.ds(0, 15)], f_rsem.at[0])
    total = jnp.zeros((16, 128), F32)
    for group in range(8):
        value = frecv[group].astype(F32) + frecv[8 + group].astype(F32)
        total = total + clip(value, limrecv[group].astype(F32))
    high = total.astype(BF16)
    low = (total - high.astype(F32)).astype(BF16)
    signs = table[0:128, 0:128]
    result = jnp.dot(high, signs, preferred_element_type=F32)
    result = result + jnp.dot(low, signs, preferred_element_type=F32)
    out_ref[...] = result * F32(RSQRT)


def shards(grads, first_exponents, second_exponents):
    rows, columns = grads.shape[2], grads.shape[3]
    first = first_exponents.reshape(rows, columns // 128).T
    second = second_exponents.reshape(1, rows)
    operands = (grads.reshape(rows, columns), first, second)
    dma = pltpu.SemaphoreType.DMA
    c, r = CHUNKS, CHUNK_ROWS
    return pl.pallas_call(
        kernel,
        out_shape=jax.ShapeDtypeStruct((16, 128), F32),
        in_specs=[pl.BlockSpec(memory_space=pltpu.HBM)] * 3,
        out_specs=pl.BlockSpec(memory_space=pltpu.VMEM),
        scratch_shapes=[
            pltpu.VMEM((c, 4, r, 1024), F32),
            pltpu.VMEM((columns // 128, rows), jnp.int32),
            pltpu.VMEM((1, rows), jnp.int32),
            pltpu.VMEM((256, 256), BF16),
            pltpu.VMEM((128, 128), BF16),
            pltpu.VMEM((8, 16, 128), BF16),
            pltpu.VMEM((c, 2, 4, 4, r, 128), BF16),
            pltpu.VMEM((c, 4, 4, r, 128), BF16),
            pltpu.VMEM((c, 2, 2, r, 128), BF16),
            pltpu.VMEM((c, 2, 2, r, 128), BF16),
            pltpu.VMEM((c, 2, 2, 2, r, 128), BF16),
            pltpu.VMEM((c, 2, 2, 2, r, 128), BF16),
            pltpu.VMEM((c, 3, r, 128), BF16),
            pltpu.VMEM((c, r, 128), F32),
            pltpu.VMEM((c, 3, r, 128), BF16),
            pltpu.VMEM((len(DIRECT), 2, 2, 2, r, 128), BF16),
            pltpu.VMEM((2, 8, 16, 128), BF16),
            pltpu.VMEM((16, 16, 128), BF16),
            pltpu.VMEM((8, 16, 128), BF16),
            dma((c, 4)),
            dma((2,)),
            dma((8,)),
            dma((c, 4)),
            dma((c,)),
            dma((c,)),
            dma((c,)),
            dma((1,)),
            dma((1,)),
        ],
        compiler_params=pltpu.CompilerParams(
            collective_id=0, has_side_effects=True, vmem_limit_bytes=48 * 1024 * 1024
        ),
        name="reduce_scatter",
    )(*(pltpu.with_memory_space_constraint(x, pltpu.HBM) for x in operands))


def solution(mesh):
    placed = (
        P("inner", "outer", None, None),
        P("inner", "outer", None, None),
        P("outer", None, "inner"),
    )
    return jax.shard_map(
        shards, mesh=mesh, in_specs=placed, out_specs=P("outer", "inner"), check_vma=False
    )
```

```python
import math

import jax
import jax.numpy as jnp
from jax import lax
from jax.experimental import pallas as pl
from jax.experimental.pallas import tpu as pltpu
from jax.sharding import PartitionSpec as P

SATURATION = 448.0
RSQRT = 1.0 / math.sqrt(128.0)
LOGICAL = pl.DeviceIdType.MESH
F32 = jnp.float32
BF16 = jnp.bfloat16
CHUNKS = 4
CHUNK_ROWS = 64
HALF = (0, 1, 1, 0)
DIRECT = (0, 1)
ORDER = tuple(
    (item[0], int(item[1:]))
    for line in (
        "f0 h0 h1 f1", "h2 f2 f3 p0", "k0 n0 o0 h3", "k1 m2 o1 n1", "m3 r0 l0 o2",
        "k2 o3 n2 k3", "r1 n3 s0 r2", "r3 s1 s2 s3",
    )
    for item in line.split()
)


def sign_table():
    row = lax.broadcasted_iota(jnp.int32, (256, 256), 0)
    col = lax.broadcasted_iota(jnp.int32, (256, 256), 1)
    shared = row & col & 127
    shared = shared ^ (shared >> 4)
    shared = shared ^ (shared >> 2)
    shared = shared ^ (shared >> 1)
    signs = (1 - 2 * (shared & 1)).astype(F32)
    return jnp.where((row // 128) == (col // 128), signs, 0.0).astype(BF16)


def limits(exponents):
    return jnp.left_shift(1, exponents + 13).astype(F32) * F32(SATURATION / 8192.0)


def clip(value, bound):
    return jnp.minimum(jnp.maximum(value, -bound), bound)


def kernel(
    grads_ref, first_ref, second_ref, out_ref,
    gbuf, first_buf, second_buf, table, lim1, lim2, enc, arecv,
    y1send, y1recv, y2send, y2recv, z1send, z1own, z1recv, xrecv, fsend, frecv, limrecv,
    load_sem, scale_sem, send_sem, a_rsem, y1_rsem, y2_rsem, z1_rsem, l_rsem, f_rsem,
):
    inner = lax.axis_index("inner")
    outer = lax.axis_index("outer")
    core = inner % 2
    z = (inner // 2) % 8
    y = inner // 16
    run, role = z // 4, z % 4
    y_right, y_left, y_far = (y + 1) % 4, (y + 3) % 4, (y + 2) % 4

    def inner_of(yy, zz, cc):
        return (yy * 8 + zz) * 2 + cc

    sibling = inner_of(y, z, 1 - core)
    right = inner_of(y_right, z, core)
    left = inner_of(y_left, z, core)
    beside = [inner_of(y_right, z, 1 - core), inner_of(y_left, z, 1 - core)]
    across = inner_of(y, (1 - run) * 4 + role, core)
    mates = [inner_of(y, run * 4 + (role + d) % 4, core) for d in (1, 2, 3)]

    def remote(src, dst, stage, rsem, i, o=None):
        return pltpu.make_async_remote_copy(
            src_ref=src, dst_ref=dst, send_sem=send_sem.at[stage], recv_sem=rsem,
            device_id=(i, outer if o is None else o), device_id_type=LOGICAL,
        )

    def wait_recv(dst, rsem):
        remote(dst, dst, 0, rsem, sibling).wait_recv()

    def wait_send(like, stage):
        remote(like, like, stage, f_rsem.at[0], sibling).wait_send()

    scale_loads = [
        pltpu.make_async_copy(first_ref, first_buf, scale_sem.at[0]),
        pltpu.make_async_copy(second_ref, second_buf, scale_sem.at[1]),
    ]
    places = (y_far, y_right, y_left, y)
    parts = {"f": (0,), "h": (1, 2), "o": (3,)}

    def rows_of(q):
        return pl.ds(q // 2 * CHUNK_ROWS, CHUNK_ROWS)

    def load(q, d):
        columns = pl.ds(pl.multiple_of(places[d] * 2048 + HALF[q] * 1024, 1024), 1024)
        return pltpu.make_async_copy(
            grads_ref.at[rows_of(q), columns], gbuf.at[q, d], load_sem.at[q, d]
        )

    def start_loads(q):
        for d in range(4):
            load(q, d).start()

    for copy in scale_loads:
        copy.start()
    load(0, 0).start()

    lower, first_run = 1 - outer // 4, 1 - run
    klass = lower * first_run
    barrier = pltpu.get_barrier_semaphore()

    def hello(i, o):
        pl.semaphore_signal(barrier, inc=1, device_id=(i, o), device_id_type=LOGICAL)

    def hello_first():
        for i in [sibling, right, left] + beside + mates:
            hello(i, outer)
        for d in range(1, 4):
            hello(inner, outer // 4 * 4 + (outer + d) % 4)

        @pl.when(klass == 0)
        def _():
            other = lower * inner + (1 - lower) * (first_run * across + run * inner)
            for j in range(4):
                hello(across, 4 + j)
                hello(other, 4 * lower + j)

    def hello_second(q):
        @pl.when(klass == 1)
        def _():
            for j in range(4):
                hello(across, j)
                hello(across, 4 + j)
                hello(inner, 4 + j)

        @pl.when(klass == 0)
        def _():
            early = lower * across + (1 - lower) * (first_run * inner + run * across)
            for j in range(4):
                hello(early, j)

    def enter():
        pl.semaphore_wait(barrier, 23 - 12 * klass)

    def enter_outer():
        @pl.when(klass == 1)
        def _():
            pl.semaphore_wait(barrier, 12)

    hello_first()
    for d in (1, 2, 3):
        load(0, d).start()

    start_loads(1)
    table[...] = sign_table()
    for copy in scale_loads:
        copy.wait()
    first = jnp.concatenate(
        [first_buf[pl.ds(pl.multiple_of(place * 16, 16), 16), :] for place in places] * 2, axis=0
    )
    lim1[...] = limits(first).T.astype(BF16)

    def encode(q, part):
        bounds = lim1[rows_of(q), :]
        pairs = [(d, k) for d in parts[part] for k in range(4)]
        for d in parts[part]:
            load(q, d).wait()
        if part == "h" and q + 2 < CHUNKS:
            start_loads(q + 2)
        lhs = jnp.concatenate(
            [gbuf[q, d, :, k * 256 : (k + 1) * 256].astype(BF16) for d, k in pairs], axis=0
        )
        rotated = jnp.dot(lhs, table[...], preferred_element_type=F32) * F32(RSQRT)
        rotated = rotated.astype(BF16)
        for i, (d, k) in enumerate(pairs):
            for c in range(2):
                lane = 16 * d + 8 * HALF[q] + 2 * k + c
                bound = jnp.broadcast_to(bounds[:, lane : lane + 1], (CHUNK_ROWS, 128))
                value = rotated[i * CHUNK_ROWS : (i + 1) * CHUNK_ROWS, c * 128 : (c + 1) * 128]
                enc[q, c, d, k] = clip(value, bound)

    def part_copy(q, part):
        span = pl.ds(parts[part][0], len(parts[part]))
        return remote(
            enc.at[q, 1 - core, span], arecv.at[q, span], 7 if q in DIRECT else 0,
            a_rsem.at[q, parts[part][0]], sibling,
        )

    def direct_copy(q, way, c):
        two = pl.ds(2 * way, 2)
        target = inner_of((y_right, y_left)[way], z, c)
        return remote(enc.at[q, c, 0, two], xrecv.at[q, core, way], 6, y1_rsem.at[q], target)

    def encode_send(part):
        def stage(q):
            encode(q, part)
            if part == "f" and q == 0:
                enter()
            if part == "f" and q in DIRECT:
                for way in range(2):
                    for c in range(2):
                        direct_copy(q, way, c).start()
            else:
                part_copy(q, part).start()

        return stage

    def pair_sum(q, d, way):
        two = pl.ds(2 * way, 2)
        return enc[q, core, d, two] + arecv[q, d, two]

    def limit_send(q):
        second = jnp.broadcast_to(limits(second_buf[...]), (128, 128)).T.astype(BF16)
        for owner in range(8):
            lim2[owner] = second[owner * 16 : (owner + 1) * 16]
        limrecv[outer] = lim2[outer]
        enter_outer()
        for d in range(1, 8):
            owner = (outer + d) % 8
            remote(lim2.at[owner], limrecv.at[outer], 4, l_rsem.at[0], inner, owner).start()

    def ring_far(q):
        if q in DIRECT:
            return
        part_copy(q, "f").wait_recv()
        for way, to in ((0, right), (1, left)):
            y1send[q, way] = pair_sum(q, 0, way)
            remote(y1send.at[q, way], y1recv.at[q, way], 1, y1_rsem.at[q], to).start()

    def ring_near(q):
        part_copy(q, "h").wait_recv()
        for way, to in ((0, right), (1, left)):
            y2send[q, way, 0] = pair_sum(q, 1 + way, 1 - way)
            remote(y2send.at[q, way, 0], y2recv.at[q, way, 0], 2, y2_rsem.at[q], to).start()

    def ring_on(q):
        wait_recv(xrecv.at[q] if q in DIRECT else y1recv.at[q], y1_rsem.at[q])
        for way, to in ((0, right), (1, left)):
            two = pl.ds(2 * way, 2)
            value = enc[q, core, 1 + way, two].astype(F32) + arecv[q, 1 + way, two].astype(F32)
            if q in DIRECT:
                value = value + xrecv[q, 0, way].astype(F32) + xrecv[q, 1, way].astype(F32)
            else:
                value = value + y1recv[q, way].astype(F32)
            y2send[q, way, 1] = value.astype(BF16)
            remote(y2send.at[q, way, 1], y2recv.at[q, way, 1], 2, y2_rsem.at[q], to).start()

    def run_one(q):
        part_copy(q, "o").wait_recv()
        wait_recv(y2recv.at[q], y2_rsem.at[q])
        for d in (1, 2, 3, 0):
            r = (role + d) % 4
            way, place = r // 2, r % 2
            value = enc[q, core, 3, r].astype(F32) + arecv[q, 3, r].astype(F32)
            value = value + y2recv[q, way, 1, place].astype(F32)
            value = value + y2recv[q, 1 - way, 0, place].astype(F32)
            if d:
                z1send[q, d - 1] = value.astype(BF16)
                remote(z1send.at[q, d - 1], z1recv.at[q, d - 1], 3, z1_rsem.at[q], mates[d - 1]).start()
            else:
                z1own[q] = value

    def run_two(q):
        wait_recv(z1recv.at[q], z1_rsem.at[q])
        value = z1own[q]
        for d in range(3):
            value = value + z1recv[q, d].astype(F32)
        value = value.astype(BF16)
        half = HALF[q]
        band = q // 2
        for h in range(4):
            fsend[half, band * 4 + h] = value[h * 16 : (h + 1) * 16]

        def owner_copy(h):
            owner = band * 4 + (outer + h) % 4
            return remote(
                fsend.at[half, owner], frecv.at[8 * run + outer], 5, f_rsem.at[0],
                inner_of(y, 4 * half + role, core), owner,
            )

        for h in range(1, 4):
            owner_copy(h).start()
        here = jnp.logical_and(outer // 4 == band, half == run)

        @pl.when(jnp.logical_not(here))
        def _():
            owner_copy(0).start()

    first_pair, pairs = len(DIRECT), CHUNKS - len(DIRECT)
    stages = {part: encode_send(part) for part in parts}
    stages.update(p=hello_second, l=limit_send, m=ring_far, k=ring_near, n=ring_on, r=run_one, s=run_two)
    for name, q in ORDER:
        stages[name](q)

    frecv[8 * run + outer] = fsend[run, outer]
    for stage, like in enumerate(
        (y1send.at[pl.ds(first_pair, pairs)], y2send, z1send, lim2.at[pl.ds(0, 7)], frecv.at[pl.ds(0, 15)])
    ):
        wait_send(like, stage + 1)
    wait_send(xrecv, 6)
    wait_send(arecv.at[pl.ds(first_pair, pairs)], 0)
    wait_send(arecv.at[pl.ds(0, len(DIRECT)), pl.ds(1, 3)], 7)
    wait_recv(limrecv.at[pl.ds(0, 7)], l_rsem.at[0])
    wait_recv(frecv.at[pl.ds(0, 15)], f_rsem.at[0])
    total = jnp.zeros((16, 128), F32)
    for group in range(8):
        value = frecv[group].astype(F32) + frecv[8 + group].astype(F32)
        total = total + clip(value, limrecv[group].astype(F32))
    high = total.astype(BF16)
    low = (total - high.astype(F32)).astype(BF16)
    signs = table[0:128, 0:128]
    result = jnp.dot(high, signs, preferred_element_type=F32)
    result = result + jnp.dot(low, signs, preferred_element_type=F32)
    out_ref[...] = result * F32(RSQRT)


def shards(grads, first_exponents, second_exponents):
    rows, columns = grads.shape[2], grads.shape[3]
    first = first_exponents.reshape(rows, columns // 128).T
    second = second_exponents.reshape(1, rows)
    operands = (grads.reshape(rows, columns), first, second)
    dma = pltpu.SemaphoreType.DMA
    c, r = CHUNKS, CHUNK_ROWS
    return pl.pallas_call(
        kernel,
        out_shape=jax.ShapeDtypeStruct((16, 128), F32),
        in_specs=[pl.BlockSpec(memory_space=pltpu.HBM)] * 3,
        out_specs=pl.BlockSpec(memory_space=pltpu.VMEM),
        scratch_shapes=[
            pltpu.VMEM((c, 4, r, 1024), F32),
            pltpu.VMEM((columns // 128, rows), jnp.int32),
            pltpu.VMEM((1, rows), jnp.int32),
            pltpu.VMEM((256, 256), BF16),
            pltpu.VMEM((128, 128), BF16),
            pltpu.VMEM((8, 16, 128), BF16),
            pltpu.VMEM((c, 2, 4, 4, r, 128), BF16),
            pltpu.VMEM((c, 4, 4, r, 128), BF16),
            pltpu.VMEM((c, 2, 2, r, 128), BF16),
            pltpu.VMEM((c, 2, 2, r, 128), BF16),
            pltpu.VMEM((c, 2, 2, 2, r, 128), BF16),
            pltpu.VMEM((c, 2, 2, 2, r, 128), BF16),
            pltpu.VMEM((c, 3, r, 128), BF16),
            pltpu.VMEM((c, r, 128), F32),
            pltpu.VMEM((c, 3, r, 128), BF16),
            pltpu.VMEM((len(DIRECT), 2, 2, 2, r, 128), BF16),
            pltpu.VMEM((2, 8, 16, 128), BF16),
            pltpu.VMEM((16, 16, 128), BF16),
            pltpu.VMEM((8, 16, 128), BF16),
            dma((c, 4)),
            dma((2,)),
            dma((8,)),
            dma((c, 4)),
            dma((c,)),
            dma((c,)),
            dma((c,)),
            dma((1,)),
            dma((1,)),
        ],
        compiler_params=pltpu.CompilerParams(
            collective_id=0, has_side_effects=True, vmem_limit_bytes=48 * 1024 * 1024
        ),
        name="reduce_scatter",
    )(*(pltpu.with_memory_space_constraint(x, pltpu.HBM) for x in operands))


def solution(mesh):
    placed = (
        P("inner", "outer", None, None),
        P("inner", "outer", None, None),
        P("outer", None, "inner"),
    )
    return jax.shard_map(
        shards, mesh=mesh, in_specs=placed, out_specs=P("outer", "inner"), check_vma=False
    )
```
